32 devices in a mesh: tok: 8 (over z, x), head: 4 (over y, core).
Axes of the slice: x: 2, y: 2, z: 4, core: 2. Of those that a mesh axis runs over, the one named last changes fastest.
Arguments:
- queries: bfloat16 [2, 1024, 2048], P(None, 'tok', 'head'), may hold values from -6 to 6
- keys: bfloat16 [1024, 2048], P('tok', 'head'), may hold values from -6 to 6
- values: bfloat16 [1024, 2048], P('tok', 'head'), may hold values from -6 to 6
- upstream: bfloat16 [2, 1024, 2048], P(None, 'tok', 'head'), may hold values from -6 to 6
- out_gain: float32 [2048], P('head'), may hold values from 0.5 to 2
- gate_weight: bfloat16 [4, 512, 512], P('head', 'tok'), may hold values from -0.25 to 0.25
- up_weight: bfloat16 [4, 512, 512], P('head', 'tok'), may hold values from -0.25 to 0.25
- down_weight: bfloat16 [4, 512, 512], P('head', 'tok'), may hold values from -0.25 to 0.25
Outputs:
- grad_queries: bfloat16 [2, 1024, 2048], P(None, 'tok', 'head')
- grad_keys: bfloat16 [1024, 2048], P('tok', 'head')
- grad_values: bfloat16 [1024, 2048], P('tok', 'head')
- grad_gate: float32 [4, 512, 512], P('head', 'tok')
- grad_up: float32 [4, 512, 512], P('head', 'tok')
- grad_down: float32 [4, 512, 512], P('head', 'tok')
The draws below stay inside these ranges and needn't reach their ends.
All inputs are finite; a program needn't handle non-finite values.
Results may differ from the reference program's by a relative error of at most 0.02.
Values may be sent and summed in bfloat16 or wider, within the bound.
No kernel may reach another device: no remote copies, remote signals or barrier semaphores. Data moves between devices by JAX's collectives and lax.ppermute only.
A program may use at most 128 MiB of HBM per device.

```python
import math
import jax
import jax.numpy as jnp
from jax import lax

D = 512
H = 512
NS_STEPS = 2
HEADS = 4
BLOCK = 1024


def strengthened(values, rng, source, target, blocks, factor):
    owner, partner = [(jnp.arange(values.shape[dim]) // (values.shape[dim] // blocks)).reshape([-1 if axis == dim else 1 for axis in range(values.ndim)]) for dim in (source, target)]
    chosen = jax.random.permutation(rng, blocks)[partner]
    strong = (owner == chosen) | (owner == (partner + blocks // 2) % blocks)
    return jnp.where(strong, factor * values, values)


def block_scale(own_key, shape, split, smallest, top_value):
    factor_of, own = 1.0, jax.random.fold_in(own_key, 6)
    for position, parts in split:
        heights = jnp.exp(jax.random.uniform(jax.random.fold_in(own, position), (parts,), jnp.float32, smallest / len(split), top_value / len(split)))
        factor_of = factor_of * jnp.repeat(heights, shape[position] // parts).reshape([-1 if axis == position else 1 for axis in range(len(shape))])
    return factor_of


def bell_draw(stream_key, shape, spread, limit, pieces=(), dtype=jnp.bfloat16):
    loudness = block_scale(stream_key, shape, pieces, -0.22, 0.18) if pieces else 1.0
    result = jax.random.normal(stream_key, shape, jnp.float32) * spread * loudness
    return jnp.minimum(jnp.maximum(result, -limit), limit).astype(dtype)


def gaussian_with(stream_key, shape, scale, limit, pieces, heavy, held_as=jnp.bfloat16):
    result = scale * jax.random.normal(stream_key, shape, jnp.float32)
    if pieces:
        result = result * block_scale(stream_key, shape, pieces, -0.22, 0.18)
    return jnp.clip(strengthened(result, jax.random.fold_in(stream_key, 3), *heavy), -limit, limit).astype(held_as)


def setup_inputs(seed: int = 0) -> dict:
    seeds = jax.random.split(jax.random.key(seed), 9)
    return {
        "queries": gaussian_with(seeds[0], (2, BLOCK, HEADS * D), 1.0, 6.0, ((1, 8), (2, 4)), (1, 2, 8, 2.0)),
        "keys": gaussian_with(seeds[1], (BLOCK, HEADS * D), 1.0, 6.0, ((0, 8), (1, 4)), (0, 1, 8, 2.0)),
        "values": bell_draw(seeds[2], (BLOCK, HEADS * D), 1.0, 6.0, ((0, 8), (1, 4))),
        "upstream": bell_draw(seeds[3], (2, BLOCK, HEADS * D), 1.0, 6.0, ((1, 8), (2, 4))),
        "out_gain": jnp.clip(jnp.exp(math.log(2.0) - 1.3862944 * jax.random.uniform(seeds[4], (HEADS * D,), jnp.float32) ** block_scale(seeds[4], (HEADS * D,), ((0, 4),), -0.2, 0.2)), 0.5, 2.0),
        "gate_weight": bell_draw(seeds[5], (HEADS, D, H), D ** -0.5, 0.25, ((0, 4), (1, 8))),
        "up_weight": bell_draw(seeds[6], (HEADS, D, H), D ** -0.5, 0.25, ((0, 4), (1, 8))),
        "down_weight": bell_draw(seeds[7], (HEADS, H, D), H ** -0.5, 0.25, ((0, 4), (1, 8))),
    }


lin_coef = 3.4445
cube_coef = -4.775
fifth_coef = 2.0315
rms_eps = 1e-06
fro_eps = 1e-07

def product(left, right):
    return jnp.dot(left, right, preferred_element_type=jnp.float32)

def across(left, right):
    return lax.dot_general(left, right, (((0,), (0,)), ((), ())), preferred_element_type=jnp.float32)

def against(left, right):
    return lax.dot_general(left, right, (((1,), (1,)), ((), ())), preferred_element_type=jnp.float32)

def fast_forward(keys, values, weights):
    gate_weight, up_weight, down_weight = weights
    gate_pre = product(keys, gate_weight)
    up_pre = product(keys, up_weight)
    sigma = jax.nn.sigmoid(gate_pre)
    active = gate_pre * sigma
    hidden = (active * up_pre).astype(jnp.bfloat16)
    back = -against(values, down_weight)
    slope = sigma * (1.0 + gate_pre * (1.0 - sigma))
    d_gate = (back * up_pre * slope).astype(jnp.bfloat16)
    d_up = (back * active).astype(jnp.bfloat16)
    fast = (across(keys, d_gate), across(keys, d_up), -across(hidden, values))
    saved = (gate_pre, up_pre, sigma, active, hidden, back, slope, d_gate, d_up)
    return (fast, saved)

def fast_second(keys, values, weights, saved, cots):
    gate_weight, up_weight, down_weight = weights
    gate_pre, up_pre, sigma, active, hidden, back, slope, d_gate, d_up = saved
    cot_gate, cot_up, cot_down = cots
    along_gate = product(keys, cot_gate)
    along_up = product(keys, cot_up)
    along_hidden = -against(values, cot_down)
    curve = sigma * (1.0 - sigma) * (2.0 + gate_pre * (1.0 - 2.0 * sigma))
    d_back = (along_gate * up_pre * slope + along_up * active).astype(jnp.bfloat16)
    d_upper = (along_gate * back * slope + along_hidden * active).astype(jnp.bfloat16)
    d_lower = (along_gate * back * up_pre * curve + along_up * back * slope + along_hidden * up_pre * slope).astype(jnp.bfloat16)
    grad_keys = (against(d_gate, cot_gate) + against(d_up, cot_up) + against(d_lower, gate_weight) + against(d_upper, up_weight)).astype(jnp.bfloat16)
    grad_values = (-product(hidden, cot_down) - product(d_back, down_weight)).astype(jnp.bfloat16)
    partial_value = (across(keys, d_lower), across(keys, d_upper), -across(d_back, values))
    return (grad_keys, grad_values, partial_value)

def apply_forward(queries, weights):
    gate_weight, up_weight, down_weight = weights
    gate_pre = product(queries, gate_weight)
    up_pre = product(queries, up_weight)
    sigma = jax.nn.sigmoid(gate_pre)
    hidden = (gate_pre * sigma * up_pre).astype(jnp.bfloat16)
    output = product(hidden, down_weight)
    return (gate_pre, up_pre, sigma, hidden, output)

def apply_backward(queries, weights, saved, upstream, out_gain, inverse_rms, mean_dot):
    gate_weight, up_weight, down_weight = weights
    gate_pre, up_pre, sigma, hidden, output = saved
    weighted = out_gain * upstream.astype(jnp.float32)
    d_output = (inverse_rms[:, None] * weighted - output * (inverse_rms * inverse_rms * inverse_rms * mean_dot)[:, None]).astype(jnp.bfloat16)
    back = against(d_output, down_weight)
    slope = sigma * (1.0 + gate_pre * (1.0 - sigma))
    d_gate = (back * up_pre * slope).astype(jnp.bfloat16)
    d_up = (back * gate_pre * sigma).astype(jnp.bfloat16)
    grad_queries = (against(d_gate, gate_weight) + against(d_up, up_weight)).astype(jnp.bfloat16)
    partial_value = (across(queries, d_gate), across(queries, d_up), across(hidden, d_output))
    return (grad_queries, partial_value)

def schulz_forward(begin):
    current = begin
    saved = []
    for sweep in range(NS_STEPS):
        gram = against(current, current).astype(jnp.bfloat16)
        blend = (cube_coef * gram.astype(jnp.float32) + fifth_coef * product(gram, gram)).astype(jnp.bfloat16)
        following = (lin_coef * current.astype(jnp.float32) + product(blend, current)).astype(jnp.bfloat16)
        saved.append((current, gram, blend))
        current = following
    return (current, saved)

def schulz_backward(cotan, saved):
    current = cotan
    for iterate, gram, blend in reversed(saved):
        cross = against(current, iterate)
        symmetric = (cross + cross.T).astype(jnp.bfloat16)
        bent = product(symmetric, gram)
        mixed = (cube_coef * symmetric.astype(jnp.float32) + fifth_coef * (bent + bent.T)).astype(jnp.bfloat16)
        current = (lin_coef * current.astype(jnp.float32) + product(blend, current) + product(mixed, iterate)).astype(jnp.bfloat16)
    return current

def restore(bottom, fast, root):
    norm = root + fro_eps
    inner = jnp.sum(bottom.astype(jnp.float32) * fast)
    return (bottom.astype(jnp.float32) / norm - fast * (inner / (norm * norm * root))).astype(jnp.bfloat16)

def reference(queries, keys, values, upstream, out_gain, gate_weight, up_weight, down_weight):
    heads = gate_weight.shape[0]
    width = heads * D
    scale = 1.0 / math.sqrt(BLOCK)
    records = []
    power_sums = [jnp.zeros((BLOCK,), jnp.float32), jnp.zeros((BLOCK,), jnp.float32)]
    dot_sums = [jnp.zeros((BLOCK,), jnp.float32), jnp.zeros((BLOCK,), jnp.float32)]
    for head in range(heads):
        lower = head * D
        first = (gate_weight[head], up_weight[head], down_weight[head])
        fast, unused = fast_forward(keys[:, lower:lower + D], values[:, lower:lower + D], first)
        roots = [jnp.sqrt(jnp.sum(item * item)) for item in fast]
        begins = [(fast[which] / (roots[which] + fro_eps)).astype(jnp.bfloat16) for which in range(3)]
        forward = [schulz_forward(begin) for begin in begins]
        second = tuple(((first[which].astype(jnp.float32) - forward[which][0].astype(jnp.float32)).astype(jnp.bfloat16) for which in range(3)))
        for block_index, weights in ((0, first), (1, second)):
            output = apply_forward(queries[block_index][:, lower:lower + D], weights)[4]
            weighted = out_gain[lower:lower + D] * upstream[block_index][:, lower:lower + D].astype(jnp.float32)
            power_sums[block_index] = power_sums[block_index] + lax.optimization_barrier(jnp.sum(output * output, axis=1))
            dot_sums[block_index] = dot_sums[block_index] + lax.optimization_barrier(jnp.sum(weighted * output, axis=1))
        records.append((first, second, fast, roots, forward))
    inverse = [lax.rsqrt(power_sums[which] / width + rms_eps) for which in range(2)]
    means = [dot_sums[which] / width for which in range(2)]
    query_grads, key_grads, value_grads = ([], [], [])
    gate_grads, up_grads, down_grads = ([], [], [])
    for head in range(heads):
        lower = head * D
        first, second, fast, roots, forward = records[head]
        gain_part = out_gain[lower:lower + D]
        block_grads = []
        partials = []
        for block_index, weights in ((0, first), (1, second)):
            local_queries = queries[block_index][:, lower:lower + D]
            saved = apply_forward(local_queries, weights)
            grad_part, partial_value = apply_backward(local_queries, weights, saved, upstream[block_index][:, lower:lower + D], gain_part, inverse[block_index], means[block_index])
            block_grads.append(grad_part)
            partials.append(partial_value)
        tops = [(-partials[1][which]).astype(jnp.bfloat16) for which in range(3)]
        bottoms = [schulz_backward(tops[which], forward[which][1]) for which in range(3)]
        cots = tuple((restore(bottoms[which], fast[which], roots[which]) for which in range(3)))
        local_keys = keys[:, lower:lower + D]
        local_values = values[:, lower:lower + D]
        unused, saved_keys = fast_forward(local_keys, local_values, first)
        grad_key_part, grad_value_part, second_order = fast_second(local_keys, local_values, first, saved_keys, cots)
        totals = [(partials[0][which] + second_order[which] + partials[1][which]) * scale for which in range(3)]
        query_grads.append(jnp.stack(block_grads))
        key_grads.append(grad_key_part)
        value_grads.append(grad_value_part)
        gate_grads.append(totals[0])
        up_grads.append(totals[1])
        down_grads.append(totals[2])
    return (jnp.concatenate(query_grads, axis=2), jnp.concatenate(key_grads, axis=1), jnp.concatenate(value_grads, axis=1), jnp.stack(gate_grads), jnp.stack(up_grads), jnp.stack(down_grads))
```

```python
import functools
import math

import jax
import jax.numpy as jnp
from jax import lax
from jax.experimental import pallas as pl
from jax.experimental.pallas import tpu as pltpu
from jax.sharding import PartitionSpec as P

NS_STEPS = 2


lin_coef = 3.4445
cube_coef = -4.775
fifth_coef = 2.0315
rms_eps = 1e-06
fro_eps = 1e-07

bf16 = jnp.bfloat16
f32 = jnp.float32
ROWS = 256


def product(left, right):
    return jnp.dot(left, right, preferred_element_type=jnp.float32)


def across(left, right):
    return lax.dot_general(
        left, right, (((0,), (0,)), ((), ())), preferred_element_type=jnp.float32
    )


def against(left, right):
    return lax.dot_general(
        left, right, (((1,), (1,)), ((), ())), preferred_element_type=jnp.float32
    )


def fast_forward(keys, values, weights):
    gate_weight, up_weight, down_weight = weights
    gate_pre = product(keys, gate_weight)
    up_pre = product(keys, up_weight)
    sigma = jax.nn.sigmoid(gate_pre)
    active = gate_pre * sigma
    hidden = (active * up_pre).astype(jnp.bfloat16)
    back = -against(values, down_weight)
    slope = sigma * (1.0 + gate_pre * (1.0 - sigma))
    d_gate = (back * up_pre * slope).astype(jnp.bfloat16)
    d_up = (back * active).astype(jnp.bfloat16)
    fast = (across(keys, d_gate), across(keys, d_up), -across(hidden, values))
    saved = (gate_pre, up_pre, sigma, active, hidden, back, slope, d_gate, d_up)
    return (fast, saved)


def fast_second(keys, values, weights, saved, cots):
    gate_weight, up_weight, down_weight = weights
    gate_pre, up_pre, sigma, active, hidden, back, slope, d_gate, d_up = saved
    cot_gate, cot_up, cot_down = cots
    along_gate = product(keys, cot_gate)
    along_up = product(keys, cot_up)
    along_hidden = -against(values, cot_down)
    curve = sigma * (1.0 - sigma) * (2.0 + gate_pre * (1.0 - 2.0 * sigma))
    d_back = (along_gate * up_pre * slope + along_up * active).astype(jnp.bfloat16)
    d_upper = (along_gate * back * slope + along_hidden * active).astype(jnp.bfloat16)
    d_lower = (
        along_gate * back * up_pre * curve + along_up * back * slope + along_hidden * up_pre * slope
    ).astype(jnp.bfloat16)
    grad_keys = (
        against(d_gate, cot_gate)
        + against(d_up, cot_up)
        + against(d_lower, gate_weight)
        + against(d_upper, up_weight)
    ).astype(jnp.bfloat16)
    grad_values = (-product(hidden, cot_down) - product(d_back, down_weight)).astype(jnp.bfloat16)
    partial_value = (across(keys, d_lower), across(keys, d_upper), -across(d_back, values))
    return (grad_keys, grad_values, partial_value)


def apply_forward(queries, weights):
    gate_weight, up_weight, down_weight = weights
    gate_pre = product(queries, gate_weight)
    up_pre = product(queries, up_weight)
    sigma = jax.nn.sigmoid(gate_pre)
    hidden = (gate_pre * sigma * up_pre).astype(jnp.bfloat16)
    output = product(hidden, down_weight)
    return (gate_pre, up_pre, sigma, hidden, output)


def statistics(output, upstream, out_gain, width):
    weighted = out_gain * upstream.astype(jnp.float32)
    sums = lax.psum((jnp.sum(output * output, axis=1), jnp.sum(weighted * output, axis=1)), "head")
    return (lax.rsqrt(sums[0] / width + rms_eps), sums[1] / width)


def apply_backward(queries, weights, saved, upstream, out_gain, width):
    gate_weight, up_weight, down_weight = weights
    gate_pre, up_pre, sigma, hidden, output = saved
    inverse_rms, mean_dot = statistics(output, upstream, out_gain, width)
    weighted = out_gain * upstream.astype(jnp.float32)
    d_output = (
        inverse_rms[:, None] * weighted
        - output * (inverse_rms * inverse_rms * inverse_rms * mean_dot)[:, None]
    ).astype(jnp.bfloat16)
    back = against(d_output, down_weight)
    slope = sigma * (1.0 + gate_pre * (1.0 - sigma))
    d_gate = (back * up_pre * slope).astype(jnp.bfloat16)
    d_up = (back * gate_pre * sigma).astype(jnp.bfloat16)
    grad_queries = (against(d_gate, gate_weight) + against(d_up, up_weight)).astype(jnp.bfloat16)
    partial_value = (across(queries, d_gate), across(queries, d_up), across(hidden, d_output))
    return (grad_queries, partial_value)


def schulz_forward(begin):
    current = begin
    saved = []
    for sweep in range(NS_STEPS):
        gram = against(current, current).astype(jnp.bfloat16)
        blend = (cube_coef * gram.astype(jnp.float32) + fifth_coef * product(gram, gram)).astype(
            jnp.bfloat16
        )
        following = (lin_coef * current.astype(jnp.float32) + product(blend, current)).astype(
            jnp.bfloat16
        )
        saved.append((current, gram, blend))
        current = following
    return (current, saved)


def schulz_backward(cotan, saved):
    current = cotan
    for iterate, gram, blend in reversed(saved):
        cross = against(current, iterate)
        symmetric = (cross + cross.T).astype(jnp.bfloat16)
        bent = product(symmetric, gram)
        mixed = (cube_coef * symmetric.astype(jnp.float32) + fifth_coef * (bent + bent.T)).astype(
            jnp.bfloat16
        )
        current = (
            lin_coef * current.astype(jnp.float32)
            + product(blend, current)
            + product(mixed, iterate)
        ).astype(jnp.bfloat16)
    return current


def split_tokens(queries, keys, values, upstream, out_gain, gate_weight, up_weight, down_weight):
    shards = lax.axis_size("tok")
    owner = lax.axis_index("tok")
    width = out_gain.shape[0] * lax.axis_size("head")
    scale = 1.0 / math.sqrt(queries.shape[1] * shards)
    own_rows = (gate_weight[0], up_weight[0], down_weight[0])
    starts = [owner * own_rows[which].shape[0] for which in range(3)]
    first = tuple(lax.all_gather(rows, "tok", axis=0, tiled=True) for rows in own_rows)
    fast, saved_keys = fast_forward(keys, values, first)
    apply_first = apply_forward(queries[0], first)
    grad_first, partial_first = apply_backward(
        queries[0], first, apply_first, upstream[0], out_gain, width
    )
    totals = lax.psum((fast[0], fast[1], fast[2]), "tok")
    roots = [jnp.sqrt(jnp.sum(totals[which] * totals[which])) for which in range(3)]
    forward = [
        schulz_forward((totals[which] / (roots[which] + fro_eps)).astype(jnp.bfloat16))
        for which in range(3)
    ]
    second = tuple(
        (first[which].astype(jnp.float32) - forward[which][0].astype(jnp.float32)).astype(
            jnp.bfloat16
        )
        for which in range(3)
    )
    apply_second = apply_forward(queries[1], second)
    grad_second, partial_second = apply_backward(
        queries[1], second, apply_second, upstream[1], out_gain, width
    )
    rates = lax.psum((partial_second[0], partial_second[1], partial_second[2]), "tok")
    bottoms = [
        schulz_backward((-rates[which]).astype(jnp.bfloat16), forward[which][1])
        for which in range(3)
    ]
    cots = []
    for which in range(3):
        norm = roots[which] + fro_eps
        inner = jnp.sum(bottoms[which].astype(jnp.float32) * totals[which])
        cots.append(
            (
                bottoms[which].astype(jnp.float32) / norm
                - totals[which] * (inner / (norm * norm * roots[which]))
            ).astype(jnp.bfloat16)
        )
    grad_keys, grad_values, second_order = fast_second(keys, values, first, saved_keys, cots)
    grads = []
    for which in range(3):
        rate_rows = lax.dynamic_slice_in_dim(
            rates[which], starts[which], own_rows[which].shape[0], 0
        )
        summed = lax.psum_scatter(
            partial_first[which] + second_order[which], "tok", scatter_dimension=0, tiled=True
        )
        grads.append(((summed + rate_rows) * scale)[None])
    grad_queries = jnp.stack([grad_first, grad_second])
    return (grad_queries, grad_keys, grad_values, *grads)


def shift(array, ring, step):
    pairs = [
        (o * 2 + i, ((o + step) % ring) * 2 + i) for o in range(ring) for i in range(2)
    ]
    return lax.ppermute(array, "tok", pairs)


def swap(array, ring):
    return lax.ppermute(array, "tok", [(i, i ^ 1) for i in range(2 * ring)])


def gather_pieces(own, ring):
    rows = own.shape[0]
    found = [(0, 0, own)]
    up = down = own
    for step in range(1, ring // 2 + 1):
        if 2 * step < ring:
            up, down = shift(up, ring, 1), shift(down, ring, -1)
            found += [(-step, 0, up), (step, 0, down)]
        else:
            half = rows // 2
            found.append((-step, 0, shift(up[:half], ring, 1)))
            found.append((-step, half, shift(down[half:], ring, -1)))
    pieces = [(outer, 0, first, array) for outer, first, array in found]
    pieces += [(outer, 1, first, swap(array, ring)) for outer, first, array in found]
    return pieces


def head_sums(stats):
    heads = lax.axis_size("head")
    others = [
        lax.ppermute(stats, "head", [(i, (i + k) % heads) for i in range(heads)])
        for k in range(1, heads)
    ]
    return jnp.stack([stats, *others])


def unpack_copies(layout, segments, ring, me, refs, targets, sems):
    copies = []
    outer_me, inner_me = me // 2, me % 2
    slots = {}
    for (outer, flip, first, rows), ref in zip(layout, refs):
        slot = slots.setdefault((outer, flip), len(slots))
        owner = ((outer_me + outer + ring) % ring) * 2 + (inner_me + flip) % 2
        begin = 0
        for (count, by_slot), target in zip(segments, targets):
            low, high = max(begin, first), min(begin + count, first + rows)
            if low < high:
                place = slot * count + low - begin
                if not by_slot:
                    place = pl.multiple_of(owner * count, 16) + (low - begin)
                copies.append(
                    pltpu.make_async_copy(
                        ref.at[pl.ds(low - first, high - low)],
                        target.at[pl.ds(place, high - low)],
                        sems.at[len(copies)],
                    )
                )
            begin += count
    return copies


def chunks_of(tokens):
    step = min(ROWS, tokens)
    return [slice(i, i + step) for i in range(0, tokens, step)]


def fast_kernel(layout, segments, ring, me_ref, *refs):
    count = len(layout)
    pieces, refs = refs[:count], refs[count:]
    (wg, wu, wd, keys, values, gk_ref, uk_ref, back_ref) = refs[:8]
    xs, grams, blends, nexts, totals, roots = refs[8:14]
    d_gate, d_up, hidden, sems = refs[14:]
    copies = unpack_copies(
        layout, segments, ring, me_ref[0], pieces, (wg, wu, wd, keys, values), sems
    )
    for copy in copies:
        copy.start()
    for copy in copies:
        copy.wait()
    for part in chunks_of(keys.shape[0]):
        gk = product(keys[part], wg[...])
        uk = product(keys[part], wu[...])
        back = -against(values[part], wd[...])
        sigma = jax.nn.sigmoid(gk)
        active = gk * sigma
        slope = sigma * (1.0 + gk * (1.0 - sigma))
        hidden[part] = (active * uk).astype(bf16)
        d_gate[part] = (back * uk * slope).astype(bf16)
        d_up[part] = (back * active).astype(bf16)
        gk_ref[part], uk_ref[part], back_ref[part] = gk, uk, back
    totals[0] = across(keys[...], d_gate[...])
    totals[1] = across(keys[...], d_up[...])
    totals[2] = -across(hidden[...], values[...])
    for which, weight in enumerate((wg, wu, wd)):
        total = totals[which]
        root = jnp.sqrt(jnp.sum(total * total, keepdims=True))
        roots[which] = jnp.broadcast_to(root, roots.shape[1:])
        xs[which, 0] = (total / (root + fro_eps)).astype(bf16)
        for sweep in range(NS_STEPS):
            current = xs[which, sweep]
            gram = against(current, current).astype(bf16)
            blend = (cube_coef * gram.astype(f32) + fifth_coef * product(gram, gram)).astype(bf16)
            following = (lin_coef * current.astype(f32) + product(blend, current)).astype(bf16)
            grams[which, sweep] = gram
            blends[which, sweep] = blend
            if sweep + 1 < NS_STEPS:
                xs[which, sweep + 1] = following
        nexts[which] = (weight[...].astype(f32) - following.astype(f32)).astype(bf16)


def row_sums(columns, tokens):
    lanes = lax.broadcasted_iota(jnp.int32, (tokens, 128), 1)
    spread = jnp.where(lanes == 0, columns[0], jnp.where(lanes == 1, columns[1], 0.0))
    return spread.T[:8]


def forward_part(queries, upstream, gain, wg, wu, wd, gq_ref, uq_ref, hidden_ref, out_ref, stats):
    for part in chunks_of(queries.shape[0]):
        gq = product(queries[part], wg[...])
        uq = product(queries[part], wu[...])
        hidden = (gq * jax.nn.sigmoid(gq) * uq).astype(bf16)
        output = product(hidden, wd[...])
        weighted = gain[...] * upstream[part].astype(f32)
        sums = (
            jnp.sum(output * output, axis=1, keepdims=True),
            jnp.sum(weighted * output, axis=1, keepdims=True),
        )
        stats[:, part] = row_sums(sums, output.shape[0])
        gq_ref[part], uq_ref[part], hidden_ref[part], out_ref[part] = gq, uq, hidden, output


def backward_part(
    width, queries, upstream, gain, wg, wu, wd, gq_ref, uq_ref, hidden, out_ref, sums,
    grad_ref, d_gate, d_up, d_out, own,
):
    for part in chunks_of(queries.shape[0]):
        total = jnp.sum(sums[:, :, part], axis=0)
        tokens = total.shape[1]
        square = total[0:1] / width
        inverse = lax.rsqrt(square + rms_eps)
        pull = inverse * inverse * inverse * (total[1:2] / width)
        index = lax.broadcasted_iota(jnp.int32, (128, tokens), 0)
        columns = jnp.where(index == 0, inverse, jnp.where(index == 1, pull, 0.0)).T
        inverse, pull = columns[:, 0:1], columns[:, 1:2]
        weighted = gain[...] * upstream[part].astype(f32)
        d_output = (inverse * weighted - out_ref[part] * pull).astype(bf16)
        back = against(d_output, wd[...])
        gq, uq = gq_ref[part], uq_ref[part]
        sigma = jax.nn.sigmoid(gq)
        d_gate[part] = (back * uq * sigma * (1.0 + gq * (1.0 - sigma))).astype(bf16)
        d_up[part] = (back * gq * sigma).astype(bf16)
        d_out[part] = d_output
    grad_ref[...] = (
        against(d_gate[:own], wg[...]) + against(d_up[:own], wu[...])
    ).astype(bf16)


def first_forward_kernel(queries, upstream, gain, wg, wu, wd, gq, uq, hidden, out, stats):
    forward_part(queries, upstream, gain, wg, wu, wd, gq, uq, hidden, out, stats)


def first_backward_kernel(
    width, queries, upstream, gain, wg, wu, wd, gq, uq, hidden, out, sums,
    grad, partial, d_gate, d_up, d_out,
):
    backward_part(
        width, queries, upstream, gain, wg, wu, wd, gq, uq, hidden, out, sums,
        grad, d_gate, d_up, d_out, queries.shape[0],
    )
    partial[0] = across(queries[...], d_gate[...]).astype(bf16)
    partial[1] = across(queries[...], d_up[...]).astype(bf16)
    partial[2] = across(hidden[...], d_out[...]).astype(bf16)


def second_forward_kernel(
    layout, segments, ring, me_ref, gain, nexts, *refs
):
    count = len(layout)
    pieces, refs = refs[:count], refs[count:]
    queries, upstream, gq, uq, hidden, out, stats, sems = refs
    copies = unpack_copies(layout, segments, ring, me_ref[0], pieces, (queries, upstream), sems)
    for copy in copies:
        copy.start()
    for copy in copies:
        copy.wait()
    forward_part(
        queries, upstream, gain, nexts.at[0], nexts.at[1], nexts.at[2], gq, uq, hidden, out, stats
    )


def last_kernel(
    width, own, me_ref, queries, upstream, gain, nexts, gq, uq, hidden_q, out, sums,
    wg, wu, wd, keys, values, gk_ref, uk_ref, back_ref, xs, grams, blends, totals, roots,
    grad_queries, grad_keys, grad_values, grads,
    d_gate, d_up, d_out, rates, cots, lower, upper, d_back, pk, rk, hk,
):
    backward_part(
        width, queries, upstream, gain, nexts.at[0], nexts.at[1], nexts.at[2],
        gq, uq, hidden_q, out, sums, grad_queries, d_gate, d_up, d_out, own,
    )
    rates[0] = across(queries[...], d_gate[...])
    rates[1] = across(queries[...], d_up[...])
    rates[2] = across(hidden_q[...], d_out[...])
    for which in range(3):
        current = (-rates[which]).astype(bf16)
        for sweep in reversed(range(NS_STEPS)):
            iterate, gram, blend = xs[which, sweep], grams[which, sweep], blends[which, sweep]
            symmetric = (against(current, iterate) + against(iterate, current)).astype(bf16)
            bent = product(symmetric, gram) + product(gram, symmetric)
            mixed = (cube_coef * symmetric.astype(f32) + fifth_coef * bent).astype(bf16)
            current = (
                lin_coef * current.astype(f32) + product(blend, current) + product(mixed, iterate)
            ).astype(bf16)
        root = roots[which, 0:1, 0:1]
        norm = root + fro_eps
        total = totals[which]
        bottom = current.astype(f32)
        inner = jnp.sum(bottom * total, keepdims=True)
        cots[which] = (bottom / norm - total * (inner / (norm * norm * root))).astype(bf16)
    for part in chunks_of(keys.shape[0]):
        gk, uk, back = gk_ref[part], uk_ref[part], back_ref[part]
        sigma = jax.nn.sigmoid(gk)
        active = gk * sigma
        slope = sigma * (1.0 + gk * (1.0 - sigma))
        curve = sigma * (1.0 - sigma) * (2.0 + gk * (1.0 - 2.0 * sigma))
        ek = product(keys[part], cots[0])
        fk = product(keys[part], cots[1])
        hk_part = -against(values[part], cots[2])
        d_back[part] = (ek * uk * slope + fk * active).astype(bf16)
        upper[part] = (ek * back * slope + hk_part * active).astype(bf16)
        lower[part] = (
            ek * back * uk * curve + fk * back * slope + hk_part * uk * slope
        ).astype(bf16)
        if part.start == 0:
            pk[...] = (back * uk * slope).astype(bf16)[:own]
            rk[...] = (back * active).astype(bf16)[:own]
            hk[...] = (active * uk).astype(bf16)[:own]
    grad_keys[...] = (
        against(pk[...], cots[0])
        + against(rk[...], cots[1])
        + against(lower[:own], wg[...])
        + against(upper[:own], wu[...])
    ).astype(bf16)
    grad_values[...] = (-product(hk[...], cots[2]) - product(d_back[:own], wd[...])).astype(bf16)
    rates[0] += across(keys[...], lower[...])
    rates[1] += across(keys[...], upper[...])
    rates[2] -= across(d_back[...], values[...])
    rows = grads.shape[1]
    start = pl.multiple_of(me_ref[0] * rows, 16)
    for which in range(3):
        grads[which] = rates[which, pl.ds(start, rows)]


def vmem():
    return pl.BlockSpec(memory_space=pltpu.VMEM)


def smem():
    return pl.BlockSpec(memory_space=pltpu.SMEM)


def anywhere():
    return pl.BlockSpec(memory_space=pl.ANY)


def params(mib):
    return pltpu.CompilerParams(vmem_limit_bytes=mib * 2**20)


def reduce_first(partial, ring, me):
    whole, height, depth = partial.shape
    inner = me % 2
    blocks = partial.reshape(whole, ring, 2, height // (2 * ring), depth)
    kept = lax.dynamic_index_in_dim(blocks, inner, 2, keepdims=False)
    sent = lax.dynamic_index_in_dim(blocks, 1 - inner, 2, keepdims=False)
    pair = kept.astype(f32) + swap(sent, ring).astype(f32)
    outer = me // 2
    result = lax.dynamic_index_in_dim(pair, outer, 1, keepdims=False)
    for step in range(1, ring):
        block = lax.dynamic_index_in_dim(pair, (outer + step) % ring, 1, keepdims=False)
        result = result + shift(block.astype(bf16), ring, step).astype(f32)
    return result


def gather_tokens(queries, keys, values, upstream, out_gain, gate_weight, up_weight, down_weight):
    shards = lax.axis_size("tok")
    ring = shards // 2
    me = lax.axis_index("tok")
    me_ref = jnp.reshape(me, (1,)).astype(jnp.int32)
    own, depth = keys.shape
    rows = gate_weight.shape[1]
    hidden = gate_weight.shape[2]
    tokens = own * shards
    width = out_gain.shape[0] * lax.axis_size("head")
    scale = 1.0 / math.sqrt(tokens)
    gain = out_gain[None]
    S = jax.ShapeDtypeStruct

    packed = jnp.concatenate([gate_weight[0], up_weight[0], down_weight[0], keys, values])
    pieces = gather_pieces(packed, ring)
    segments = ((rows, False), (rows, False), (down_weight.shape[1], False), (own, True), (own, True))
    layout = [(o, f, r, a.shape[0]) for o, f, r, a in pieces]
    matrix = (depth, hidden)
    (
        wg, wu, wd, all_keys, all_values, gk, uk, back, xs, grams, blends, nexts, totals, roots
    ) = pl.pallas_call(
        functools.partial(fast_kernel, layout, segments, ring),
        out_shape=(
            S(matrix, bf16), S(matrix, bf16), S(matrix, bf16),
            S((tokens, depth), bf16), S((tokens, depth), bf16),
            S((tokens, hidden), f32), S((tokens, hidden), f32), S((tokens, hidden), f32),
            S((3, NS_STEPS, *matrix), bf16), S((3, NS_STEPS, *matrix), bf16),
            S((3, NS_STEPS, *matrix), bf16), S((3, *matrix), bf16),
            S((3, *matrix), f32), S((3, 8, 128), f32),
        ),
        in_specs=[smem()] + [anywhere()] * len(pieces),
        out_specs=[vmem()] * 14,
        scratch_shapes=[
            pltpu.VMEM((tokens, hidden), bf16),
            pltpu.VMEM((tokens, hidden), bf16),
            pltpu.VMEM((tokens, hidden), bf16),
            pltpu.SemaphoreType.DMA((5 * len(pieces),)),
        ],
        compiler_params=params(56),
    )(me_ref, *[piece[3] for piece in pieces])

    gq0, uq0, hidden0, out0, stats0 = pl.pallas_call(
        first_forward_kernel,
        out_shape=(
            S((own, hidden), f32), S((own, hidden), f32), S((own, hidden), bf16),
            S((own, depth), f32), S((8, own), f32),
        ),
        in_specs=[vmem()] * 6,
        out_specs=[vmem()] * 5,
        compiler_params=params(16),
    )(queries[0], upstream[0], gain, wg, wu, wd)
    sums0 = head_sums(stats0)
    grad_first, partial = pl.pallas_call(
        functools.partial(first_backward_kernel, width),
        out_shape=(S((own, depth), bf16), S((3, *matrix), bf16)),
        in_specs=[vmem()] * 11,
        out_specs=[vmem()] * 2,
        scratch_shapes=[pltpu.VMEM((own, hidden), bf16)] * 2 + [pltpu.VMEM((own, depth), bf16)],
        compiler_params=params(24),
    )(queries[0], upstream[0], gain, wg, wu, wd, gq0, uq0, hidden0, out0, sums0)
    first_rows = reduce_first(partial, ring, me)

    packed = jnp.concatenate([queries[1], upstream[1]])
    packed, _ = lax.optimization_barrier((packed, pieces[-1][3]))
    pieces = gather_pieces(packed, ring)
    segments = ((own, True), (own, True))
    layout = [(o, f, r, a.shape[0]) for o, f, r, a in pieces]
    all_queries, all_upstream, gq, uq, hidden_q, out, stats = pl.pallas_call(
        functools.partial(second_forward_kernel, layout, segments, ring),
        out_shape=(
            S((tokens, depth), bf16), S((tokens, depth), bf16),
            S((tokens, hidden), f32), S((tokens, hidden), f32), S((tokens, hidden), bf16),
            S((tokens, depth), f32), S((8, tokens), f32),
        ),
        in_specs=[smem(), vmem(), vmem()] + [anywhere()] * len(pieces),
        out_specs=[vmem()] * 7,
        scratch_shapes=[pltpu.SemaphoreType.DMA((2 * len(pieces),))],
        compiler_params=params(32),
    )(me_ref, gain, nexts, *[piece[3] for piece in pieces])
    sums = head_sums(stats)

    grad_second, grad_keys, grad_values, last_rows = pl.pallas_call(
        functools.partial(last_kernel, width, own),
        out_shape=(
            S((own, depth), bf16), S((own, depth), bf16), S((own, depth), bf16),
            S((3, rows, hidden), f32),
        ),
        in_specs=[smem()] + [vmem()] * 22,
        out_specs=[vmem()] * 4,
        scratch_shapes=[
            pltpu.VMEM((tokens, hidden), bf16),
            pltpu.VMEM((tokens, hidden), bf16),
            pltpu.VMEM((tokens, depth), bf16),
            pltpu.VMEM((3, *matrix), f32),
            pltpu.VMEM((3, *matrix), bf16),
            pltpu.VMEM((tokens, hidden), bf16),
            pltpu.VMEM((tokens, hidden), bf16),
            pltpu.VMEM((tokens, hidden), bf16),
            pltpu.VMEM((own, hidden), bf16),
            pltpu.VMEM((own, hidden), bf16),
            pltpu.VMEM((own, hidden), bf16),
        ],
        compiler_params=params(60),
    )(
        me_ref, all_queries, all_upstream, gain, nexts, gq, uq, hidden_q, out, sums,
        wg, wu, wd, all_keys, all_values, gk, uk, back, xs, grams, blends, totals, roots,
    )
    grads = (last_rows + first_rows) * scale
    grad_queries = jnp.stack([grad_first, grad_second])
    return (grad_queries, grad_keys, grad_values, grads[0:1], grads[1:2], grads[2:3])


def per_device(queries, keys, values, upstream, out_gain, gate_weight, up_weight, down_weight):
    shards = lax.axis_size("tok")
    tokens = keys.shape[0] * shards
    few = 4 * tokens <= 12 * gate_weight.shape[2] and shards % 2 == 0
    plan = gather_tokens if few else split_tokens
    return plan(queries, keys, values, upstream, out_gain, gate_weight, up_weight, down_weight)


def solution(mesh):
    in_specs = (
        P(None, "tok", "head"),
        P("tok", "head"),
        P("tok", "head"),
        P(None, "tok", "head"),
        P("head"),
        P("head", "tok", None),
        P("head", "tok", None),
        P("head", "tok", None),
    )
    out_specs = (
        P(None, "tok", "head"),
        P("tok", "head"),
        P("tok", "head"),
        P("head", "tok", None),
        P("head", "tok", None),
        P("head", "tok", None),
    )
    return jax.shard_map(
        per_device, mesh=mesh, in_specs=in_specs, out_specs=out_specs, check_vma=False
    )
```

```python
import functools
import math

import jax
import jax.numpy as jnp
from jax import lax
from jax.experimental import pallas as pl
from jax.experimental.pallas import tpu as pltpu
from jax.sharding import PartitionSpec as P

NS_STEPS = 2


lin_coef = 3.4445
cube_coef = -4.775
fifth_coef = 2.0315
rms_eps = 1e-06
fro_eps = 1e-07

bf16 = jnp.bfloat16
f32 = jnp.float32
ROWS = 256


def product(left, right):
    return jnp.dot(left, right, preferred_element_type=jnp.float32)


def across(left, right):
    return lax.dot_general(
        left, right, (((0,), (0,)), ((), ())), preferred_element_type=jnp.float32
    )


def against(left, right):
    return lax.dot_general(
        left, right, (((1,), (1,)), ((), ())), preferred_element_type=jnp.float32
    )


def fast_forward(keys, values, weights):
    gate_weight, up_weight, down_weight = weights
    gate_pre = product(keys, gate_weight)
    up_pre = product(keys, up_weight)
    sigma = jax.nn.sigmoid(gate_pre)
    active = gate_pre * sigma
    hidden = (active * up_pre).astype(jnp.bfloat16)
    back = -against(values, down_weight)
    slope = sigma * (1.0 + gate_pre * (1.0 - sigma))
    d_gate = (back * up_pre * slope).astype(jnp.bfloat16)
    d_up = (back * active).astype(jnp.bfloat16)
    fast = (across(keys, d_gate), across(keys, d_up), -across(hidden, values))
    saved = (gate_pre, up_pre, sigma, active, hidden, back, slope, d_gate, d_up)
    return (fast, saved)


def fast_second(keys, values, weights, saved, cots):
    gate_weight, up_weight, down_weight = weights
    gate_pre, up_pre, sigma, active, hidden, back, slope, d_gate, d_up = saved
    cot_gate, cot_up, cot_down = cots
    along_gate = product(keys, cot_gate)
    along_up = product(keys, cot_up)
    along_hidden = -against(values, cot_down)
    curve = sigma * (1.0 - sigma) * (2.0 + gate_pre * (1.0 - 2.0 * sigma))
    d_back = (along_gate * up_pre * slope + along_up * active).astype(jnp.bfloat16)
    d_upper = (along_gate * back * slope + along_hidden * active).astype(jnp.bfloat16)
    d_lower = (
        along_gate * back * up_pre * curve + along_up * back * slope + along_hidden * up_pre * slope
    ).astype(jnp.bfloat16)
    grad_keys = (
        against(d_gate, cot_gate)
        + against(d_up, cot_up)
        + against(d_lower, gate_weight)
        + against(d_upper, up_weight)
    ).astype(jnp.bfloat16)
    grad_values = (-product(hidden, cot_down) - product(d_back, down_weight)).astype(jnp.bfloat16)
    partial_value = (across(keys, d_lower), across(keys, d_upper), -across(d_back, values))
    return (grad_keys, grad_values, partial_value)


def apply_forward(queries, weights):
    gate_weight, up_weight, down_weight = weights
    gate_pre = product(queries, gate_weight)
    up_pre = product(queries, up_weight)
    sigma = jax.nn.sigmoid(gate_pre)
    hidden = (gate_pre * sigma * up_pre).astype(jnp.bfloat16)
    output = product(hidden, down_weight)
    return (gate_pre, up_pre, sigma, hidden, output)


def statistics(output, upstream, out_gain, width):
    weighted = out_gain * upstream.astype(jnp.float32)
    sums = lax.psum((jnp.sum(output * output, axis=1), jnp.sum(weighted * output, axis=1)), "head")
    return (lax.rsqrt(sums[0] / width + rms_eps), sums[1] / width)


def apply_backward(queries, weights, saved, upstream, out_gain, width):
    gate_weight, up_weight, down_weight = weights
    gate_pre, up_pre, sigma, hidden, output = saved
    inverse_rms, mean_dot = statistics(output, upstream, out_gain, width)
    weighted = out_gain * upstream.astype(jnp.float32)
    d_output = (
        inverse_rms[:, None] * weighted
        - output * (inverse_rms * inverse_rms * inverse_rms * mean_dot)[:, None]
    ).astype(jnp.bfloat16)
    back = against(d_output, down_weight)
    slope = sigma * (1.0 + gate_pre * (1.0 - sigma))
    d_gate = (back * up_pre * slope).astype(jnp.bfloat16)
    d_up = (back * gate_pre * sigma).astype(jnp.bfloat16)
    grad_queries = (against(d_gate, gate_weight) + against(d_up, up_weight)).astype(jnp.bfloat16)
    partial_value = (across(queries, d_gate), across(queries, d_up), across(hidden, d_output))
    return (grad_queries, partial_value)


def schulz_forward(begin):
    current = begin
    saved = []
    for sweep in range(NS_STEPS):
        gram = against(current, current).astype(jnp.bfloat16)
        blend = (cube_coef * gram.astype(jnp.float32) + fifth_coef * product(gram, gram)).astype(
            jnp.bfloat16
        )
        following = (lin_coef * current.astype(jnp.float32) + product(blend, current)).astype(
            jnp.bfloat16
        )
        saved.append((current, gram, blend))
        current = following
    return (current, saved)


def schulz_backward(cotan, saved):
    current = cotan
    for iterate, gram, blend in reversed(saved):
        cross = against(current, iterate)
        symmetric = (cross + cross.T).astype(jnp.bfloat16)
        bent = product(symmetric, gram)
        mixed = (cube_coef * symmetric.astype(jnp.float32) + fifth_coef * (bent + bent.T)).astype(
            jnp.bfloat16
        )
        current = (
            lin_coef * current.astype(jnp.float32)
            + product(blend, current)
            + product(mixed, iterate)
        ).astype(jnp.bfloat16)
    return current


def split_tokens(queries, keys, values, upstream, out_gain, gate_weight, up_weight, down_weight):
    shards = lax.axis_size("tok")
    owner = lax.axis_index("tok")
    width = out_gain.shape[0] * lax.axis_size("head")
    scale = 1.0 / math.sqrt(queries.shape[1] * shards)
    own_rows = (gate_weight[0], up_weight[0], down_weight[0])
    starts = [owner * own_rows[which].shape[0] for which in range(3)]
    first = tuple(lax.all_gather(rows, "tok", axis=0, tiled=True) for rows in own_rows)
    fast, saved_keys = fast_forward(keys, values, first)
    apply_first = apply_forward(queries[0], first)
    grad_first, partial_first = apply_backward(
        queries[0], first, apply_first, upstream[0], out_gain, width
    )
    totals = lax.psum((fast[0], fast[1], fast[2]), "tok")
    roots = [jnp.sqrt(jnp.sum(totals[which] * totals[which])) for which in range(3)]
    forward = [
        schulz_forward((totals[which] / (roots[which] + fro_eps)).astype(jnp.bfloat16))
        for which in range(3)
    ]
    second = tuple(
        (first[which].astype(jnp.float32) - forward[which][0].astype(jnp.float32)).astype(
            jnp.bfloat16
        )
        for which in range(3)
    )
    apply_second = apply_forward(queries[1], second)
    grad_second, partial_second = apply_backward(
        queries[1], second, apply_second, upstream[1], out_gain, width
    )
    rates = lax.psum((partial_second[0], partial_second[1], partial_second[2]), "tok")
    bottoms = [
        schulz_backward((-rates[which]).astype(jnp.bfloat16), forward[which][1])
        for which in range(3)
    ]
    cots = []
    for which in range(3):
        norm = roots[which] + fro_eps
        inner = jnp.sum(bottoms[which].astype(jnp.float32) * totals[which])
        cots.append(
            (
                bottoms[which].astype(jnp.float32) / norm
                - totals[which] * (inner / (norm * norm * roots[which]))
            ).astype(jnp.bfloat16)
        )
    grad_keys, grad_values, second_order = fast_second(keys, values, first, saved_keys, cots)
    grads = []
    for which in range(3):
        rate_rows = lax.dynamic_slice_in_dim(
            rates[which], starts[which], own_rows[which].shape[0], 0
        )
        summed = lax.psum_scatter(
            partial_first[which] + second_order[which], "tok", scatter_dimension=0, tiled=True
        )
        grads.append(((summed + rate_rows) * scale)[None])
    grad_queries = jnp.stack([grad_first, grad_second])
    return (grad_queries, grad_keys, grad_values, *grads)


def shift(array, ring, step):
    pairs = [
        (o * 2 + i, ((o + step) % ring) * 2 + i) for o in range(ring) for i in range(2)
    ]
    return lax.ppermute(array, "tok", pairs)


def swap(array, ring):
    return lax.ppermute(array, "tok", [(i, i ^ 1) for i in range(2 * ring)])


def tie(array, *earlier):
    return lax.optimization_barrier((array, *earlier))[0]


def along_ring(own, ring, earlier):
    found = [(0, own)]
    up, down = own, tie(own, earlier)
    for step in range(1, ring // 2 + 1):
        up = shift(up, ring, 1)
        found.append((-step, up))
        if 2 * step < ring:
            down = shift(down, ring, -1)
            found.append((step, down))
    return found


def head_terms(stats):
    heads = lax.axis_size("head")
    return [stats] + [
        lax.ppermute(stats, "head", [(i, (i + k) % heads) for i in range(heads)])
        for k in range(1, heads)
    ]


def unpack(layout, segments, ring, me, refs, targets, sems):
    copies = []
    for slot, ((outer, flip), ref) in enumerate(zip(layout, refs)):
        owner = ((me // 2 + outer + ring) % ring) * 2 + (me % 2 + flip) % 2
        begin = 0
        for (count, by_slot), target in zip(segments, targets):
            place = slot * count if by_slot else pl.multiple_of(owner * count, 16)
            copies.append(
                pltpu.make_async_copy(
                    ref.at[pl.ds(begin, count)],
                    target.at[pl.ds(place, count)],
                    sems.at[len(copies)],
                )
            )
            begin += count
    for copy in copies:
        copy.start()
    for copy in copies:
        copy.wait()


def chunks_of(tokens):
    step = min(ROWS, tokens)
    return [slice(i, i + step) for i in range(0, tokens, step)]


def pack_kernel(lead, *refs):
    sources, target, sems = refs[:-2], refs[-2], refs[-1]
    copies, begin = [], 0
    for place, source in enumerate(sources):
        source = source.at[lead[place]] if lead[place] is not None else source
        rows = source.shape[0]
        copies.append(
            pltpu.make_async_copy(source, target.at[pl.ds(begin, rows)], sems.at[place])
        )
        begin += rows
    for copy in copies:
        copy.start()
    for copy in copies:
        copy.wait()


def fast_kernel(layout, segments, ring, me_ref, *refs):
    count = len(layout)
    pieces, refs = refs[:count], refs[count:]
    (wg, wu, wd, keys, values, gk_ref, uk_ref, back_ref, totals_g, totals_u, totals_d) = refs[:11]
    d_gate, d_up, hidden, sems = refs[11:]
    unpack(layout, segments, ring, me_ref[0], pieces, (wg, wu, wd, keys, values), sems)
    for part in chunks_of(keys.shape[0]):
        gk = product(keys[part], wg[...])
        uk = product(keys[part], wu[...])
        back = -against(values[part], wd[...])
        sigma = jax.nn.sigmoid(gk)
        active = gk * sigma
        slope = sigma * (1.0 + gk * (1.0 - sigma))
        hidden[part] = (active * uk).astype(bf16)
        d_gate[part] = (back * uk * slope).astype(bf16)
        d_up[part] = (back * active).astype(bf16)
        gk_ref[part], uk_ref[part], back_ref[part] = gk, uk, back
    totals_g[...] = across(keys[...], d_gate[...])
    totals_u[...] = across(keys[...], d_up[...])
    totals_d[...] = -across(hidden[...], values[...])


def schulz_kernel(total_ref, weight, xs, grams, blends, following_ref, root_ref):
    total = total_ref[...]
    root = jnp.sqrt(jnp.sum(total * total, keepdims=True))
    root_ref[...] = jnp.broadcast_to(root, root_ref.shape)
    xs[0] = (total / (root + fro_eps)).astype(bf16)
    for sweep in range(NS_STEPS):
        current = xs[sweep]
        gram = against(current, current).astype(bf16)
        blend = (cube_coef * gram.astype(f32) + fifth_coef * product(gram, gram)).astype(bf16)
        following = (lin_coef * current.astype(f32) + product(blend, current)).astype(bf16)
        grams[sweep] = gram
        blends[sweep] = blend
        if sweep + 1 < NS_STEPS:
            xs[sweep + 1] = following
    following_ref[...] = (weight[...].astype(f32) - following.astype(f32)).astype(bf16)


def row_sums(columns, tokens):
    lanes = lax.broadcasted_iota(jnp.int32, (tokens, 128), 1)
    spread = jnp.where(lanes == 0, columns[0], jnp.where(lanes == 1, columns[1], 0.0))
    return spread.T[:8]


def forward_part(queries, upstream, gain, wg, wu, wd, gq_ref, uq_ref, hidden_ref, out_ref, stats):
    for part in chunks_of(queries.shape[0]):
        gq = product(queries[part], wg[...])
        uq = product(queries[part], wu[...])
        hidden = (gq * jax.nn.sigmoid(gq) * uq).astype(bf16)
        output = product(hidden, wd[...])
        weighted = gain[...] * upstream[part].astype(f32)
        sums = (
            jnp.sum(output * output, axis=1, keepdims=True),
            jnp.sum(weighted * output, axis=1, keepdims=True),
        )
        stats[:, part] = row_sums(sums, output.shape[0])
        gq_ref[part], uq_ref[part], hidden_ref[part], out_ref[part] = gq, uq, hidden, output


def backward_part(
    width, queries, upstream, gain, wg, wu, wd, gq_ref, uq_ref, hidden, out_ref, sums,
    grad_ref, d_gate, d_up, d_out, own,
):
    for part in chunks_of(queries.shape[0]):
        total = sum(term[:, part] for term in sums)
        tokens = total.shape[1]
        square = total[0:1] / width
        inverse = lax.rsqrt(square + rms_eps)
        pull = inverse * inverse * inverse * (total[1:2] / width)
        index = lax.broadcasted_iota(jnp.int32, (128, tokens), 0)
        columns = jnp.where(index == 0, inverse, jnp.where(index == 1, pull, 0.0)).T
        inverse, pull = columns[:, 0:1], columns[:, 1:2]
        weighted = gain[...] * upstream[part].astype(f32)
        d_output = (inverse * weighted - out_ref[part] * pull).astype(bf16)
        back = against(d_output, wd[...])
        gq, uq = gq_ref[part], uq_ref[part]
        sigma = jax.nn.sigmoid(gq)
        d_gate[part] = (back * uq * sigma * (1.0 + gq * (1.0 - sigma))).astype(bf16)
        d_up[part] = (back * gq * sigma).astype(bf16)
        d_out[part] = d_output
    grad_ref[...] = (
        against(d_gate[:own], wg[...]) + against(d_up[:own], wu[...])
    ).astype(bf16)


def first_forward_kernel(
    queries_ref, upstream_ref, gain, wg, wu, wd, queries, upstream, gq, uq, hidden, out, stats
):
    queries[...], upstream[...] = queries_ref[0], upstream_ref[0]
    forward_part(queries, upstream, gain, wg, wu, wd, gq, uq, hidden, out, stats)


def first_backward_kernel(
    width, ring, me_ref, queries, upstream, gain, wg, wu, wd, gq, uq, hidden, out, *refs
):
    count = len(refs) - 7
    sums = refs[:count]
    grad, kept, sent, d_gate, d_up, d_out, partial = refs[count:]
    backward_part(
        width, queries, upstream, gain, wg, wu, wd, gq, uq, hidden, out, sums,
        grad, d_gate, d_up, d_out, queries.shape[0],
    )
    inner = me_ref[0] % 2
    rows = kept.shape[2]
    for which, (left, right) in enumerate(((queries, d_gate), (queries, d_up), (hidden, d_out))):
        partial[...] = across(left[...], right[...]).astype(bf16)
        for outer in range(ring):
            mine = pl.multiple_of((outer * 2 + inner) * rows, 16)
            other = pl.multiple_of((outer * 2 + 1 - inner) * rows, 16)
            kept[outer, which] = partial[pl.ds(mine, rows)]
            sent[outer, which] = partial[pl.ds(other, rows)]


def pair_kernel(ring, me_ref, kept, received, own, *others):
    outer = me_ref[0] // 2
    own[...] = kept[outer].astype(f32) + received[outer].astype(f32)
    for step, target in enumerate(others, 1):
        place = (outer + step) % ring
        target[...] = (kept[place].astype(f32) + received[place].astype(f32)).astype(bf16)


def second_forward_kernel(layout, segments, ring, me_ref, gain, wg, wu, wd, *refs):
    count = len(layout)
    pieces, refs = refs[:count], refs[count:]
    queries, upstream, gq, uq, hidden, out, stats, sems = refs
    unpack(layout, segments, ring, me_ref[0], pieces, (queries, upstream), sems)
    forward_part(queries, upstream, gain, wg, wu, wd, gq, uq, hidden, out, stats)


def second_backward_kernel(
    width, own, grad_first, queries, upstream, gain, wg, wu, wd, gq, uq, hidden, out, *refs
):
    count = len(refs) - 7
    sums = refs[:count]
    grad, rate_g, rate_u, rate_d, d_gate, d_up, d_out = refs[count:]
    grad[0] = grad_first[...]
    backward_part(
        width, queries, upstream, gain, wg, wu, wd, gq, uq, hidden, out, sums,
        grad.at[1], d_gate, d_up, d_out, own,
    )
    rate_g[...] = across(queries[...], d_gate[...])
    rate_u[...] = across(queries[...], d_up[...])
    rate_d[...] = across(hidden[...], d_out[...])


def schulz_back_kernel(rate, total_ref, xs, grams, blends, root_ref, cot):
    current = (-rate[...]).astype(bf16)
    for sweep in reversed(range(NS_STEPS)):
        iterate, gram, blend = xs[sweep], grams[sweep], blends[sweep]
        symmetric = (against(current, iterate) + against(iterate, current)).astype(bf16)
        bent = product(symmetric, gram) + product(gram, symmetric)
        mixed = (cube_coef * symmetric.astype(f32) + fifth_coef * bent).astype(bf16)
        current = (
            lin_coef * current.astype(f32) + product(blend, current) + product(mixed, iterate)
        ).astype(bf16)
    root = root_ref[0:1, 0:1]
    norm = root + fro_eps
    total = total_ref[...]
    bottom = current.astype(f32)
    inner = jnp.sum(bottom * total, keepdims=True)
    cot[...] = (bottom / norm - total * (inner / (norm * norm * root))).astype(bf16)


def last_kernel(
    own, scale, me_ref, keys, values, wg, wu, wd, gk_ref, uk_ref, back_ref,
    cot_g, cot_u, cot_d, rate_g, rate_u, rate_d, *refs,
):
    count = len(refs) - 12
    firsts = refs[:count]
    grad_keys, grad_values, grad_g, grad_u, grad_d = refs[count:count + 5]
    lower, upper, d_back, pk, rk, hk, total = refs[count + 5:]
    for part in chunks_of(keys.shape[0]):
        gk, uk, back = gk_ref[part], uk_ref[part], back_ref[part]
        sigma = jax.nn.sigmoid(gk)
        active = gk * sigma
        slope = sigma * (1.0 + gk * (1.0 - sigma))
        curve = sigma * (1.0 - sigma) * (2.0 + gk * (1.0 - 2.0 * sigma))
        ek = product(keys[part], cot_g[...])
        fk = product(keys[part], cot_u[...])
        hk_part = -against(values[part], cot_d[...])
        d_back[part] = (ek * uk * slope + fk * active).astype(bf16)
        upper[part] = (ek * back * slope + hk_part * active).astype(bf16)
        lower[part] = (
            ek * back * uk * curve + fk * back * slope + hk_part * uk * slope
        ).astype(bf16)
        if part.start == 0:
            pk[...] = (back * uk * slope).astype(bf16)[:own]
            rk[...] = (back * active).astype(bf16)[:own]
            hk[...] = (active * uk).astype(bf16)[:own]
    grad_keys[...] = (
        against(pk[...], cot_g[...])
        + against(rk[...], cot_u[...])
        + against(lower[:own], wg[...])
        + against(upper[:own], wu[...])
    ).astype(bf16)
    grad_values[...] = (
        -product(hk[...], cot_d[...]) - product(d_back[:own], wd[...])
    ).astype(bf16)
    rows = grad_g.shape[1]
    start = pl.multiple_of(me_ref[0] * rows, 16)
    for which, (left, right, rate, grad) in enumerate((
        (keys, lower, rate_g, grad_g), (keys, upper, rate_u, grad_u), (d_back, values, rate_d, grad_d)
    )):
        total[...] = across(left[...], right[...])
        second = total[pl.ds(start, rows)]
        first = sum(ref[which].astype(f32) for ref in firsts)
        rate_rows = rate[pl.ds(start, rows)]
        both = first - second if which == 2 else first + second
        grad[0] = (both + rate_rows) * scale


def vmem():
    return pl.BlockSpec(memory_space=pltpu.VMEM)


def smem():
    return pl.BlockSpec(memory_space=pltpu.SMEM)


def anywhere():
    return pl.BlockSpec(memory_space=pl.ANY)


def cost(rows, depth, columns, products):
    flops = 2 * rows * depth * columns * products
    return pl.CostEstimate(flops=flops, bytes_accessed=flops // 512, transcendentals=0)


def params(mib):
    return pltpu.CompilerParams(vmem_limit_bytes=mib * 2**20)


def gather_tokens(queries, keys, values, upstream, out_gain, gate_weight, up_weight, down_weight):
    shards = lax.axis_size("tok")
    ring = shards // 2
    me = lax.axis_index("tok")
    me_ref = jnp.reshape(me, (1,)).astype(jnp.int32)
    own, depth = keys.shape
    rows = gate_weight.shape[1]
    hidden = gate_weight.shape[2]
    tokens = own * shards
    width = out_gain.shape[0] * lax.axis_size("head")
    scale = 1.0 / math.sqrt(tokens)
    gain = out_gain[None]
    S = jax.ShapeDtypeStruct

    matrix = (depth, hidden)
    wide, narrow = S(matrix, f32), S(matrix, bf16)

    def pack(arrays, lead):
        rows = sum(array.shape[-2] for array in arrays)
        return pl.pallas_call(
            functools.partial(pack_kernel, lead),
            out_shape=S((rows, depth), bf16),
            in_specs=[anywhere()] * len(arrays),
            out_specs=anywhere(),
            scratch_shapes=[pltpu.SemaphoreType.DMA((len(arrays),))],
            compiler_params=params(4),
        )(*arrays)

    packed = pack((gate_weight, up_weight, down_weight, keys, values), (0, 0, 0, None, None))
    packed_second = pack((queries, upstream), (1, 1))
    swapped = [swap(packed, ring)]
    outers = along_ring(packed, ring, swapped[0])
    swapped += [swap(array, ring) for _, array in outers[1:]]
    last = outers[-1][1]
    near = swapped[max(ring - 2, 0)]
    layout = [(outer, 0) for outer, _ in outers] + [(outer, 1) for outer, _ in outers]
    pieces = [array for _, array in outers] + swapped
    segments = ((rows, False), (rows, False), (down_weight.shape[1], False), (own, True), (own, True))
    (wg, wu, wd, all_keys, all_values, gk, uk, back, *totals) = pl.pallas_call(
        functools.partial(fast_kernel, layout, segments, ring),
        out_shape=(
            narrow, narrow, narrow, S((tokens, depth), bf16), S((tokens, depth), bf16),
            S((tokens, hidden), f32), S((tokens, hidden), f32), S((tokens, hidden), f32),
            wide, wide, wide,
        ),
        in_specs=[smem()] + [anywhere()] * len(pieces),
        out_specs=[vmem()] * 11,
        scratch_shapes=[pltpu.VMEM((tokens, hidden), bf16)] * 3
        + [pltpu.SemaphoreType.DMA((5 * len(pieces),))],
        cost_estimate=cost(tokens, depth, hidden, 6),
        compiler_params=params(24),
    )(me_ref, *pieces)

    queries0, upstream0, gq0, uq0, hidden0, out0, stats0 = pl.pallas_call(
        first_forward_kernel,
        out_shape=(
            S((own, depth), bf16), S((own, depth), bf16),
            S((own, hidden), f32), S((own, hidden), f32), S((own, hidden), bf16),
            S((own, depth), f32), S((8, own), f32),
        ),
        in_specs=[vmem()] * 6,
        out_specs=[vmem()] * 7,
        cost_estimate=cost(own, depth, hidden, 3),
        compiler_params=params(16),
    )(queries, upstream, gain, wg, wu, wd)

    def schulz(which, total):
        return pl.pallas_call(
            schulz_kernel,
            out_shape=(
                S((NS_STEPS, *matrix), bf16), S((NS_STEPS, *matrix), bf16),
                S((NS_STEPS, *matrix), bf16), narrow, S((8, 128), f32),
            ),
            in_specs=[vmem()] * 2,
            out_specs=[vmem()] * 5,
            cost_estimate=cost(depth, depth, hidden, 3 * NS_STEPS),
            compiler_params=params(16),
        )(total, (wg, wu, wd)[which])

    terms0 = head_terms(stats0)
    grad_first, kept, sent = pl.pallas_call(
        functools.partial(first_backward_kernel, width, ring),
        out_shape=(
            S((own, depth), bf16), S((ring, 3, rows, hidden), bf16), S((ring, 3, rows, hidden), bf16),
        ),
        in_specs=[smem()] + [vmem()] * (10 + len(terms0)),
        out_specs=[vmem()] * 3,
        scratch_shapes=[pltpu.VMEM((own, hidden), bf16)] * 2
        + [pltpu.VMEM((own, depth), bf16), pltpu.VMEM(matrix, bf16)],
        cost_estimate=cost(own, depth, hidden, 6),
        compiler_params=params(20),
    )(me_ref, queries0, upstream0, gain, wg, wu, wd, gq0, uq0, hidden0, out0, *terms0)

    forward = [
        schulz(0, totals[0]), schulz(1, tie(totals[1], *terms0)), schulz(2, tie(totals[2], sent))
    ]

    outers = along_ring(tie(packed_second, last), ring, last)
    after = (near, None, totals[0], forward[0][3])
    swapped = []
    for place, (_, array) in enumerate(outers):
        earlier = after[min(place, 3)]
        swapped.append(swap(array if earlier is None else tie(array, earlier), ring))
    near = swapped[max(ring - 2, 0)]
    pieces = [array for _, array in outers] + swapped
    segments = ((own, True), (own, True))
    seconds = [forward[which][3] for which in range(3)]
    all_queries, all_upstream, gq, uq, hidden_q, out, stats = pl.pallas_call(
        functools.partial(second_forward_kernel, layout, segments, ring),
        out_shape=(
            S((tokens, depth), bf16), S((tokens, depth), bf16),
            S((tokens, hidden), f32), S((tokens, hidden), f32), S((tokens, hidden), bf16),
            S((tokens, depth), f32), S((8, tokens), f32),
        ),
        in_specs=[smem()] + [vmem()] * 4 + [anywhere()] * len(pieces),
        out_specs=[vmem()] * 7,
        scratch_shapes=[pltpu.SemaphoreType.DMA((2 * len(pieces),))],
        cost_estimate=cost(tokens, depth, hidden, 3),
        compiler_params=params(24),
    )(me_ref, gain, *seconds, *pieces)
    terms = head_terms(stats)

    block = S((3, rows, hidden), bf16)
    summed = pl.pallas_call(
        functools.partial(pair_kernel, ring),
        out_shape=(S((3, rows, hidden), f32),) + (block,) * (ring - 1),
        in_specs=[smem()] + [vmem()] * 2,
        out_specs=[vmem()] * ring,
        compiler_params=params(12),
    )(me_ref, kept, swap(tie(sent, near), ring))
    firsts = [summed[0]] + [shift(summed[step], ring, step) for step in range(1, ring)]

    grad_queries, *rates = pl.pallas_call(
        functools.partial(second_backward_kernel, width, own),
        out_shape=(S((2, own, depth), bf16), wide, wide, wide),
        in_specs=[vmem()] * (11 + len(terms)),
        out_specs=[vmem()] * 4,
        scratch_shapes=[pltpu.VMEM((tokens, hidden), bf16)] * 2
        + [pltpu.VMEM((tokens, depth), bf16)],
        cost_estimate=cost(tokens, depth, hidden, 4),
        compiler_params=params(20),
    )(grad_first, all_queries, all_upstream, gain, *seconds, gq, uq, hidden_q, out, *terms)

    cots = [
        pl.pallas_call(
            schulz_back_kernel,
            out_shape=narrow,
            in_specs=[vmem()] * 6,
            out_specs=vmem(),
            cost_estimate=cost(depth, depth, hidden, 6 * NS_STEPS),
            compiler_params=params(16),
        )(rates[which], totals[which], *forward[which][:3], forward[which][4])
        for which in range(3)
    ]

    return (grad_queries, *pl.pallas_call(
        functools.partial(last_kernel, own, scale),
        out_shape=(
            S((own, depth), bf16), S((own, depth), bf16),
            S((1, rows, hidden), f32), S((1, rows, hidden), f32), S((1, rows, hidden), f32),
        ),
        in_specs=[smem()] + [vmem()] * (14 + len(firsts)),
        out_specs=[vmem()] * 5,
        scratch_shapes=[
            pltpu.VMEM((tokens, hidden), bf16),
            pltpu.VMEM((tokens, hidden), bf16),
            pltpu.VMEM((tokens, hidden), bf16),
            pltpu.VMEM((own, hidden), bf16),
            pltpu.VMEM((own, hidden), bf16),
            pltpu.VMEM((own, hidden), bf16),
            pltpu.VMEM(matrix, f32),
        ],
        cost_estimate=cost(tokens, depth, hidden, 7),
        compiler_params=params(24),
    )(
        me_ref, all_keys, all_values, wg, wu, wd, gk, uk, back, *cots, *rates, *firsts,
    ))


def per_device(queries, keys, values, upstream, out_gain, gate_weight, up_weight, down_weight):
    shards = lax.axis_size("tok")
    tokens = keys.shape[0] * shards
    few = 4 * tokens <= 12 * gate_weight.shape[2] and shards % 2 == 0
    plan = gather_tokens if few else split_tokens
    return plan(queries, keys, values, upstream, out_gain, gate_weight, up_weight, down_weight)


def solution(mesh):
    in_specs = (
        P(None, "tok", "head"),
        P("tok", "head"),
        P("tok", "head"),
        P(None, "tok", "head"),
        P("head"),
        P("head", "tok", None),
        P("head", "tok", None),
        P("head", "tok", None),
    )
    out_specs = (
        P(None, "tok", "head"),
        P("tok", "head"),
        P("tok", "head"),
        P("head", "tok", None),
        P("head", "tok", None),
        P("head", "tok", None),
    )
    return jax.shard_map(
        per_device, mesh=mesh, in_specs=in_specs, out_specs=out_specs, check_vma=False
    )
```

```python
import functools
import math

import jax
import jax.numpy as jnp
from jax import lax
from jax.experimental import pallas as pl
from jax.experimental.pallas import tpu as pltpu
from jax.sharding import PartitionSpec as P

NS_STEPS = 2


lin_coef = 3.4445
cube_coef = -4.775
fifth_coef = 2.0315
rms_eps = 1e-06
fro_eps = 1e-07

bf16 = jnp.bfloat16
f32 = jnp.float32
ROWS = 256


def product(left, right):
    return jnp.dot(left, right, preferred_element_type=jnp.float32)


def across(left, right):
    return lax.dot_general(
        left, right, (((0,), (0,)), ((), ())), preferred_element_type=jnp.float32
    )


def against(left, right):
    return lax.dot_general(
        left, right, (((1,), (1,)), ((), ())), preferred_element_type=jnp.float32
    )


def fast_forward(keys, values, weights):
    gate_weight, up_weight, down_weight = weights
    gate_pre = product(keys, gate_weight)
    up_pre = product(keys, up_weight)
    sigma = jax.nn.sigmoid(gate_pre)
    active = gate_pre * sigma
    hidden = (active * up_pre).astype(jnp.bfloat16)
    back = -against(values, down_weight)
    slope = sigma * (1.0 + gate_pre * (1.0 - sigma))
    d_gate = (back * up_pre * slope).astype(jnp.bfloat16)
    d_up = (back * active).astype(jnp.bfloat16)
    fast = (across(keys, d_gate), across(keys, d_up), -across(hidden, values))
    saved = (gate_pre, up_pre, sigma, active, hidden, back, slope, d_gate, d_up)
    return (fast, saved)


def fast_second(keys, values, weights, saved, cots):
    gate_weight, up_weight, down_weight = weights
    gate_pre, up_pre, sigma, active, hidden, back, slope, d_gate, d_up = saved
    cot_gate, cot_up, cot_down = cots
    along_gate = product(keys, cot_gate)
    along_up = product(keys, cot_up)
    along_hidden = -against(values, cot_down)
    curve = sigma * (1.0 - sigma) * (2.0 + gate_pre * (1.0 - 2.0 * sigma))
    d_back = (along_gate * up_pre * slope + along_up * active).astype(jnp.bfloat16)
    d_upper = (along_gate * back * slope + along_hidden * active).astype(jnp.bfloat16)
    d_lower = (
        along_gate * back * up_pre * curve + along_up * back * slope + along_hidden * up_pre * slope
    ).astype(jnp.bfloat16)
    grad_keys = (
        against(d_gate, cot_gate)
        + against(d_up, cot_up)
        + against(d_lower, gate_weight)
        + against(d_upper, up_weight)
    ).astype(jnp.bfloat16)
    grad_values = (-product(hidden, cot_down) - product(d_back, down_weight)).astype(jnp.bfloat16)
    partial_value = (across(keys, d_lower), across(keys, d_upper), -across(d_back, values))
    return (grad_keys, grad_values, partial_value)


def apply_forward(queries, weights):
    gate_weight, up_weight, down_weight = weights
    gate_pre = product(queries, gate_weight)
    up_pre = product(queries, up_weight)
    sigma = jax.nn.sigmoid(gate_pre)
    hidden = (gate_pre * sigma * up_pre).astype(jnp.bfloat16)
    output = product(hidden, down_weight)
    return (gate_pre, up_pre, sigma, hidden, output)


def statistics(output, upstream, out_gain, width):
    weighted = out_gain * upstream.astype(jnp.float32)
    sums = lax.psum((jnp.sum(output * output, axis=1), jnp.sum(weighted * output, axis=1)), "head")
    return (lax.rsqrt(sums[0] / width + rms_eps), sums[1] / width)


def apply_backward(queries, weights, saved, upstream, out_gain, width):
    gate_weight, up_weight, down_weight = weights
    gate_pre, up_pre, sigma, hidden, output = saved
    inverse_rms, mean_dot = statistics(output, upstream, out_gain, width)
    weighted = out_gain * upstream.astype(jnp.float32)
    d_output = (
        inverse_rms[:, None] * weighted
        - output * (inverse_rms * inverse_rms * inverse_rms * mean_dot)[:, None]
    ).astype(jnp.bfloat16)
    back = against(d_output, down_weight)
    slope = sigma * (1.0 + gate_pre * (1.0 - sigma))
    d_gate = (back * up_pre * slope).astype(jnp.bfloat16)
    d_up = (back * gate_pre * sigma).astype(jnp.bfloat16)
    grad_queries = (against(d_gate, gate_weight) + against(d_up, up_weight)).astype(jnp.bfloat16)
    partial_value = (across(queries, d_gate), across(queries, d_up), across(hidden, d_output))
    return (grad_queries, partial_value)


def schulz_forward(begin):
    current = begin
    saved = []
    for sweep in range(NS_STEPS):
        gram = against(current, current).astype(jnp.bfloat16)
        blend = (cube_coef * gram.astype(jnp.float32) + fifth_coef * product(gram, gram)).astype(
            jnp.bfloat16
        )
        following = (lin_coef * current.astype(jnp.float32) + product(blend, current)).astype(
            jnp.bfloat16
        )
        saved.append((current, gram, blend))
        current = following
    return (current, saved)


def schulz_backward(cotan, saved):
    current = cotan
    for iterate, gram, blend in reversed(saved):
        cross = against(current, iterate)
        symmetric = (cross + cross.T).astype(jnp.bfloat16)
        bent = product(symmetric, gram)
        mixed = (cube_coef * symmetric.astype(jnp.float32) + fifth_coef * (bent + bent.T)).astype(
            jnp.bfloat16
        )
        current = (
            lin_coef * current.astype(jnp.float32)
            + product(blend, current)
            + product(mixed, iterate)
        ).astype(jnp.bfloat16)
    return current


def split_tokens(queries, keys, values, upstream, out_gain, gate_weight, up_weight, down_weight):
    shards = lax.axis_size("tok")
    owner = lax.axis_index("tok")
    width = out_gain.shape[0] * lax.axis_size("head")
    scale = 1.0 / math.sqrt(queries.shape[1] * shards)
    own_rows = (gate_weight[0], up_weight[0], down_weight[0])
    starts = [owner * own_rows[which].shape[0] for which in range(3)]
    first = tuple(lax.all_gather(rows, "tok", axis=0, tiled=True) for rows in own_rows)
    fast, saved_keys = fast_forward(keys, values, first)
    apply_first = apply_forward(queries[0], first)
    grad_first, partial_first = apply_backward(
        queries[0], first, apply_first, upstream[0], out_gain, width
    )
    totals = lax.psum((fast[0], fast[1], fast[2]), "tok")
    roots = [jnp.sqrt(jnp.sum(totals[which] * totals[which])) for which in range(3)]
    forward = [
        schulz_forward((totals[which] / (roots[which] + fro_eps)).astype(jnp.bfloat16))
        for which in range(3)
    ]
    second = tuple(
        (first[which].astype(jnp.float32) - forward[which][0].astype(jnp.float32)).astype(
            jnp.bfloat16
        )
        for which in range(3)
    )
    apply_second = apply_forward(queries[1], second)
    grad_second, partial_second = apply_backward(
        queries[1], second, apply_second, upstream[1], out_gain, width
    )
    rates = lax.psum((partial_second[0], partial_second[1], partial_second[2]), "tok")
    bottoms = [
        schulz_backward((-rates[which]).astype(jnp.bfloat16), forward[which][1])
        for which in range(3)
    ]
    cots = []
    for which in range(3):
        norm = roots[which] + fro_eps
        inner = jnp.sum(bottoms[which].astype(jnp.float32) * totals[which])
        cots.append(
            (
                bottoms[which].astype(jnp.float32) / norm
                - totals[which] * (inner / (norm * norm * roots[which]))
            ).astype(jnp.bfloat16)
        )
    grad_keys, grad_values, second_order = fast_second(keys, values, first, saved_keys, cots)
    grads = []
    for which in range(3):
        rate_rows = lax.dynamic_slice_in_dim(
            rates[which], starts[which], own_rows[which].shape[0], 0
        )
        summed = lax.psum_scatter(
            partial_first[which] + second_order[which], "tok", scatter_dimension=0, tiled=True
        )
        grads.append(((summed + rate_rows) * scale)[None])
    grad_queries = jnp.stack([grad_first, grad_second])
    return (grad_queries, grad_keys, grad_values, *grads)


def shift(array, ring, step):
    pairs = [
        (o * 2 + i, ((o + step) % ring) * 2 + i) for o in range(ring) for i in range(2)
    ]
    return lax.ppermute(array, "tok", pairs)


def swap(array, ring):
    return lax.ppermute(array, "tok", [(i, i ^ 1) for i in range(2 * ring)])


def tie(array, *earlier):
    return lax.optimization_barrier((array, *earlier))[0]


def head_terms(stats):
    heads = lax.axis_size("head")
    return [stats] + [
        lax.ppermute(stats, "head", [(i, (i + k) % heads) for i in range(heads)])
        for k in range(1, heads)
    ]


def owner_of(ring, me, outer, flip):
    return ((me // 2 + outer + ring) % ring) * 2 + (me % 2 + flip) % 2


def move(rows, sems):
    copies = [
        pltpu.make_async_copy(
            source.at[pl.ds(begin, count)], target.at[pl.ds(place, count)], sems.at[index]
        )
        for index, (source, begin, target, place, count) in enumerate(rows)
    ]
    for copy in copies:
        copy.start()
    for copy in copies:
        copy.wait()


def chunks_of(tokens):
    step = min(ROWS, tokens)
    return [slice(i, i + step) for i in range(0, tokens, step)]


def pack_kernel(gate, up, down, keys, values, queries, upstream, first, second, sems):
    rows = []
    for target, sources in (
        (first, (gate.at[0], up.at[0], down.at[0], keys, values)),
        (second, (queries.at[1], upstream.at[1])),
    ):
        begin = 0
        for source in sources:
            rows.append((source, 0, target, begin, source.shape[0]))
            begin += source.shape[0]
    move(rows, sems)


def place_rows(layout, ring, me, pieces, targets):
    rows = []
    for (outer, flip, slot), piece in zip(layout, pieces):
        owner = owner_of(ring, me, outer, flip)
        begin = 0
        for index, target in enumerate(targets):
            count = target.shape[0] // (2 * ring)
            place = pl.multiple_of(owner * count, 16) if index < 3 else slot * count
            rows.append((piece, begin, target, place, count))
            begin += count
    return rows


def place_kernel(layout, ring, carried, me_ref, *refs):
    sems = refs[-1]
    refs = refs[:-1]
    targets = refs[-6:-1] if carried else refs[-5:]
    rows = place_rows(layout, ring, me_ref[0], refs, targets)
    begin = 0
    for source in refs[len(layout):len(layout) + carried]:
        rows.append((source, 0, refs[-1], begin, source.shape[0]))
        begin += source.shape[0]
    move(rows, sems)


def fast_kernel(layout, ring, me_ref, *refs):
    pieces, refs = refs[:len(layout)], refs[len(layout) + 5:]
    (wg, wu, wd, keys, values, gk_ref, uk_ref, back_ref, totals_g, totals_u, totals_d) = refs[:11]
    d_gate, d_up, hidden, sems = refs[11:]
    move(place_rows(layout, ring, me_ref[0], pieces, (wg, wu, wd, keys, values)), sems)
    for part in chunks_of(keys.shape[0]):
        gk = product(keys[part], wg[...])
        uk = product(keys[part], wu[...])
        back = -against(values[part], wd[...])
        sigma = jax.nn.sigmoid(gk)
        active = gk * sigma
        slope = sigma * (1.0 + gk * (1.0 - sigma))
        hidden[part] = (active * uk).astype(bf16)
        d_gate[part] = (back * uk * slope).astype(bf16)
        d_up[part] = (back * active).astype(bf16)
        gk_ref[part], uk_ref[part], back_ref[part] = gk, uk, back
    totals_g[...] = across(keys[...], d_gate[...])
    totals_u[...] = across(keys[...], d_up[...])
    totals_d[...] = -across(hidden[...], values[...])


def schulz_kernel(total_ref, weight, xs, grams, blends, following_ref, root_ref):
    total = total_ref[...]
    root = jnp.sqrt(jnp.sum(total * total, keepdims=True))
    root_ref[...] = jnp.broadcast_to(root, root_ref.shape)
    xs[0] = (total / (root + fro_eps)).astype(bf16)
    for sweep in range(NS_STEPS):
        current = xs[sweep]
        gram = against(current, current).astype(bf16)
        blend = (cube_coef * gram.astype(f32) + fifth_coef * product(gram, gram)).astype(bf16)
        following = (lin_coef * current.astype(f32) + product(blend, current)).astype(bf16)
        grams[sweep] = gram
        blends[sweep] = blend
        if sweep + 1 < NS_STEPS:
            xs[sweep + 1] = following
    following_ref[...] = (weight[...].astype(f32) - following.astype(f32)).astype(bf16)


def row_sums(columns, tokens):
    lanes = lax.broadcasted_iota(jnp.int32, (tokens, 128), 1)
    spread = jnp.where(lanes == 0, columns[0], jnp.where(lanes == 1, columns[1], 0.0))
    return spread.T[:8]


def forward_part(queries, upstream, gain, wg, wu, wd, gq_ref, uq_ref, hidden_ref, out_ref, stats):
    for part in chunks_of(queries.shape[0]):
        gq = product(queries[part], wg[...])
        uq = product(queries[part], wu[...])
        hidden = (gq * jax.nn.sigmoid(gq) * uq).astype(bf16)
        output = product(hidden, wd[...])
        weighted = gain[...] * upstream[part].astype(f32)
        sums = (
            jnp.sum(output * output, axis=1, keepdims=True),
            jnp.sum(weighted * output, axis=1, keepdims=True),
        )
        stats[:, part] = row_sums(sums, output.shape[0])
        gq_ref[part], uq_ref[part], hidden_ref[part], out_ref[part] = gq, uq, hidden, output


def backward_part(
    width, queries, upstream, gain, wg, wu, wd, gq_ref, uq_ref, hidden, out_ref, sums,
    grad_ref, d_gate, d_up, d_out, own,
):
    for part in chunks_of(queries.shape[0]):
        total = sum(term[:, part] for term in sums)
        tokens = total.shape[1]
        square = total[0:1] / width
        inverse = lax.rsqrt(square + rms_eps)
        pull = inverse * inverse * inverse * (total[1:2] / width)
        index = lax.broadcasted_iota(jnp.int32, (128, tokens), 0)
        columns = jnp.where(index == 0, inverse, jnp.where(index == 1, pull, 0.0)).T
        inverse, pull = columns[:, 0:1], columns[:, 1:2]
        weighted = gain[...] * upstream[part].astype(f32)
        d_output = (inverse * weighted - out_ref[part] * pull).astype(bf16)
        back = against(d_output, wd[...])
        gq, uq = gq_ref[part], uq_ref[part]
        sigma = jax.nn.sigmoid(gq)
        d_gate[part] = (back * uq * sigma * (1.0 + gq * (1.0 - sigma))).astype(bf16)
        d_up[part] = (back * gq * sigma).astype(bf16)
        d_out[part] = d_output
    grad_ref[...] = (
        against(d_gate[:own], wg[...]) + against(d_up[:own], wu[...])
    ).astype(bf16)


def first_forward_kernel(
    queries_ref, upstream_ref, gain, wg, wu, wd, queries, upstream, gq, uq, hidden, out, stats
):
    queries[...], upstream[...] = queries_ref[0], upstream_ref[0]
    forward_part(queries, upstream, gain, wg, wu, wd, gq, uq, hidden, out, stats)


def first_backward_kernel(
    width, ring, me_ref, queries, upstream, gain, wg, wu, wd, gq, uq, hidden, out, *refs
):
    count = len(refs) - 7
    sums = refs[:count]
    grad, kept, sent, d_gate, d_up, d_out, partial = refs[count:]
    backward_part(
        width, queries, upstream, gain, wg, wu, wd, gq, uq, hidden, out, sums,
        grad, d_gate, d_up, d_out, queries.shape[0],
    )
    inner = me_ref[0] % 2
    rows = kept.shape[2]
    for which, (left, right) in enumerate(((queries, d_gate), (queries, d_up), (hidden, d_out))):
        partial[...] = across(left[...], right[...]).astype(bf16)
        for outer in range(ring):
            mine = pl.multiple_of((outer * 2 + inner) * rows, 16)
            other = pl.multiple_of((outer * 2 + 1 - inner) * rows, 16)
            kept[outer, which] = partial[pl.ds(mine, rows)]
            sent[outer, which] = partial[pl.ds(other, rows)]


def pair_kernel(ring, me_ref, kept, received, own, *others):
    outer = me_ref[0] // 2
    own[...] = kept[outer].astype(f32) + received[outer].astype(f32)
    for step, target in enumerate(others, 1):
        place = (outer + step) % ring
        target[...] = (kept[place].astype(f32) + received[place].astype(f32)).astype(bf16)


def second_forward_kernel(gain, wg, wu, wd, *refs):
    count = len(refs) - 8
    pieces, refs = refs[:count], refs[count:]
    queries, upstream, gq, uq, hidden, out, stats, sems = refs
    tokens = queries.shape[0] // (2 * count)
    rows = []
    for slot, piece in enumerate(pieces):
        for half in range(2):
            place = (2 * slot + half) * tokens
            rows.append((piece, 2 * half * tokens, queries, place, tokens))
            rows.append((piece, (2 * half + 1) * tokens, upstream, place, tokens))
    move(rows, sems)
    forward_part(queries, upstream, gain, wg, wu, wd, gq, uq, hidden, out, stats)


def second_backward_kernel(
    width, own, grad_first, queries, upstream, gain, wg, wu, wd, gq, uq, hidden, out, *refs
):
    count = len(refs) - 7
    sums = refs[:count]
    grad, rate_g, rate_u, rate_d, d_gate, d_up, d_out = refs[count:]
    grad[0] = grad_first[...]
    backward_part(
        width, queries, upstream, gain, wg, wu, wd, gq, uq, hidden, out, sums,
        grad.at[1], d_gate, d_up, d_out, own,
    )
    rate_g[...] = across(queries[...], d_gate[...])
    rate_u[...] = across(queries[...], d_up[...])
    rate_d[...] = across(hidden[...], d_out[...])


def schulz_back_kernel(rate, total_ref, xs, grams, blends, root_ref, cot):
    current = (-rate[...]).astype(bf16)
    for sweep in reversed(range(NS_STEPS)):
        iterate, gram, blend = xs[sweep], grams[sweep], blends[sweep]
        symmetric = (against(current, iterate) + against(iterate, current)).astype(bf16)
        bent = product(symmetric, gram) + product(gram, symmetric)
        mixed = (cube_coef * symmetric.astype(f32) + fifth_coef * bent).astype(bf16)
        current = (
            lin_coef * current.astype(f32) + product(blend, current) + product(mixed, iterate)
        ).astype(bf16)
    root = root_ref[0:1, 0:1]
    norm = root + fro_eps
    total = total_ref[...]
    bottom = current.astype(f32)
    inner = jnp.sum(bottom * total, keepdims=True)
    cot[...] = (bottom / norm - total * (inner / (norm * norm * root))).astype(bf16)


def last_kernel(
    own, scale, me_ref, keys, values, wg, wu, wd, gk_ref, uk_ref, back_ref,
    cot_g, cot_u, cot_d, rate_g, rate_u, rate_d, *refs,
):
    count = len(refs) - 12
    firsts = refs[:count]
    grad_keys, grad_values, grad_g, grad_u, grad_d = refs[count:count + 5]
    lower, upper, d_back, pk, rk, hk, total = refs[count + 5:]
    for part in chunks_of(keys.shape[0]):
        gk, uk, back = gk_ref[part], uk_ref[part], back_ref[part]
        sigma = jax.nn.sigmoid(gk)
        active = gk * sigma
        slope = sigma * (1.0 + gk * (1.0 - sigma))
        curve = sigma * (1.0 - sigma) * (2.0 + gk * (1.0 - 2.0 * sigma))
        ek = product(keys[part], cot_g[...])
        fk = product(keys[part], cot_u[...])
        hk_part = -against(values[part], cot_d[...])
        d_back[part] = (ek * uk * slope + fk * active).astype(bf16)
        upper[part] = (ek * back * slope + hk_part * active).astype(bf16)
        lower[part] = (
            ek * back * uk * curve + fk * back * slope + hk_part * uk * slope
        ).astype(bf16)
        if part.start == 0:
            pk[...] = (back * uk * slope).astype(bf16)[:own]
            rk[...] = (back * active).astype(bf16)[:own]
            hk[...] = (active * uk).astype(bf16)[:own]
    grad_keys[...] = (
        against(pk[...], cot_g[...])
        + against(rk[...], cot_u[...])
        + against(lower[:own], wg[...])
        + against(upper[:own], wu[...])
    ).astype(bf16)
    grad_values[...] = (
        -product(hk[...], cot_d[...]) - product(d_back[:own], wd[...])
    ).astype(bf16)
    rows = grad_g.shape[1]
    start = pl.multiple_of(me_ref[0] * rows, 16)
    for which, (left, right, rate, grad) in enumerate((
        (keys, lower, rate_g, grad_g), (keys, upper, rate_u, grad_u), (d_back, values, rate_d, grad_d)
    )):
        total[...] = across(left[...], right[...])
        second = total[pl.ds(start, rows)]
        first = sum(ref[which].astype(f32) for ref in firsts)
        rate_rows = rate[pl.ds(start, rows)]
        both = first - second if which == 2 else first + second
        grad[0] = (both + rate_rows) * scale


def vmem():
    return pl.BlockSpec(memory_space=pltpu.VMEM)


def smem():
    return pl.BlockSpec(memory_space=pltpu.SMEM)


def hbm():
    return pl.BlockSpec(memory_space=pltpu.HBM)


def anywhere():
    return pl.BlockSpec(memory_space=pl.ANY)


def light():
    return pl.CostEstimate(flops=1, bytes_accessed=1, transcendentals=0)


def params(mib):
    return pltpu.CompilerParams(vmem_limit_bytes=mib * 2**20)


def gather_tokens(queries, keys, values, upstream, out_gain, gate_weight, up_weight, down_weight):
    shards = lax.axis_size("tok")
    ring = shards // 2
    me = lax.axis_index("tok")
    me_ref = jnp.reshape(me, (1,)).astype(jnp.int32)
    own, depth = keys.shape
    rows = gate_weight.shape[1]
    hidden = gate_weight.shape[2]
    tokens = own * shards
    width = out_gain.shape[0] * lax.axis_size("head")
    scale = 1.0 / math.sqrt(tokens)
    gain = out_gain[None]
    S = jax.ShapeDtypeStruct

    matrix = (depth, hidden)
    wide, narrow = S(matrix, f32), S(matrix, bf16)

    packed, packed_second = pl.pallas_call(
        pack_kernel,
        out_shape=(
            S((2 * rows + down_weight.shape[1] + 2 * own, depth), bf16), S((2 * own, depth), bf16),
        ),
        in_specs=[hbm()] * 7,
        out_specs=[vmem()] * 2,
        scratch_shapes=[pltpu.SemaphoreType.DMA((7,))],
        compiler_params=params(60),
    )(gate_weight, up_weight, down_weight, keys, values, queries, upstream)
    buffers = (narrow, narrow, narrow, S((tokens, depth), bf16), S((tokens, depth), bf16))

    def place(pieces, layout, state=(), carry=(), others=()):
        out_shape = buffers
        if carry:
            out_shape += (S((sum(array.shape[0] for array in carry), depth), bf16),)
        start = 1 + len(pieces) + len(carry) + len(others)
        out = pl.pallas_call(
            functools.partial(place_kernel, layout, ring, len(carry)),
            out_shape=out_shape,
            in_specs=[smem()] + [anywhere()] * (start - 1 + len(state)),
            out_specs=[anywhere()] * len(out_shape),
            scratch_shapes=[pltpu.SemaphoreType.DMA((5 * len(pieces) + len(carry),))],
            input_output_aliases={start + index: index for index in range(len(state))},
            cost_estimate=light(),
            compiler_params=params(4),
        )(me_ref, *pieces, *carry, *others, *state)
        return (out[:5], out[5]) if carry else (out, None)

    crossed = swap(packed, ring)
    crossed_second = swap(packed_second, ring)
    up = shift(packed, ring, 1)
    state, carried = place((packed, crossed), ((0, 0, 0), (0, 1, 1)), carry=(packed,))
    down = shift(carried, ring, -1)
    crossed_up = swap(up, ring)
    crossed_down = swap(down, ring)
    state, carried = place((up,), ((-1, 0, 2),), state, (up,), (crossed_second,))
    far = shift(carried, ring, 1)
    crossed_far = swap(far, ring)
    state, pair = place(
        (down, crossed_up), ((1, 0, 3), (-1, 1, 4)), state, (packed_second, crossed_second)
    )
    state, _ = place((far, crossed_down), ((-2, 0, 5), (1, 1, 6)), state)
    layout = ((-2, 1, 7),)
    (wg, wu, wd, all_keys, all_values, gk, uk, back, *totals) = pl.pallas_call(
        functools.partial(fast_kernel, layout, ring),
        out_shape=(
            narrow, narrow, narrow, S((tokens, depth), bf16), S((tokens, depth), bf16),
            S((tokens, hidden), f32), S((tokens, hidden), f32), S((tokens, hidden), f32),
            wide, wide, wide,
        ),
        in_specs=[smem(), anywhere()] + [anywhere()] * 5,
        out_specs=[vmem()] * 11,
        scratch_shapes=[pltpu.VMEM((tokens, hidden), bf16)] * 3 + [pltpu.SemaphoreType.DMA((5,))],
        input_output_aliases={2 + index: index for index in range(5)},
        cost_estimate=light(),
        compiler_params=params(24),
    )(me_ref, crossed_far, *state)

    up, down = shift(pair, ring, 1), shift(pair, ring, -1)
    pairs = [pair, up, down, shift(tie(up, totals[0]), ring, 1)]

    queries0, upstream0, gq0, uq0, hidden0, out0, stats0 = pl.pallas_call(
        first_forward_kernel,
        out_shape=(
            S((own, depth), bf16), S((own, depth), bf16),
            S((own, hidden), f32), S((own, hidden), f32), S((own, hidden), bf16),
            S((own, depth), f32), S((8, own), f32),
        ),
        in_specs=[vmem()] * 6,
        out_specs=[vmem()] * 7,
        cost_estimate=light(),
        compiler_params=params(16),
    )(queries, upstream, gain, wg, wu, wd)

    def schulz(which, total):
        return pl.pallas_call(
            schulz_kernel,
            out_shape=(
                S((NS_STEPS, *matrix), bf16), S((NS_STEPS, *matrix), bf16),
                S((NS_STEPS, *matrix), bf16), narrow, S((8, 128), f32),
            ),
            in_specs=[vmem()] * 2,
            out_specs=[vmem()] * 5,
            cost_estimate=light(),
            compiler_params=params(16),
        )(total, (wg, wu, wd)[which])

    terms0 = head_terms(stats0)
    first_weight = schulz(0, totals[0])
    terms0[0] = tie(terms0[0], first_weight[4])
    grad_first, kept, sent = pl.pallas_call(
        functools.partial(first_backward_kernel, width, ring),
        out_shape=(
            S((own, depth), bf16), S((ring, 3, rows, hidden), bf16), S((ring, 3, rows, hidden), bf16),
        ),
        in_specs=[smem()] + [vmem()] * (10 + len(terms0)),
        out_specs=[vmem()] * 3,
        scratch_shapes=[pltpu.VMEM((own, hidden), bf16)] * 2
        + [pltpu.VMEM((own, depth), bf16), pltpu.VMEM(matrix, bf16)],
        cost_estimate=light(),
        compiler_params=params(20),
    )(me_ref, queries0, upstream0, gain, wg, wu, wd, gq0, uq0, hidden0, out0, *terms0)

    forward = [first_weight, schulz(1, totals[1]), schulz(2, tie(totals[2], down))]

    seconds = [forward[which][3] for which in range(3)]
    all_queries, all_upstream, gq, uq, hidden_q, out, stats = pl.pallas_call(
        second_forward_kernel,
        out_shape=(
            S((tokens, depth), bf16), S((tokens, depth), bf16),
            S((tokens, hidden), f32), S((tokens, hidden), f32), S((tokens, hidden), bf16),
            S((tokens, depth), f32), S((8, tokens), f32),
        ),
        in_specs=[vmem()] * 4 + [anywhere()] * len(pairs),
        out_specs=[vmem()] * 7,
        scratch_shapes=[pltpu.SemaphoreType.DMA((4 * len(pairs),))],
        cost_estimate=light(),
        compiler_params=params(24),
    )(gain, *seconds, *pairs)
    terms = head_terms(stats)

    block = S((3, rows, hidden), bf16)
    summed = pl.pallas_call(
        functools.partial(pair_kernel, ring),
        out_shape=(S((3, rows, hidden), f32),) + (block,) * (ring - 1),
        in_specs=[smem()] + [vmem()] * 2,
        out_specs=[vmem()] * ring,
        compiler_params=params(12),
    )(me_ref, tie(kept, terms[1]), swap(tie(sent, down), ring))
    firsts = [summed[0]] + [shift(summed[step], ring, step) for step in range(1, ring)]

    grad_queries, *rates = pl.pallas_call(
        functools.partial(second_backward_kernel, width, own),
        out_shape=(S((2, own, depth), bf16), wide, wide, wide),
        in_specs=[vmem()] * (11 + len(terms)),
        out_specs=[vmem()] * 4,
        scratch_shapes=[pltpu.VMEM((tokens, hidden), bf16)] * 2
        + [pltpu.VMEM((tokens, depth), bf16)],
        cost_estimate=light(),
        compiler_params=params(20),
    )(grad_first, all_queries, all_upstream, gain, *seconds, gq, uq, hidden_q, out, *terms)

    cots = [
        pl.pallas_call(
            schulz_back_kernel,
            out_shape=narrow,
            in_specs=[vmem()] * 6,
            out_specs=vmem(),
            cost_estimate=light(),
            compiler_params=params(16),
        )(rates[which], totals[which], *forward[which][:3], forward[which][4])
        for which in range(3)
    ]

    return (grad_queries, *pl.pallas_call(
        functools.partial(last_kernel, own, scale),
        out_shape=(
            S((own, depth), bf16), S((own, depth), bf16),
            S((1, rows, hidden), f32), S((1, rows, hidden), f32), S((1, rows, hidden), f32),
        ),
        in_specs=[smem()] + [vmem()] * (14 + len(firsts)),
        out_specs=[vmem()] * 5,
        scratch_shapes=[
            pltpu.VMEM((tokens, hidden), bf16),
            pltpu.VMEM((tokens, hidden), bf16),
            pltpu.VMEM((tokens, hidden), bf16),
            pltpu.VMEM((own, hidden), bf16),
            pltpu.VMEM((own, hidden), bf16),
            pltpu.VMEM((own, hidden), bf16),
            pltpu.VMEM(matrix, f32),
        ],
        cost_estimate=light(),
        compiler_params=params(24),
    )(
        me_ref, all_keys, all_values, wg, wu, wd, gk, uk, back, *cots, *rates, *firsts,
    ))


def per_device(queries, keys, values, upstream, out_gain, gate_weight, up_weight, down_weight):
    shards = lax.axis_size("tok")
    tokens = keys.shape[0] * shards
    few = 4 * tokens <= 12 * gate_weight.shape[2] and shards == 8
    plan = gather_tokens if few else split_tokens
    return plan(queries, keys, values, upstream, out_gain, gate_weight, up_weight, down_weight)


def solution(mesh):
    in_specs = (
        P(None, "tok", "head"),
        P("tok", "head"),
        P("tok", "head"),
        P(None, "tok", "head"),
        P("head"),
        P("head", "tok", None),
        P("head", "tok", None),
        P("head", "tok", None),
    )
    out_specs = (
        P(None, "tok", "head"),
        P("tok", "head"),
        P("tok", "head"),
        P("head", "tok", None),
        P("head", "tok", None),
        P("head", "tok", None),
    )
    return jax.shard_map(
        per_device, mesh=mesh, in_specs=in_specs, out_specs=out_specs, check_vma=False
    )
```

```python
import functools
import math

import jax
import jax.numpy as jnp
from jax import lax
from jax.experimental import pallas as pl
from jax.experimental.pallas import tpu as pltpu
from jax.sharding import PartitionSpec as P

NS_STEPS = 2


lin_coef = 3.4445
cube_coef = -4.775
fifth_coef = 2.0315
rms_eps = 1e-06
fro_eps = 1e-07

bf16 = jnp.bfloat16
f32 = jnp.float32
ROWS = 256


def product(left, right):
    return jnp.dot(left, right, preferred_element_type=jnp.float32)


def across(left, right):
    return lax.dot_general(
        left, right, (((0,), (0,)), ((), ())), preferred_element_type=jnp.float32
    )


def against(left, right):
    return lax.dot_general(
        left, right, (((1,), (1,)), ((), ())), preferred_element_type=jnp.float32
    )


def fast_forward(keys, values, weights):
    gate_weight, up_weight, down_weight = weights
    gate_pre = product(keys, gate_weight)
    up_pre = product(keys, up_weight)
    sigma = jax.nn.sigmoid(gate_pre)
    active = gate_pre * sigma
    hidden = (active * up_pre).astype(jnp.bfloat16)
    back = -against(values, down_weight)
    slope = sigma * (1.0 + gate_pre * (1.0 - sigma))
    d_gate = (back * up_pre * slope).astype(jnp.bfloat16)
    d_up = (back * active).astype(jnp.bfloat16)
    fast = (across(keys, d_gate), across(keys, d_up), -across(hidden, values))
    saved = (gate_pre, up_pre, sigma, active, hidden, back, slope, d_gate, d_up)
    return (fast, saved)


def fast_second(keys, values, weights, saved, cots):
    gate_weight, up_weight, down_weight = weights
    gate_pre, up_pre, sigma, active, hidden, back, slope, d_gate, d_up = saved
    cot_gate, cot_up, cot_down = cots
    along_gate = product(keys, cot_gate)
    along_up = product(keys, cot_up)
    along_hidden = -against(values, cot_down)
    curve = sigma * (1.0 - sigma) * (2.0 + gate_pre * (1.0 - 2.0 * sigma))
    d_back = (along_gate * up_pre * slope + along_up * active).astype(jnp.bfloat16)
    d_upper = (along_gate * back * slope + along_hidden * active).astype(jnp.bfloat16)
    d_lower = (
        along_gate * back * up_pre * curve + along_up * back * slope + along_hidden * up_pre * slope
    ).astype(jnp.bfloat16)
    grad_keys = (
        against(d_gate, cot_gate)
        + against(d_up, cot_up)
        + against(d_lower, gate_weight)
        + against(d_upper, up_weight)
    ).astype(jnp.bfloat16)
    grad_values = (-product(hidden, cot_down) - product(d_back, down_weight)).astype(jnp.bfloat16)
    partial_value = (across(keys, d_lower), across(keys, d_upper), -across(d_back, values))
    return (grad_keys, grad_values, partial_value)


def apply_forward(queries, weights):
    gate_weight, up_weight, down_weight = weights
    gate_pre = product(queries, gate_weight)
    up_pre = product(queries, up_weight)
    sigma = jax.nn.sigmoid(gate_pre)
    hidden = (gate_pre * sigma * up_pre).astype(jnp.bfloat16)
    output = product(hidden, down_weight)
    return (gate_pre, up_pre, sigma, hidden, output)


def statistics(output, upstream, out_gain, width):
    weighted = out_gain * upstream.astype(jnp.float32)
    sums = lax.psum((jnp.sum(output * output, axis=1), jnp.sum(weighted * output, axis=1)), "head")
    return (lax.rsqrt(sums[0] / width + rms_eps), sums[1] / width)


def apply_backward(queries, weights, saved, upstream, out_gain, width):
    gate_weight, up_weight, down_weight = weights
    gate_pre, up_pre, sigma, hidden, output = saved
    inverse_rms, mean_dot = statistics(output, upstream, out_gain, width)
    weighted = out_gain * upstream.astype(jnp.float32)
    d_output = (
        inverse_rms[:, None] * weighted
        - output * (inverse_rms * inverse_rms * inverse_rms * mean_dot)[:, None]
    ).astype(jnp.bfloat16)
    back = against(d_output, down_weight)
    slope = sigma * (1.0 + gate_pre * (1.0 - sigma))
    d_gate = (back * up_pre * slope).astype(jnp.bfloat16)
    d_up = (back * gate_pre * sigma).astype(jnp.bfloat16)
    grad_queries = (against(d_gate, gate_weight) + against(d_up, up_weight)).astype(jnp.bfloat16)
    partial_value = (across(queries, d_gate), across(queries, d_up), across(hidden, d_output))
    return (grad_queries, partial_value)


def schulz_forward(begin):
    current = begin
    saved = []
    for sweep in range(NS_STEPS):
        gram = against(current, current).astype(jnp.bfloat16)
        blend = (cube_coef * gram.astype(jnp.float32) + fifth_coef * product(gram, gram)).astype(
            jnp.bfloat16
        )
        following = (lin_coef * current.astype(jnp.float32) + product(blend, current)).astype(
            jnp.bfloat16
        )
        saved.append((current, gram, blend))
        current = following
    return (current, saved)


def schulz_backward(cotan, saved):
    current = cotan
    for iterate, gram, blend in reversed(saved):
        cross = against(current, iterate)
        symmetric = (cross + cross.T).astype(jnp.bfloat16)
        bent = product(symmetric, gram)
        mixed = (cube_coef * symmetric.astype(jnp.float32) + fifth_coef * (bent + bent.T)).astype(
            jnp.bfloat16
        )
        current = (
            lin_coef * current.astype(jnp.float32)
            + product(blend, current)
            + product(mixed, iterate)
        ).astype(jnp.bfloat16)
    return current


def split_tokens(queries, keys, values, upstream, out_gain, gate_weight, up_weight, down_weight):
    shards = lax.axis_size("tok")
    owner = lax.axis_index("tok")
    width = out_gain.shape[0] * lax.axis_size("head")
    scale = 1.0 / math.sqrt(queries.shape[1] * shards)
    own_rows = (gate_weight[0], up_weight[0], down_weight[0])
    starts = [owner * own_rows[which].shape[0] for which in range(3)]
    first = tuple(lax.all_gather(rows, "tok", axis=0, tiled=True) for rows in own_rows)
    fast, saved_keys = fast_forward(keys, values, first)
    apply_first = apply_forward(queries[0], first)
    grad_first, partial_first = apply_backward(
        queries[0], first, apply_first, upstream[0], out_gain, width
    )
    totals = lax.psum((fast[0], fast[1], fast[2]), "tok")
    roots = [jnp.sqrt(jnp.sum(totals[which] * totals[which])) for which in range(3)]
    forward = [
        schulz_forward((totals[which] / (roots[which] + fro_eps)).astype(jnp.bfloat16))
        for which in range(3)
    ]
    second = tuple(
        (first[which].astype(jnp.float32) - forward[which][0].astype(jnp.float32)).astype(
            jnp.bfloat16
        )
        for which in range(3)
    )
    apply_second = apply_forward(queries[1], second)
    grad_second, partial_second = apply_backward(
        queries[1], second, apply_second, upstream[1], out_gain, width
    )
    rates = lax.psum((partial_second[0], partial_second[1], partial_second[2]), "tok")
    bottoms = [
        schulz_backward((-rates[which]).astype(jnp.bfloat16), forward[which][1])
        for which in range(3)
    ]
    cots = []
    for which in range(3):
        norm = roots[which] + fro_eps
        inner = jnp.sum(bottoms[which].astype(jnp.float32) * totals[which])
        cots.append(
            (
                bottoms[which].astype(jnp.float32) / norm
                - totals[which] * (inner / (norm * norm * roots[which]))
            ).astype(jnp.bfloat16)
        )
    grad_keys, grad_values, second_order = fast_second(keys, values, first, saved_keys, cots)
    grads = []
    for which in range(3):
        rate_rows = lax.dynamic_slice_in_dim(
            rates[which], starts[which], own_rows[which].shape[0], 0
        )
        summed = lax.psum_scatter(
            partial_first[which] + second_order[which], "tok", scatter_dimension=0, tiled=True
        )
        grads.append(((summed + rate_rows) * scale)[None])
    grad_queries = jnp.stack([grad_first, grad_second])
    return (grad_queries, grad_keys, grad_values, *grads)


def shift(array, ring, step):
    pairs = [
        (o * 2 + i, ((o + step) % ring) * 2 + i) for o in range(ring) for i in range(2)
    ]
    return lax.ppermute(array, "tok", pairs)


def swap(array, ring):
    return lax.ppermute(array, "tok", [(i, i ^ 1) for i in range(2 * ring)])


def tie(array, *earlier):
    return lax.optimization_barrier((array, *earlier))[0]


def head_terms(stats):
    heads = lax.axis_size("head")
    return [stats] + [
        lax.ppermute(stats, "head", [(i, (i + k) % heads) for i in range(heads)])
        for k in range(1, heads)
    ]


def owner_of(ring, me, outer, flip):
    return ((me // 2 + outer + ring) % ring) * 2 + (me % 2 + flip) % 2


def move(rows, sems):
    copies = [
        pltpu.make_async_copy(
            source.at[pl.ds(begin, count)], target.at[pl.ds(place, count)], sems.at[index]
        )
        for index, (source, begin, target, place, count) in enumerate(rows)
    ]
    for copy in copies:
        copy.start()
    for copy in copies:
        copy.wait()


def chunks_of(tokens):
    step = min(ROWS, tokens)
    return [slice(i, i + step) for i in range(0, tokens, step)]


def pack_kernel(gate, up, down, keys, values, queries, upstream, first, second, sems):
    rows = []
    for target, sources in (
        (first, (gate.at[0], up.at[0], down.at[0], keys, values)),
        (second, (queries.at[1], upstream.at[1])),
    ):
        begin = 0
        for source in sources:
            rows.append((source, 0, target, begin, source.shape[0]))
            begin += source.shape[0]
    move(rows, sems)


def place_rows(layout, ring, me, pieces, targets):
    rows = []
    for (outer, flip, slot), piece in zip(layout, pieces):
        owner = owner_of(ring, me, outer, flip)
        begin = 0
        for index, target in enumerate(targets):
            count = target.shape[0] // (2 * ring)
            place = pl.multiple_of(owner * count, 16) if index < 3 else slot * count
            rows.append((piece, begin, target, place, count))
            begin += count
    return rows


def place_kernel(layout, ring, carried, me_ref, *refs):
    sems = refs[-1]
    refs = refs[:-1]
    targets = refs[-6:-1] if carried else refs[-5:]
    rows = place_rows(layout, ring, me_ref[0], refs, targets)
    begin = 0
    for source in refs[len(layout):len(layout) + carried]:
        rows.append((source, 0, refs[-1], begin, source.shape[0]))
        begin += source.shape[0]
    move(rows, sems)


def fast_kernel(layout, ring, me_ref, *refs):
    pieces, refs = refs[:len(layout)], refs[len(layout) + 5:]
    (wg, wu, wd, keys, values, gk_ref, uk_ref, back_ref, totals_g, totals_u, totals_d) = refs[:11]
    d_gate, d_up, hidden, sems = refs[11:]
    move(place_rows(layout, ring, me_ref[0], pieces, (wg, wu, wd, keys, values)), sems)
    for part in chunks_of(keys.shape[0]):
        gk = product(keys[part], wg[...])
        uk = product(keys[part], wu[...])
        back = -against(values[part], wd[...])
        sigma = jax.nn.sigmoid(gk)
        active = gk * sigma
        slope = sigma * (1.0 + gk * (1.0 - sigma))
        hidden[part] = (active * uk).astype(bf16)
        d_gate[part] = (back * uk * slope).astype(bf16)
        d_up[part] = (back * active).astype(bf16)
        gk_ref[part], uk_ref[part], back_ref[part] = gk, uk, back
    totals_g[...] = across(keys[...], d_gate[...])
    totals_u[...] = across(keys[...], d_up[...])
    totals_d[...] = -across(hidden[...], values[...])


def schulz_kernel(total_ref, weight, xs, grams, blends, following_ref, root_ref):
    total = total_ref[...]
    root = jnp.sqrt(jnp.sum(total * total, keepdims=True))
    root_ref[...] = jnp.broadcast_to(root, root_ref.shape)
    xs[0] = (total / (root + fro_eps)).astype(bf16)
    for sweep in range(NS_STEPS):
        current = xs[sweep]
        gram = against(current, current).astype(bf16)
        blend = (cube_coef * gram.astype(f32) + fifth_coef * product(gram, gram)).astype(bf16)
        following = (lin_coef * current.astype(f32) + product(blend, current)).astype(bf16)
        grams[sweep] = gram
        blends[sweep] = blend
        if sweep + 1 < NS_STEPS:
            xs[sweep + 1] = following
    following_ref[...] = (weight[...].astype(f32) - following.astype(f32)).astype(bf16)


def row_sums(columns, tokens):
    lanes = lax.broadcasted_iota(jnp.int32, (tokens, 128), 1)
    spread = jnp.where(lanes == 0, columns[0], jnp.where(lanes == 1, columns[1], 0.0))
    return spread.T[:8]


def forward_part(
    parts, queries, upstream, gain, wg, wu, wd, gq_ref, uq_ref, hidden_ref, out_ref, stats
):
    for part in parts:
        gq = product(queries[part], wg[...])
        uq = product(queries[part], wu[...])
        hidden = (gq * jax.nn.sigmoid(gq) * uq).astype(bf16)
        output = product(hidden, wd[...])
        weighted = gain[...] * upstream[part].astype(f32)
        sums = (
            jnp.sum(output * output, axis=1, keepdims=True),
            jnp.sum(weighted * output, axis=1, keepdims=True),
        )
        stats[:, part] = row_sums(sums, output.shape[0])
        gq_ref[part], uq_ref[part], hidden_ref[part], out_ref[part] = gq, uq, hidden, output


def backward_part(
    width, queries, upstream, gain, wg, wu, wd, gq_ref, uq_ref, hidden, out_ref, sums,
    grad_ref, d_gate, d_up, d_out, own,
):
    for part in chunks_of(queries.shape[0]):
        total = sum(term[:, part] for term in sums)
        tokens = total.shape[1]
        square = total[0:1] / width
        inverse = lax.rsqrt(square + rms_eps)
        pull = inverse * inverse * inverse * (total[1:2] / width)
        index = lax.broadcasted_iota(jnp.int32, (128, tokens), 0)
        columns = jnp.where(index == 0, inverse, jnp.where(index == 1, pull, 0.0)).T
        inverse, pull = columns[:, 0:1], columns[:, 1:2]
        weighted = gain[...] * upstream[part].astype(f32)
        d_output = (inverse * weighted - out_ref[part] * pull).astype(bf16)
        back = against(d_output, wd[...])
        gq, uq = gq_ref[part], uq_ref[part]
        sigma = jax.nn.sigmoid(gq)
        d_gate[part] = (back * uq * sigma * (1.0 + gq * (1.0 - sigma))).astype(bf16)
        d_up[part] = (back * gq * sigma).astype(bf16)
        d_out[part] = d_output
    grad_ref[...] = (
        against(d_gate[:own], wg[...]) + against(d_up[:own], wu[...])
    ).astype(bf16)


def first_forward_kernel(
    queries_ref, upstream_ref, gain, wg, wu, wd, queries, upstream, gq, uq, hidden, out, stats
):
    queries[...], upstream[...] = queries_ref[0], upstream_ref[0]
    parts = chunks_of(queries.shape[0])
    forward_part(parts, queries, upstream, gain, wg, wu, wd, gq, uq, hidden, out, stats)


def first_backward_kernel(
    width, ring, me_ref, queries, upstream, gain, wg, wu, wd, gq, uq, hidden, out, *refs
):
    count = len(refs) - 7
    sums = refs[:count]
    grad, kept, sent, d_gate, d_up, d_out, partial = refs[count:]
    backward_part(
        width, queries, upstream, gain, wg, wu, wd, gq, uq, hidden, out, sums,
        grad, d_gate, d_up, d_out, queries.shape[0],
    )
    inner = me_ref[0] % 2
    rows = kept.shape[2]
    for which, (left, right) in enumerate(((queries, d_gate), (queries, d_up), (hidden, d_out))):
        partial[...] = across(left[...], right[...]).astype(bf16)
        for outer in range(ring):
            mine = pl.multiple_of((outer * 2 + inner) * rows, 16)
            other = pl.multiple_of((outer * 2 + 1 - inner) * rows, 16)
            kept[outer, which] = partial[pl.ds(mine, rows)]
            sent[outer, which] = partial[pl.ds(other, rows)]


def pair_kernel(ring, me_ref, kept, received, own, *others):
    outer = me_ref[0] // 2
    own[...] = kept[outer].astype(f32) + received[outer].astype(f32)
    for step, target in enumerate(others, 1):
        place = (outer + step) % ring
        target[...] = (kept[place].astype(f32) + received[place].astype(f32)).astype(bf16)


def second_forward_kernel(first, count, gain, wg, wu, wd, *refs):
    pieces = refs[:count]
    queries, upstream, gq, uq, hidden, out, stats, sems = refs[-8:]
    tokens = pieces[0].shape[0] // 4
    rows = []
    for slot, piece in enumerate(pieces):
        for half in range(2):
            place = (2 * (first + slot) + half) * tokens
            rows.append((piece, 2 * half * tokens, queries, place, tokens))
            rows.append((piece, (2 * half + 1) * tokens, upstream, place, tokens))
    move(rows, sems)
    parts = [
        slice(part.start + 2 * first * tokens, part.stop + 2 * first * tokens)
        for part in chunks_of(2 * count * tokens)
    ]
    forward_part(parts, queries, upstream, gain, wg, wu, wd, gq, uq, hidden, out, stats)


def second_backward_kernel(
    width, own, grad_first, queries, upstream, gain, wg, wu, wd, gq, uq, hidden, out, *refs
):
    count = len(refs) - 7
    sums = refs[:count]
    grad, rate_g, rate_u, rate_d, d_gate, d_up, d_out = refs[count:]
    grad[0] = grad_first[...]
    backward_part(
        width, queries, upstream, gain, wg, wu, wd, gq, uq, hidden, out, sums,
        grad.at[1], d_gate, d_up, d_out, own,
    )
    rate_g[...] = across(queries[...], d_gate[...])
    rate_u[...] = across(queries[...], d_up[...])
    rate_d[...] = across(hidden[...], d_out[...])


def schulz_back_kernel(*refs):
    rates, totals, xs, grams, blends, roots, cots = (refs[i:i + 3] for i in range(0, 21, 3))
    symmetric, mixed = refs[21:]
    for which in range(3):
        cots[which][...] = (-rates[which][...]).astype(bf16)
    for sweep in reversed(range(NS_STEPS)):
        for which in range(3):
            cross = against(cots[which][...], xs[which][sweep])
            symmetric[which] = (cross + cross.T).astype(bf16)
        for which in range(3):
            bent = product(symmetric[which], grams[which][sweep])
            mixed[which] = (
                cube_coef * symmetric[which].astype(f32) + fifth_coef * (bent + bent.T)
            ).astype(bf16)
        for which in range(3):
            cots[which][...] = (
                lin_coef * cots[which][...].astype(f32)
                + product(blends[which][sweep], cots[which][...])
                + product(mixed[which], xs[which][sweep])
            ).astype(bf16)
    for which in range(3):
        root = roots[which][0:1, 0:1]
        norm = root + fro_eps
        total = totals[which][...]
        bottom = cots[which][...].astype(f32)
        inner = jnp.sum(bottom * total, keepdims=True)
        cots[which][...] = (bottom / norm - total * (inner / (norm * norm * root))).astype(bf16)


def last_kernel(
    own, scale, me_ref, keys, values, wg, wu, wd, gk_ref, uk_ref, back_ref,
    cot_g, cot_u, cot_d, rate_g, rate_u, rate_d, *refs,
):
    count = len(refs) - 13
    firsts = refs[:count]
    grad_keys, grad_values, grad_g, grad_u, grad_d = refs[count:count + 5]
    lower, upper, d_back, pk, rk, hk, keys_t, back_t = refs[count + 5:]
    for part in chunks_of(keys.shape[0]):
        gk, uk, back = gk_ref[part], uk_ref[part], back_ref[part]
        sigma = jax.nn.sigmoid(gk)
        active = gk * sigma
        slope = sigma * (1.0 + gk * (1.0 - sigma))
        curve = sigma * (1.0 - sigma) * (2.0 + gk * (1.0 - 2.0 * sigma))
        ek = product(keys[part], cot_g[...])
        fk = product(keys[part], cot_u[...])
        hk_part = -against(values[part], cot_d[...])
        d_back_part = (ek * uk * slope + fk * active).astype(bf16)
        d_back[part] = d_back_part
        back_t[:, part] = d_back_part.T
        keys_t[:, part] = keys[part].T
        upper[part] = (ek * back * slope + hk_part * active).astype(bf16)
        lower[part] = (
            ek * back * uk * curve + fk * back * slope + hk_part * uk * slope
        ).astype(bf16)
        if part.start == 0:
            pk[...] = (back * uk * slope).astype(bf16)[:own]
            rk[...] = (back * active).astype(bf16)[:own]
            hk[...] = (active * uk).astype(bf16)[:own]
    grad_keys[...] = (
        against(pk[...], cot_g[...])
        + against(rk[...], cot_u[...])
        + against(lower[:own], wg[...])
        + against(upper[:own], wu[...])
    ).astype(bf16)
    grad_values[...] = (
        -product(hk[...], cot_d[...]) - product(d_back[:own], wd[...])
    ).astype(bf16)
    rows = grad_g.shape[1]
    start = pl.multiple_of(me_ref[0] * rows, 16)
    for which, (left, right, rate, grad) in enumerate((
        (keys_t, lower, rate_g, grad_g), (keys_t, upper, rate_u, grad_u), (back_t, values, rate_d, grad_d)
    )):
        second = product(left[pl.ds(start, rows)], right[...])
        first = sum(ref[which].astype(f32) for ref in firsts)
        both = first - second if which == 2 else first + second
        grad[0] = (both + rate[pl.ds(start, rows)]) * scale


def vmem():
    return pl.BlockSpec(memory_space=pltpu.VMEM)


def smem():
    return pl.BlockSpec(memory_space=pltpu.SMEM)


def hbm():
    return pl.BlockSpec(memory_space=pltpu.HBM)


def anywhere():
    return pl.BlockSpec(memory_space=pl.ANY)


def light():
    return pl.CostEstimate(flops=1, bytes_accessed=1, transcendentals=0)


def params(mib):
    return pltpu.CompilerParams(vmem_limit_bytes=mib * 2**20)


def gather_tokens(queries, keys, values, upstream, out_gain, gate_weight, up_weight, down_weight):
    shards = lax.axis_size("tok")
    ring = shards // 2
    me = lax.axis_index("tok")
    me_ref = jnp.reshape(me, (1,)).astype(jnp.int32)
    own, depth = keys.shape
    rows = gate_weight.shape[1]
    hidden = gate_weight.shape[2]
    tokens = own * shards
    width = out_gain.shape[0] * lax.axis_size("head")
    scale = 1.0 / math.sqrt(tokens)
    gain = out_gain[None]
    S = jax.ShapeDtypeStruct

    matrix = (depth, hidden)
    wide, narrow = S(matrix, f32), S(matrix, bf16)

    packed, packed_second = pl.pallas_call(
        pack_kernel,
        out_shape=(
            S((2 * rows + down_weight.shape[1] + 2 * own, depth), bf16), S((2 * own, depth), bf16),
        ),
        in_specs=[hbm()] * 7,
        out_specs=[vmem()] * 2,
        scratch_shapes=[pltpu.SemaphoreType.DMA((7,))],
        compiler_params=params(60),
    )(gate_weight, up_weight, down_weight, keys, values, queries, upstream)
    buffers = (narrow, narrow, narrow, S((tokens, depth), bf16), S((tokens, depth), bf16))

    def place(pieces, layout, state=(), carry=(), others=()):
        out_shape = buffers
        if carry:
            out_shape += (S((sum(array.shape[0] for array in carry), depth), bf16),)
        start = 1 + len(pieces) + len(carry) + len(others)
        out = pl.pallas_call(
            functools.partial(place_kernel, layout, ring, len(carry)),
            out_shape=out_shape,
            in_specs=[smem()] + [anywhere()] * (start - 1 + len(state)),
            out_specs=[anywhere()] * len(out_shape),
            scratch_shapes=[pltpu.SemaphoreType.DMA((5 * len(pieces) + len(carry),))],
            input_output_aliases={start + index: index for index in range(len(state))},
            cost_estimate=light(),
            compiler_params=params(4),
        )(me_ref, *pieces, *carry, *others, *state)
        return (out[:5], out[5]) if carry else (out, None)

    crossed = swap(packed, ring)
    crossed_second = swap(packed_second, ring)
    up = shift(packed, ring, 1)
    state, carried = place((packed, crossed), ((0, 0, 0), (0, 1, 1)), carry=(packed,))
    down = shift(carried, ring, -1)
    crossed_up = swap(up, ring)
    crossed_down = swap(down, ring)
    state, carried = place((up,), ((-1, 0, 2),), state, (up,), (crossed_second,))
    far = shift(carried, ring, 1)
    crossed_far = swap(far, ring)
    state, pair = place(
        (down, crossed_up), ((1, 0, 3), (-1, 1, 4)), state, (packed_second, crossed_second)
    )
    state, _ = place((far, crossed_down), ((-2, 0, 5), (1, 1, 6)), state)
    layout = ((-2, 1, 7),)
    (wg, wu, wd, all_keys, all_values, gk, uk, back, *totals) = pl.pallas_call(
        functools.partial(fast_kernel, layout, ring),
        out_shape=(
            narrow, narrow, narrow, S((tokens, depth), bf16), S((tokens, depth), bf16),
            S((tokens, hidden), f32), S((tokens, hidden), f32), S((tokens, hidden), f32),
            wide, wide, wide,
        ),
        in_specs=[smem(), anywhere()] + [anywhere()] * 5,
        out_specs=[vmem()] * 11,
        scratch_shapes=[pltpu.VMEM((tokens, hidden), bf16)] * 3 + [pltpu.SemaphoreType.DMA((5,))],
        input_output_aliases={2 + index: index for index in range(5)},
        cost_estimate=light(),
        compiler_params=params(24),
    )(me_ref, crossed_far, *state)

    up, down = shift(pair, ring, 1), shift(pair, ring, -1)
    pairs = [pair, up, down, shift(tie(up, totals[0]), ring, 1)]

    queries0, upstream0, gq0, uq0, hidden0, out0, stats0 = pl.pallas_call(
        first_forward_kernel,
        out_shape=(
            S((own, depth), bf16), S((own, depth), bf16),
            S((own, hidden), f32), S((own, hidden), f32), S((own, hidden), bf16),
            S((own, depth), f32), S((8, own), f32),
        ),
        in_specs=[vmem()] * 6,
        out_specs=[vmem()] * 7,
        cost_estimate=light(),
        compiler_params=params(16),
    )(queries, upstream, gain, wg, wu, wd)

    def schulz(which, total):
        return pl.pallas_call(
            schulz_kernel,
            out_shape=(
                S((NS_STEPS, *matrix), bf16), S((NS_STEPS, *matrix), bf16),
                S((NS_STEPS, *matrix), bf16), narrow, S((8, 128), f32),
            ),
            in_specs=[vmem()] * 2,
            out_specs=[vmem()] * 5,
            cost_estimate=light(),
            compiler_params=params(16),
        )(total, (wg, wu, wd)[which])

    terms0 = head_terms(stats0)
    first_weight = schulz(0, totals[0])
    terms0[0] = tie(terms0[0], first_weight[4])
    grad_first, kept, sent = pl.pallas_call(
        functools.partial(first_backward_kernel, width, ring),
        out_shape=(
            S((own, depth), bf16), S((ring, 3, rows, hidden), bf16), S((ring, 3, rows, hidden), bf16),
        ),
        in_specs=[smem()] + [vmem()] * (10 + len(terms0)),
        out_specs=[vmem()] * 3,
        scratch_shapes=[pltpu.VMEM((own, hidden), bf16)] * 2
        + [pltpu.VMEM((own, depth), bf16), pltpu.VMEM(matrix, bf16)],
        cost_estimate=light(),
        compiler_params=params(20),
    )(me_ref, queries0, upstream0, gain, wg, wu, wd, gq0, uq0, hidden0, out0, *terms0)

    forward = [first_weight, schulz(1, totals[1]), schulz(2, tie(totals[2], down))]

    seconds = [forward[which][3] for which in range(3)]
    def second_forward(first, arrived, state=()):
        start = 4 + len(arrived)
        return pl.pallas_call(
            functools.partial(second_forward_kernel, first, len(arrived)),
            out_shape=(
                S((tokens, depth), bf16), S((tokens, depth), bf16),
                S((tokens, hidden), f32), S((tokens, hidden), f32), S((tokens, hidden), bf16),
                S((tokens, depth), f32), S((8, tokens), f32),
            ),
            in_specs=[vmem()] * 4 + [anywhere()] * (len(arrived) + len(state)),
            out_specs=[vmem()] * 7,
            scratch_shapes=[pltpu.SemaphoreType.DMA((4 * len(arrived),))],
            input_output_aliases={start + index: index for index in range(len(state))},
            cost_estimate=light(),
            compiler_params=params(24),
        )(gain, *seconds, *arrived, *state)

    state = second_forward(0, pairs[:-1])
    all_queries, all_upstream, gq, uq, hidden_q, out, stats = second_forward(
        len(pairs) - 1, pairs[-1:], state
    )
    terms = head_terms(stats)

    block = S((3, rows, hidden), bf16)
    summed = pl.pallas_call(
        functools.partial(pair_kernel, ring),
        out_shape=(S((3, rows, hidden), f32),) + (block,) * (ring - 1),
        in_specs=[smem()] + [vmem()] * 2,
        out_specs=[vmem()] * ring,
        compiler_params=params(12),
    )(me_ref, tie(kept, terms[1]), swap(tie(sent, down), ring))
    firsts = [summed[0]] + [shift(summed[step], ring, step) for step in range(1, ring)]

    grad_queries, *rates = pl.pallas_call(
        functools.partial(second_backward_kernel, width, own),
        out_shape=(S((2, own, depth), bf16), wide, wide, wide),
        in_specs=[vmem()] * (11 + len(terms)),
        out_specs=[vmem()] * 4,
        scratch_shapes=[pltpu.VMEM((tokens, hidden), bf16)] * 2
        + [pltpu.VMEM((tokens, depth), bf16)],
        cost_estimate=light(),
        compiler_params=params(20),
    )(grad_first, all_queries, all_upstream, gain, *seconds, gq, uq, hidden_q, out, *terms)

    cots = pl.pallas_call(
        schulz_back_kernel,
        out_shape=(narrow,) * 3,
        in_specs=[vmem()] * 18,
        out_specs=[vmem()] * 3,
        scratch_shapes=[pltpu.VMEM((3, *matrix), bf16)] * 2,
        cost_estimate=light(),
        compiler_params=params(20),
    )(
        *rates, *totals, *(forward[which][part] for part in (0, 1, 2) for which in range(3)),
        *(forward[which][4] for which in range(3)),
    )

    return (grad_queries, *pl.pallas_call(
        functools.partial(last_kernel, own, scale),
        out_shape=(
            S((own, depth), bf16), S((own, depth), bf16),
            S((1, rows, hidden), f32), S((1, rows, hidden), f32), S((1, rows, hidden), f32),
        ),
        in_specs=[smem()] + [vmem()] * (14 + len(firsts)),
        out_specs=[vmem()] * 5,
        scratch_shapes=[
            pltpu.VMEM((tokens, hidden), bf16),
            pltpu.VMEM((tokens, hidden), bf16),
            pltpu.VMEM((tokens, hidden), bf16),
            pltpu.VMEM((own, hidden), bf16),
            pltpu.VMEM((own, hidden), bf16),
            pltpu.VMEM((own, hidden), bf16),
            pltpu.VMEM((depth, tokens), bf16),
            pltpu.VMEM((hidden, tokens), bf16),
        ],
        cost_estimate=light(),
        compiler_params=params(24),
    )(
        me_ref, all_keys, all_values, wg, wu, wd, gk, uk, back, *cots, *rates, *firsts,
    ))


def per_device(queries, keys, values, upstream, out_gain, gate_weight, up_weight, down_weight):
    shards = lax.axis_size("tok")
    tokens = keys.shape[0] * shards
    few = 4 * tokens <= 12 * gate_weight.shape[2] and shards == 8
    plan = gather_tokens if few else split_tokens
    return plan(queries, keys, values, upstream, out_gain, gate_weight, up_weight, down_weight)


def solution(mesh):
    in_specs = (
        P(None, "tok", "head"),
        P("tok", "head"),
        P("tok", "head"),
        P(None, "tok", "head"),
        P("head"),
        P("head", "tok", None),
        P("head", "tok", None),
        P("head", "tok", None),
    )
    out_specs = (
        P(None, "tok", "head"),
        P("tok", "head"),
        P("tok", "head"),
        P("head", "tok", None),
        P("head", "tok", None),
        P("head", "tok", None),
    )
    return jax.shard_map(
        per_device, mesh=mesh, in_specs=in_specs, out_specs=out_specs, check_vma=False
    )
```

```python
import functools
import math

import jax
import jax.numpy as jnp
from jax import lax
from jax.experimental import pallas as pl
from jax.experimental.pallas import tpu as pltpu
from jax.sharding import PartitionSpec as P

NS_STEPS = 2


lin_coef = 3.4445
cube_coef = -4.775
fifth_coef = 2.0315
rms_eps = 1e-06
fro_eps = 1e-07

bf16 = jnp.bfloat16
f32 = jnp.float32
ROWS = 256


def product(left, right):
    return jnp.dot(left, right, preferred_element_type=jnp.float32)


def across(left, right):
    return lax.dot_general(
        left, right, (((0,), (0,)), ((), ())), preferred_element_type=jnp.float32
    )


def against(left, right):
    return lax.dot_general(
        left, right, (((1,), (1,)), ((), ())), preferred_element_type=jnp.float32
    )


def fast_forward(keys, values, weights):
    gate_weight, up_weight, down_weight = weights
    gate_pre = product(keys, gate_weight)
    up_pre = product(keys, up_weight)
    sigma = jax.nn.sigmoid(gate_pre)
    active = gate_pre * sigma
    hidden = (active * up_pre).astype(jnp.bfloat16)
    back = -against(values, down_weight)
    slope = sigma * (1.0 + gate_pre * (1.0 - sigma))
    d_gate = (back * up_pre * slope).astype(jnp.bfloat16)
    d_up = (back * active).astype(jnp.bfloat16)
    fast = (across(keys, d_gate), across(keys, d_up), -across(hidden, values))
    saved = (gate_pre, up_pre, sigma, active, hidden, back, slope, d_gate, d_up)
    return (fast, saved)


def fast_second(keys, values, weights, saved, cots):
    gate_weight, up_weight, down_weight = weights
    gate_pre, up_pre, sigma, active, hidden, back, slope, d_gate, d_up = saved
    cot_gate, cot_up, cot_down = cots
    along_gate = product(keys, cot_gate)
    along_up = product(keys, cot_up)
    along_hidden = -against(values, cot_down)
    curve = sigma * (1.0 - sigma) * (2.0 + gate_pre * (1.0 - 2.0 * sigma))
    d_back = (along_gate * up_pre * slope + along_up * active).astype(jnp.bfloat16)
    d_upper = (along_gate * back * slope + along_hidden * active).astype(jnp.bfloat16)
    d_lower = (
        along_gate * back * up_pre * curve + along_up * back * slope + along_hidden * up_pre * slope
    ).astype(jnp.bfloat16)
    grad_keys = (
        against(d_gate, cot_gate)
        + against(d_up, cot_up)
        + against(d_lower, gate_weight)
        + against(d_upper, up_weight)
    ).astype(jnp.bfloat16)
    grad_values = (-product(hidden, cot_down) - product(d_back, down_weight)).astype(jnp.bfloat16)
    partial_value = (across(keys, d_lower), across(keys, d_upper), -across(d_back, values))
    return (grad_keys, grad_values, partial_value)


def apply_forward(queries, weights):
    gate_weight, up_weight, down_weight = weights
    gate_pre = product(queries, gate_weight)
    up_pre = product(queries, up_weight)
    sigma = jax.nn.sigmoid(gate_pre)
    hidden = (gate_pre * sigma * up_pre).astype(jnp.bfloat16)
    output = product(hidden, down_weight)
    return (gate_pre, up_pre, sigma, hidden, output)


def statistics(output, upstream, out_gain, width):
    weighted = out_gain * upstream.astype(jnp.float32)
    sums = lax.psum((jnp.sum(output * output, axis=1), jnp.sum(weighted * output, axis=1)), "head")
    return (lax.rsqrt(sums[0] / width + rms_eps), sums[1] / width)


def apply_backward(queries, weights, saved, upstream, out_gain, width):
    gate_weight, up_weight, down_weight = weights
    gate_pre, up_pre, sigma, hidden, output = saved
    inverse_rms, mean_dot = statistics(output, upstream, out_gain, width)
    weighted = out_gain * upstream.astype(jnp.float32)
    d_output = (
        inverse_rms[:, None] * weighted
        - output * (inverse_rms * inverse_rms * inverse_rms * mean_dot)[:, None]
    ).astype(jnp.bfloat16)
    back = against(d_output, down_weight)
    slope = sigma * (1.0 + gate_pre * (1.0 - sigma))
    d_gate = (back * up_pre * slope).astype(jnp.bfloat16)
    d_up = (back * gate_pre * sigma).astype(jnp.bfloat16)
    grad_queries = (against(d_gate, gate_weight) + against(d_up, up_weight)).astype(jnp.bfloat16)
    partial_value = (across(queries, d_gate), across(queries, d_up), across(hidden, d_output))
    return (grad_queries, partial_value)


def schulz_forward(begin):
    current = begin
    saved = []
    for sweep in range(NS_STEPS):
        gram = against(current, current).astype(jnp.bfloat16)
        blend = (cube_coef * gram.astype(jnp.float32) + fifth_coef * product(gram, gram)).astype(
            jnp.bfloat16
        )
        following = (lin_coef * current.astype(jnp.float32) + product(blend, current)).astype(
            jnp.bfloat16
        )
        saved.append((current, gram, blend))
        current = following
    return (current, saved)


def schulz_backward(cotan, saved):
    current = cotan
    for iterate, gram, blend in reversed(saved):
        cross = against(current, iterate)
        symmetric = (cross + cross.T).astype(jnp.bfloat16)
        bent = product(symmetric, gram)
        mixed = (cube_coef * symmetric.astype(jnp.float32) + fifth_coef * (bent + bent.T)).astype(
            jnp.bfloat16
        )
        current = (
            lin_coef * current.astype(jnp.float32)
            + product(blend, current)
            + product(mixed, iterate)
        ).astype(jnp.bfloat16)
    return current


def split_tokens(queries, keys, values, upstream, out_gain, gate_weight, up_weight, down_weight):
    shards = lax.axis_size("tok")
    owner = lax.axis_index("tok")
    width = out_gain.shape[0] * lax.axis_size("head")
    scale = 1.0 / math.sqrt(queries.shape[1] * shards)
    own_rows = (gate_weight[0], up_weight[0], down_weight[0])
    starts = [owner * own_rows[which].shape[0] for which in range(3)]
    first = tuple(lax.all_gather(rows, "tok", axis=0, tiled=True) for rows in own_rows)
    fast, saved_keys = fast_forward(keys, values, first)
    apply_first = apply_forward(queries[0], first)
    grad_first, partial_first = apply_backward(
        queries[0], first, apply_first, upstream[0], out_gain, width
    )
    totals = lax.psum((fast[0], fast[1], fast[2]), "tok")
    roots = [jnp.sqrt(jnp.sum(totals[which] * totals[which])) for which in range(3)]
    forward = [
        schulz_forward((totals[which] / (roots[which] + fro_eps)).astype(jnp.bfloat16))
        for which in range(3)
    ]
    second = tuple(
        (first[which].astype(jnp.float32) - forward[which][0].astype(jnp.float32)).astype(
            jnp.bfloat16
        )
        for which in range(3)
    )
    apply_second = apply_forward(queries[1], second)
    grad_second, partial_second = apply_backward(
        queries[1], second, apply_second, upstream[1], out_gain, width
    )
    rates = lax.psum((partial_second[0], partial_second[1], partial_second[2]), "tok")
    bottoms = [
        schulz_backward((-rates[which]).astype(jnp.bfloat16), forward[which][1])
        for which in range(3)
    ]
    cots = []
    for which in range(3):
        norm = roots[which] + fro_eps
        inner = jnp.sum(bottoms[which].astype(jnp.float32) * totals[which])
        cots.append(
            (
                bottoms[which].astype(jnp.float32) / norm
                - totals[which] * (inner / (norm * norm * roots[which]))
            ).astype(jnp.bfloat16)
        )
    grad_keys, grad_values, second_order = fast_second(keys, values, first, saved_keys, cots)
    grads = []
    for which in range(3):
        rate_rows = lax.dynamic_slice_in_dim(
            rates[which], starts[which], own_rows[which].shape[0], 0
        )
        summed = lax.psum_scatter(
            partial_first[which] + second_order[which], "tok", scatter_dimension=0, tiled=True
        )
        grads.append(((summed + rate_rows) * scale)[None])
    grad_queries = jnp.stack([grad_first, grad_second])
    return (grad_queries, grad_keys, grad_values, *grads)


def shift(array, ring, step):
    pairs = [
        (o * 2 + i, ((o + step) % ring) * 2 + i) for o in range(ring) for i in range(2)
    ]
    return lax.ppermute(array, "tok", pairs)


def swap(array, ring):
    return lax.ppermute(array, "tok", [(i, i ^ 1) for i in range(2 * ring)])


def tie(array, *earlier):
    return lax.optimization_barrier((array, *earlier))[0]


def head_terms(stats):
    heads = lax.axis_size("head")
    return [stats] + [
        lax.ppermute(stats, "head", [(i, (i + k) % heads) for i in range(heads)])
        for k in range(1, heads)
    ]


def owner_of(ring, me, outer, flip):
    return ((me // 2 + outer + ring) % ring) * 2 + (me % 2 + flip) % 2


def move(rows, sems):
    copies = [
        pltpu.make_async_copy(
            source.at[pl.ds(begin, count)], target.at[pl.ds(place, count)], sems.at[index]
        )
        for index, (source, begin, target, place, count) in enumerate(rows)
    ]
    for copy in copies:
        copy.start()
    for copy in copies:
        copy.wait()


def chunks_of(tokens):
    step = min(ROWS, tokens)
    return [slice(i, i + step) for i in range(0, tokens, step)]


def pack_kernel(gate, up, down, keys, values, queries, upstream, first, second, sems):
    rows = []
    for target, sources in (
        (first, (gate.at[0], up.at[0], down.at[0], keys, values)),
        (second, (queries.at[1], upstream.at[1])),
    ):
        begin = 0
        for source in sources:
            rows.append((source, 0, target, begin, source.shape[0]))
            begin += source.shape[0]
    move(rows, sems)


def place_rows(layout, ring, me, pieces, targets):
    rows = []
    for (outer, flip, slot), piece in zip(layout, pieces):
        owner = owner_of(ring, me, outer, flip)
        begin = 0
        for index, target in enumerate(targets):
            count = target.shape[0] // (2 * ring)
            place = pl.multiple_of(owner * count, 16) if index < 3 else slot * count
            rows.append((piece, begin, target, place, count))
            begin += count
    return rows


def place_kernel(layout, ring, carried, me_ref, *refs):
    sems = refs[-1]
    refs = refs[:-1]
    targets = refs[-6:-1] if carried else refs[-5:]
    rows = place_rows(layout, ring, me_ref[0], refs, targets)
    begin = 0
    for source in refs[len(layout):len(layout) + carried]:
        rows.append((source, 0, refs[-1], begin, source.shape[0]))
        begin += source.shape[0]
    move(rows, sems)


def fast_kernel(layout, ring, me_ref, *refs):
    pieces, refs = refs[:len(layout)], refs[len(layout) + 5:]
    wg, wu, wd, keys, values, by_gate, by_up, by_lower, by_upper = refs[:9]
    totals_g, totals_u, totals_d, pk, rk, hk, d_gate, d_up, hidden, sems = refs[9:]
    move(place_rows(layout, ring, me_ref[0], pieces, (wg, wu, wd, keys, values)), sems)
    for part in chunks_of(keys.shape[0]):
        gk = product(keys[part], wg[...])
        uk = product(keys[part], wu[...])
        back = -against(values[part], wd[...])
        sigma = jax.nn.sigmoid(gk)
        active = gk * sigma
        slope = sigma * (1.0 + gk * (1.0 - sigma))
        curve = sigma * (1.0 - sigma) * (2.0 + gk * (1.0 - 2.0 * sigma))
        along = uk * slope
        hidden[part] = (active * uk).astype(bf16)
        d_gate[part] = (back * along).astype(bf16)
        d_up[part] = (back * active).astype(bf16)
        by_gate[part], by_up[part] = along, active
        by_lower[part], by_upper[part] = back * uk * curve, back * slope
    totals_g[...] = across(keys[...], d_gate[...])
    totals_u[...] = across(keys[...], d_up[...])
    totals_d[...] = -across(hidden[...], values[...])
    own = pk.shape[0]
    pk[...], rk[...], hk[...] = d_gate[:own], d_up[:own], hidden[:own]


def schulz_kernel(count, *refs):
    totals, weights = refs[:count], refs[count:2 * count]
    outs = [refs[i:i + 5] for i in range(2 * count, 7 * count, 5)]
    for total_ref, (xs, _, _, _, root_ref) in zip(totals, outs):
        total = total_ref[...]
        root = jnp.sqrt(jnp.sum(total * total, keepdims=True))
        root_ref[...] = jnp.broadcast_to(root, root_ref.shape)
        xs[0] = (total / (root + fro_eps)).astype(bf16)
    for sweep in range(NS_STEPS):
        for xs, grams, _, _, _ in outs:
            grams[sweep] = against(xs[sweep], xs[sweep]).astype(bf16)
        for _, grams, blends, _, _ in outs:
            gram = grams[sweep]
            blends[sweep] = (
                cube_coef * gram.astype(f32) + fifth_coef * product(gram, gram)
            ).astype(bf16)
        for weight, (xs, _, blends, following_ref, _) in zip(weights, outs):
            current = xs[sweep]
            following = (
                lin_coef * current.astype(f32) + product(blends[sweep], current)
            ).astype(bf16)
            if sweep + 1 < NS_STEPS:
                xs[sweep + 1] = following
            else:
                following_ref[...] = (weight[...].astype(f32) - following.astype(f32)).astype(bf16)


def row_sums(columns, tokens):
    lanes = lax.broadcasted_iota(jnp.int32, (tokens, 128), 1)
    spread = jnp.where(lanes == 0, columns[0], jnp.where(lanes == 1, columns[1], 0.0))
    return spread.T[:8]


def forward_part(
    parts, queries, upstream, gain, wg, wu, wd, by_gate, by_up, hidden_ref, out_ref, stats
):
    for part in parts:
        gq = product(queries[part], wg[...])
        uq = product(queries[part], wu[...])
        sigma = jax.nn.sigmoid(gq)
        active = gq * sigma
        hidden = (active * uq).astype(bf16)
        output = product(hidden, wd[...])
        weighted = gain[...] * upstream[part].astype(f32)
        sums = (
            jnp.sum(output * output, axis=1, keepdims=True),
            jnp.sum(weighted * output, axis=1, keepdims=True),
        )
        stats[:, part] = row_sums(sums, output.shape[0])
        by_gate[part], by_up[part] = uq * sigma * (1.0 + gq * (1.0 - sigma)), active
        hidden_ref[part], out_ref[part] = hidden, output


def backward_part(
    width, queries, upstream, gain, wg, wu, wd, by_gate, by_up, hidden, out_ref, sums,
    grad_ref, d_gate, d_up, d_out, own,
):
    for part in chunks_of(queries.shape[0]):
        total = sum(term[:, part] for term in sums)
        tokens = total.shape[1]
        square = total[0:1] / width
        inverse = lax.rsqrt(square + rms_eps)
        pull = inverse * inverse * inverse * (total[1:2] / width)
        index = lax.broadcasted_iota(jnp.int32, (128, tokens), 0)
        columns = jnp.where(index == 0, inverse, jnp.where(index == 1, pull, 0.0)).T
        inverse, pull = columns[:, 0:1], columns[:, 1:2]
        weighted = gain[...] * upstream[part].astype(f32)
        d_output = (inverse * weighted - out_ref[part] * pull).astype(bf16)
        back = against(d_output, wd[...])
        d_gate[part] = (back * by_gate[part]).astype(bf16)
        d_up[part] = (back * by_up[part]).astype(bf16)
        d_out[part] = d_output
    grad_ref[...] = (
        against(d_gate[:own], wg[...]) + against(d_up[:own], wu[...])
    ).astype(bf16)


def first_forward_kernel(
    queries_ref, upstream_ref, gain, wg, wu, wd, queries, upstream, gq, uq, hidden, out, stats
):
    queries[...], upstream[...] = queries_ref[0], upstream_ref[0]
    parts = chunks_of(queries.shape[0])
    forward_part(parts, queries, upstream, gain, wg, wu, wd, gq, uq, hidden, out, stats)


def first_backward_kernel(
    width, ring, me_ref, queries, upstream, gain, wg, wu, wd, gq, uq, hidden, out, *refs
):
    count = len(refs) - 7
    sums = refs[:count]
    grad, kept, sent, d_gate, d_up, d_out, partial = refs[count:]
    backward_part(
        width, queries, upstream, gain, wg, wu, wd, gq, uq, hidden, out, sums,
        grad, d_gate, d_up, d_out, queries.shape[0],
    )
    inner = me_ref[0] % 2
    rows = kept.shape[2]
    for which, (left, right) in enumerate(((queries, d_gate), (queries, d_up), (hidden, d_out))):
        partial[...] = across(left[...], right[...]).astype(bf16)
        for outer in range(ring):
            mine = pl.multiple_of((outer * 2 + inner) * rows, 16)
            other = pl.multiple_of((outer * 2 + 1 - inner) * rows, 16)
            kept[outer, which] = partial[pl.ds(mine, rows)]
            sent[outer, which] = partial[pl.ds(other, rows)]


def pair_kernel(ring, me_ref, kept, received, own, *others):
    outer = me_ref[0] // 2
    own[...] = kept[outer].astype(f32) + received[outer].astype(f32)
    for step, target in enumerate(others, 1):
        place = (outer + step) % ring
        target[...] = (kept[place].astype(f32) + received[place].astype(f32)).astype(bf16)


def second_forward_kernel(first, count, gain, wg, wu, wd, *refs):
    pieces = refs[:count]
    queries, upstream, gq, uq, hidden, out, stats, sems = refs[-8:]
    tokens = pieces[0].shape[0] // 4
    rows = []
    for slot, piece in enumerate(pieces):
        for half in range(2):
            place = (2 * (first + slot) + half) * tokens
            rows.append((piece, 2 * half * tokens, queries, place, tokens))
            rows.append((piece, (2 * half + 1) * tokens, upstream, place, tokens))
    move(rows, sems)
    parts = [
        slice(part.start + 2 * first * tokens, part.stop + 2 * first * tokens)
        for part in chunks_of(2 * count * tokens)
    ]
    forward_part(parts, queries, upstream, gain, wg, wu, wd, gq, uq, hidden, out, stats)


def second_backward_kernel(
    width, own, grad_first, queries, upstream, gain, wg, wu, wd, gq, uq, hidden, out, *refs
):
    count = len(refs) - 7
    sums = refs[:count]
    grad, rate_g, rate_u, rate_d, d_gate, d_up, d_out = refs[count:]
    grad[0] = grad_first[...]
    backward_part(
        width, queries, upstream, gain, wg, wu, wd, gq, uq, hidden, out, sums,
        grad.at[1], d_gate, d_up, d_out, own,
    )
    rate_g[...] = across(queries[...], d_gate[...])
    rate_u[...] = across(queries[...], d_up[...])
    rate_d[...] = across(hidden[...], d_out[...])


def schulz_back_kernel(*refs):
    rates, totals, xs, grams, blends, roots, cots = (refs[i:i + 3] for i in range(0, 21, 3))
    symmetric, mixed = refs[21:]
    for which in range(3):
        cots[which][...] = (-rates[which][...]).astype(bf16)
    for sweep in reversed(range(NS_STEPS)):
        for which in range(3):
            cross = against(cots[which][...], xs[which][sweep])
            symmetric[which] = (cross + cross.T).astype(bf16)
        for which in range(3):
            bent = product(symmetric[which], grams[which][sweep])
            mixed[which] = (
                cube_coef * symmetric[which].astype(f32) + fifth_coef * (bent + bent.T)
            ).astype(bf16)
        for which in range(3):
            cots[which][...] = (
                lin_coef * cots[which][...].astype(f32)
                + product(blends[which][sweep], cots[which][...])
                + product(mixed[which], xs[which][sweep])
            ).astype(bf16)
    for which in range(3):
        root = roots[which][0:1, 0:1]
        norm = root + fro_eps
        total = totals[which][...]
        bottom = cots[which][...].astype(f32)
        inner = jnp.sum(bottom * total, keepdims=True)
        cots[which][...] = (bottom / norm - total * (inner / (norm * norm * root))).astype(bf16)


def last_kernel(
    own, scale, me_ref, keys, values, wg, wu, wd, by_gate, by_up, by_lower, by_upper, pk, rk, hk,
    cot_g, cot_u, cot_d, rate_g, rate_u, rate_d, *refs,
):
    count = len(refs) - 10
    firsts = refs[:count]
    grad_keys, grad_values, grad_g, grad_u, grad_d = refs[count:count + 5]
    lower, upper, d_back, keys_t, back_t = refs[count + 5:]
    for part in chunks_of(keys.shape[0]):
        along, active, bent = by_gate[part], by_up[part], by_upper[part]
        ek = product(keys[part], cot_g[...])
        fk = product(keys[part], cot_u[...])
        hk_part = -against(values[part], cot_d[...])
        d_back_part = (ek * along + fk * active).astype(bf16)
        d_back[part] = d_back_part
        back_t[:, part] = d_back_part.T
        keys_t[:, part] = keys[part].T
        upper[part] = (ek * bent + hk_part * active).astype(bf16)
        lower[part] = (ek * by_lower[part] + fk * bent + hk_part * along).astype(bf16)
    grad_keys[...] = (
        against(pk[...], cot_g[...])
        + against(rk[...], cot_u[...])
        + against(lower[:own], wg[...])
        + against(upper[:own], wu[...])
    ).astype(bf16)
    grad_values[...] = (
        -product(hk[...], cot_d[...]) - product(d_back[:own], wd[...])
    ).astype(bf16)
    rows = grad_g.shape[1]
    start = pl.multiple_of(me_ref[0] * rows, 16)
    for which, (left, right, rate, grad) in enumerate((
        (keys_t, lower, rate_g, grad_g), (keys_t, upper, rate_u, grad_u), (back_t, values, rate_d, grad_d)
    )):
        second = product(left[pl.ds(start, rows)], right[...])
        first = sum(ref[which].astype(f32) for ref in firsts)
        both = first - second if which == 2 else first + second
        grad[0] = (both + rate[pl.ds(start, rows)]) * scale


def vmem():
    return pl.BlockSpec(memory_space=pltpu.VMEM)


def smem():
    return pl.BlockSpec(memory_space=pltpu.SMEM)


def hbm():
    return pl.BlockSpec(memory_space=pltpu.HBM)


def anywhere():
    return pl.BlockSpec(memory_space=pl.ANY)


def light():
    return pl.CostEstimate(flops=1, bytes_accessed=1, transcendentals=0)


def params(mib):
    return pltpu.CompilerParams(vmem_limit_bytes=mib * 2**20)


def gather_tokens(queries, keys, values, upstream, out_gain, gate_weight, up_weight, down_weight):
    shards = lax.axis_size("tok")
    ring = shards // 2
    me = lax.axis_index("tok")
    me_ref = jnp.reshape(me, (1,)).astype(jnp.int32)
    own, depth = keys.shape
    rows = gate_weight.shape[1]
    hidden = gate_weight.shape[2]
    tokens = own * shards
    width = out_gain.shape[0] * lax.axis_size("head")
    scale = 1.0 / math.sqrt(tokens)
    gain = out_gain[None]
    S = jax.ShapeDtypeStruct

    matrix = (depth, hidden)
    wide, narrow = S(matrix, f32), S(matrix, bf16)

    packed, packed_second = pl.pallas_call(
        pack_kernel,
        out_shape=(
            S((2 * rows + down_weight.shape[1] + 2 * own, depth), bf16), S((2 * own, depth), bf16),
        ),
        in_specs=[hbm()] * 7,
        out_specs=[vmem()] * 2,
        scratch_shapes=[pltpu.SemaphoreType.DMA((7,))],
        compiler_params=params(60),
    )(gate_weight, up_weight, down_weight, keys, values, queries, upstream)
    buffers = (narrow, narrow, narrow, S((tokens, depth), bf16), S((tokens, depth), bf16))

    def place(pieces, layout, state=(), carry=(), others=()):
        out_shape = buffers
        if carry:
            out_shape += (S((sum(array.shape[0] for array in carry), depth), bf16),)
        start = 1 + len(pieces) + len(carry) + len(others)
        out = pl.pallas_call(
            functools.partial(place_kernel, layout, ring, len(carry)),
            out_shape=out_shape,
            in_specs=[smem()] + [anywhere()] * (start - 1 + len(state)),
            out_specs=[anywhere()] * len(out_shape),
            scratch_shapes=[pltpu.SemaphoreType.DMA((5 * len(pieces) + len(carry),))],
            input_output_aliases={start + index: index for index in range(len(state))},
            cost_estimate=light(),
            compiler_params=params(4),
        )(me_ref, *pieces, *carry, *others, *state)
        return (out[:5], out[5]) if carry else (out, None)

    crossed = swap(packed, ring)
    crossed_second = swap(packed_second, ring)
    up = shift(packed, ring, 1)
    down = shift(tie(packed, crossed), ring, -1)
    state, _ = place((packed, crossed), ((0, 0, 0), (0, 1, 1)))
    crossed_up = swap(up, ring)
    crossed_down = swap(down, ring)
    state, carried = place((up,), ((-1, 0, 2),), state, (up,), (crossed_second,))
    far = shift(carried, ring, 1)
    crossed_far = swap(far, ring)
    state, pair = place(
        (down, crossed_up), ((1, 0, 3), (-1, 1, 4)), state, (packed_second, crossed_second)
    )
    state, _ = place((far, crossed_down), ((-2, 0, 5), (1, 1, 6)), state)
    layout = ((-2, 1, 7),)
    (wg, wu, wd, all_keys, all_values, *rest) = pl.pallas_call(
        functools.partial(fast_kernel, layout, ring),
        out_shape=(
            narrow, narrow, narrow, S((tokens, depth), bf16), S((tokens, depth), bf16),
            *[S((tokens, hidden), f32)] * 4, wide, wide, wide, *[S((own, hidden), bf16)] * 3,
        ),
        in_specs=[smem(), anywhere()] + [anywhere()] * 5,
        out_specs=[vmem()] * 15,
        scratch_shapes=[pltpu.VMEM((tokens, hidden), bf16)] * 3 + [pltpu.SemaphoreType.DMA((5,))],
        input_output_aliases={2 + index: index for index in range(5)},
        cost_estimate=light(),
        compiler_params=params(24),
    )(me_ref, crossed_far, *state)
    slopes, totals, own_rows = rest[:4], rest[4:7], rest[7:]

    up, down = shift(pair, ring, 1), shift(pair, ring, -1)
    pairs = [pair, up, down, shift(tie(down, totals[0]), ring, -1)]

    queries0, upstream0, gq0, uq0, hidden0, out0, stats0 = pl.pallas_call(
        first_forward_kernel,
        out_shape=(
            S((own, depth), bf16), S((own, depth), bf16),
            S((own, hidden), f32), S((own, hidden), f32), S((own, hidden), bf16),
            S((own, depth), f32), S((8, own), f32),
        ),
        in_specs=[vmem()] * 6,
        out_specs=[vmem()] * 7,
        cost_estimate=light(),
        compiler_params=params(16),
    )(queries, upstream, gain, wg, wu, wd)

    def schulz(begin, *sums):
        count = len(sums)
        out = pl.pallas_call(
            functools.partial(schulz_kernel, count),
            out_shape=(
                S((NS_STEPS, *matrix), bf16), S((NS_STEPS, *matrix), bf16),
                S((NS_STEPS, *matrix), bf16), narrow, S((8, 128), f32),
            ) * count,
            in_specs=[vmem()] * (2 * count),
            out_specs=[vmem()] * (5 * count),
            cost_estimate=light(),
            compiler_params=params(16),
        )(*sums, *(wg, wu, wd)[begin:begin + count])
        return [out[i:i + 5] for i in range(0, 5 * count, 5)]

    terms0 = head_terms(stats0)
    first_weight = schulz(0, totals[0])[0]
    terms0[0] = tie(terms0[0], first_weight[4])
    grad_first, kept, sent = pl.pallas_call(
        functools.partial(first_backward_kernel, width, ring),
        out_shape=(
            S((own, depth), bf16), S((ring, 3, rows, hidden), bf16), S((ring, 3, rows, hidden), bf16),
        ),
        in_specs=[smem()] + [vmem()] * (10 + len(terms0)),
        out_specs=[vmem()] * 3,
        scratch_shapes=[pltpu.VMEM((own, hidden), bf16)] * 2
        + [pltpu.VMEM((own, depth), bf16), pltpu.VMEM(matrix, bf16)],
        cost_estimate=light(),
        compiler_params=params(20),
    )(me_ref, queries0, upstream0, gain, wg, wu, wd, gq0, uq0, hidden0, out0, *terms0)

    forward = [first_weight, *schulz(1, *totals[1:])]

    seconds = [forward[which][3] for which in range(3)]
    def second_forward(first, arrived, state=()):
        start = 4 + len(arrived)
        return pl.pallas_call(
            functools.partial(second_forward_kernel, first, len(arrived)),
            out_shape=(
                S((tokens, depth), bf16), S((tokens, depth), bf16),
                S((tokens, hidden), f32), S((tokens, hidden), f32), S((tokens, hidden), bf16),
                S((tokens, depth), f32), S((8, tokens), f32),
            ),
            in_specs=[vmem()] * 4 + [anywhere()] * (len(arrived) + len(state)),
            out_specs=[vmem()] * 7,
            scratch_shapes=[pltpu.SemaphoreType.DMA((4 * len(arrived),))],
            input_output_aliases={start + index: index for index in range(len(state))},
            cost_estimate=light(),
            compiler_params=params(14),
        )(gain, *seconds, *arrived, *state)

    state = second_forward(0, pairs[:-1])
    all_queries, all_upstream, gq, uq, hidden_q, out, stats = second_forward(
        len(pairs) - 1, pairs[-1:], state
    )
    terms = head_terms(stats)

    block = S((3, rows, hidden), bf16)
    summed = pl.pallas_call(
        functools.partial(pair_kernel, ring),
        out_shape=(S((3, rows, hidden), f32),) + (block,) * (ring - 1),
        in_specs=[smem()] + [vmem()] * 2,
        out_specs=[vmem()] * ring,
        compiler_params=params(12),
    )(me_ref, tie(kept, *terms[1:]), swap(tie(sent, up), ring))
    firsts = [summed[0]] + [shift(summed[step], ring, step) for step in range(1, ring)]

    grad_queries, *rates = pl.pallas_call(
        functools.partial(second_backward_kernel, width, own),
        out_shape=(S((2, own, depth), bf16), wide, wide, wide),
        in_specs=[vmem()] * (11 + len(terms)),
        out_specs=[vmem()] * 4,
        scratch_shapes=[pltpu.VMEM((tokens, hidden), bf16)] * 2
        + [pltpu.VMEM((tokens, depth), bf16)],
        cost_estimate=light(),
        compiler_params=params(20),
    )(grad_first, all_queries, all_upstream, gain, *seconds, gq, uq, hidden_q, out, *terms)

    cots = pl.pallas_call(
        schulz_back_kernel,
        out_shape=(narrow,) * 3,
        in_specs=[vmem()] * 18,
        out_specs=[vmem()] * 3,
        scratch_shapes=[pltpu.VMEM((3, *matrix), bf16)] * 2,
        cost_estimate=light(),
        compiler_params=params(20),
    )(
        *rates, *totals, *(forward[which][part] for part in (0, 1, 2) for which in range(3)),
        *(forward[which][4] for which in range(3)),
    )

    return (grad_queries, *pl.pallas_call(
        functools.partial(last_kernel, own, scale),
        out_shape=(
            S((own, depth), bf16), S((own, depth), bf16),
            S((1, rows, hidden), f32), S((1, rows, hidden), f32), S((1, rows, hidden), f32),
        ),
        in_specs=[smem()] + [vmem()] * (18 + len(firsts)),
        out_specs=[vmem()] * 5,
        scratch_shapes=[
            pltpu.VMEM((tokens, hidden), bf16),
            pltpu.VMEM((tokens, hidden), bf16),
            pltpu.VMEM((tokens, hidden), bf16),
            pltpu.VMEM((depth, tokens), bf16),
            pltpu.VMEM((hidden, tokens), bf16),
        ],
        cost_estimate=light(),
        compiler_params=params(24),
    )(
        me_ref, all_keys, all_values, wg, wu, wd, *slopes, *own_rows, *cots, *rates, *firsts,
    ))


def per_device(queries, keys, values, upstream, out_gain, gate_weight, up_weight, down_weight):
    shards = lax.axis_size("tok")
    tokens = keys.shape[0] * shards
    few = 4 * tokens <= 12 * gate_weight.shape[2] and shards == 8
    plan = gather_tokens if few else split_tokens
    return plan(queries, keys, values, upstream, out_gain, gate_weight, up_weight, down_weight)


def solution(mesh):
    in_specs = (
        P(None, "tok", "head"),
        P("tok", "head"),
        P("tok", "head"),
        P(None, "tok", "head"),
        P("head"),
        P("head", "tok", None),
        P("head", "tok", None),
        P("head", "tok", None),
    )
    out_specs = (
        P(None, "tok", "head"),
        P("tok", "head"),
        P("tok", "head"),
        P("head", "tok", None),
        P("head", "tok", None),
        P("head", "tok", None),
    )
    return jax.shard_map(
        per_device, mesh=mesh, in_specs=in_specs, out_specs=out_specs, check_vma=False
    )
```

```python
import functools
import math

import jax
import jax.numpy as jnp
from jax import lax
from jax.experimental import pallas as pl
from jax.experimental.pallas import tpu as pltpu
from jax.sharding import PartitionSpec as P

NS_STEPS = 2


lin_coef = 3.4445
cube_coef = -4.775
fifth_coef = 2.0315
rms_eps = 1e-06
fro_eps = 1e-07

bf16 = jnp.bfloat16
f32 = jnp.float32
ROWS = 256


def product(left, right):
    return jnp.dot(left, right, preferred_element_type=jnp.float32)


def across(left, right):
    return lax.dot_general(
        left, right, (((0,), (0,)), ((), ())), preferred_element_type=jnp.float32
    )


def against(left, right):
    return lax.dot_general(
        left, right, (((1,), (1,)), ((), ())), preferred_element_type=jnp.float32
    )


def fast_forward(keys, values, weights):
    gate_weight, up_weight, down_weight = weights
    gate_pre = product(keys, gate_weight)
    up_pre = product(keys, up_weight)
    sigma = jax.nn.sigmoid(gate_pre)
    active = gate_pre * sigma
    hidden = (active * up_pre).astype(jnp.bfloat16)
    back = -against(values, down_weight)
    slope = sigma * (1.0 + gate_pre * (1.0 - sigma))
    d_gate = (back * up_pre * slope).astype(jnp.bfloat16)
    d_up = (back * active).astype(jnp.bfloat16)
    fast = (across(keys, d_gate), across(keys, d_up), -across(hidden, values))
    saved = (gate_pre, up_pre, sigma, active, hidden, back, slope, d_gate, d_up)
    return (fast, saved)


def fast_second(keys, values, weights, saved, cots):
    gate_weight, up_weight, down_weight = weights
    gate_pre, up_pre, sigma, active, hidden, back, slope, d_gate, d_up = saved
    cot_gate, cot_up, cot_down = cots
    along_gate = product(keys, cot_gate)
    along_up = product(keys, cot_up)
    along_hidden = -against(values, cot_down)
    curve = sigma * (1.0 - sigma) * (2.0 + gate_pre * (1.0 - 2.0 * sigma))
    d_back = (along_gate * up_pre * slope + along_up * active).astype(jnp.bfloat16)
    d_upper = (along_gate * back * slope + along_hidden * active).astype(jnp.bfloat16)
    d_lower = (
        along_gate * back * up_pre * curve + along_up * back * slope + along_hidden * up_pre * slope
    ).astype(jnp.bfloat16)
    grad_keys = (
        against(d_gate, cot_gate)
        + against(d_up, cot_up)
        + against(d_lower, gate_weight)
        + against(d_upper, up_weight)
    ).astype(jnp.bfloat16)
    grad_values = (-product(hidden, cot_down) - product(d_back, down_weight)).astype(jnp.bfloat16)
    partial_value = (across(keys, d_lower), across(keys, d_upper), -across(d_back, values))
    return (grad_keys, grad_values, partial_value)


def apply_forward(queries, weights):
    gate_weight, up_weight, down_weight = weights
    gate_pre = product(queries, gate_weight)
    up_pre = product(queries, up_weight)
    sigma = jax.nn.sigmoid(gate_pre)
    hidden = (gate_pre * sigma * up_pre).astype(jnp.bfloat16)
    output = product(hidden, down_weight)
    return (gate_pre, up_pre, sigma, hidden, output)


def statistics(output, upstream, out_gain, width):
    weighted = out_gain * upstream.astype(jnp.float32)
    sums = lax.psum((jnp.sum(output * output, axis=1), jnp.sum(weighted * output, axis=1)), "head")
    return (lax.rsqrt(sums[0] / width + rms_eps), sums[1] / width)


def apply_backward(queries, weights, saved, upstream, out_gain, width):
    gate_weight, up_weight, down_weight = weights
    gate_pre, up_pre, sigma, hidden, output = saved
    inverse_rms, mean_dot = statistics(output, upstream, out_gain, width)
    weighted = out_gain * upstream.astype(jnp.float32)
    d_output = (
        inverse_rms[:, None] * weighted
        - output * (inverse_rms * inverse_rms * inverse_rms * mean_dot)[:, None]
    ).astype(jnp.bfloat16)
    back = against(d_output, down_weight)
    slope = sigma * (1.0 + gate_pre * (1.0 - sigma))
    d_gate = (back * up_pre * slope).astype(jnp.bfloat16)
    d_up = (back * gate_pre * sigma).astype(jnp.bfloat16)
    grad_queries = (against(d_gate, gate_weight) + against(d_up, up_weight)).astype(jnp.bfloat16)
    partial_value = (across(queries, d_gate), across(queries, d_up), across(hidden, d_output))
    return (grad_queries, partial_value)


def schulz_forward(begin):
    current = begin
    saved = []
    for sweep in range(NS_STEPS):
        gram = against(current, current).astype(jnp.bfloat16)
        blend = (cube_coef * gram.astype(jnp.float32) + fifth_coef * product(gram, gram)).astype(
            jnp.bfloat16
        )
        following = (lin_coef * current.astype(jnp.float32) + product(blend, current)).astype(
            jnp.bfloat16
        )
        saved.append((current, gram, blend))
        current = following
    return (current, saved)


def schulz_backward(cotan, saved):
    current = cotan
    for iterate, gram, blend in reversed(saved):
        cross = against(current, iterate)
        symmetric = (cross + cross.T).astype(jnp.bfloat16)
        bent = product(symmetric, gram)
        mixed = (cube_coef * symmetric.astype(jnp.float32) + fifth_coef * (bent + bent.T)).astype(
            jnp.bfloat16
        )
        current = (
            lin_coef * current.astype(jnp.float32)
            + product(blend, current)
            + product(mixed, iterate)
        ).astype(jnp.bfloat16)
    return current


def split_tokens(queries, keys, values, upstream, out_gain, gate_weight, up_weight, down_weight):
    shards = lax.axis_size("tok")
    owner = lax.axis_index("tok")
    width = out_gain.shape[0] * lax.axis_size("head")
    scale = 1.0 / math.sqrt(queries.shape[1] * shards)
    own_rows = (gate_weight[0], up_weight[0], down_weight[0])
    starts = [owner * own_rows[which].shape[0] for which in range(3)]
    first = tuple(lax.all_gather(rows, "tok", axis=0, tiled=True) for rows in own_rows)
    fast, saved_keys = fast_forward(keys, values, first)
    apply_first = apply_forward(queries[0], first)
    grad_first, partial_first = apply_backward(
        queries[0], first, apply_first, upstream[0], out_gain, width
    )
    totals = lax.psum((fast[0], fast[1], fast[2]), "tok")
    roots = [jnp.sqrt(jnp.sum(totals[which] * totals[which])) for which in range(3)]
    forward = [
        schulz_forward((totals[which] / (roots[which] + fro_eps)).astype(jnp.bfloat16))
        for which in range(3)
    ]
    second = tuple(
        (first[which].astype(jnp.float32) - forward[which][0].astype(jnp.float32)).astype(
            jnp.bfloat16
        )
        for which in range(3)
    )
    apply_second = apply_forward(queries[1], second)
    grad_second, partial_second = apply_backward(
        queries[1], second, apply_second, upstream[1], out_gain, width
    )
    rates = lax.psum((partial_second[0], partial_second[1], partial_second[2]), "tok")
    bottoms = [
        schulz_backward((-rates[which]).astype(jnp.bfloat16), forward[which][1])
        for which in range(3)
    ]
    cots = []
    for which in range(3):
        norm = roots[which] + fro_eps
        inner = jnp.sum(bottoms[which].astype(jnp.float32) * totals[which])
        cots.append(
            (
                bottoms[which].astype(jnp.float32) / norm
                - totals[which] * (inner / (norm * norm * roots[which]))
            ).astype(jnp.bfloat16)
        )
    grad_keys, grad_values, second_order = fast_second(keys, values, first, saved_keys, cots)
    grads = []
    for which in range(3):
        rate_rows = lax.dynamic_slice_in_dim(
            rates[which], starts[which], own_rows[which].shape[0], 0
        )
        summed = lax.psum_scatter(
            partial_first[which] + second_order[which], "tok", scatter_dimension=0, tiled=True
        )
        grads.append(((summed + rate_rows) * scale)[None])
    grad_queries = jnp.stack([grad_first, grad_second])
    return (grad_queries, grad_keys, grad_values, *grads)


def shift(array, ring, step):
    pairs = [
        (o * 2 + i, ((o + step) % ring) * 2 + i) for o in range(ring) for i in range(2)
    ]
    return lax.ppermute(array, "tok", pairs)


def swap(array, ring):
    return lax.ppermute(array, "tok", [(i, i ^ 1) for i in range(2 * ring)])


def tie(array, *earlier):
    return lax.optimization_barrier((array, *earlier))[0]


def head_terms(stats):
    heads = lax.axis_size("head")
    return [stats] + [
        lax.ppermute(stats, "head", [(i, (i + k) % heads) for i in range(heads)])
        for k in range(1, heads)
    ]


def owner_of(ring, me, outer, flip):
    return ((me // 2 + outer + ring) % ring) * 2 + (me % 2 + flip) % 2


def move(rows, sems):
    copies = [
        pltpu.make_async_copy(
            source.at[pl.ds(begin, count)], target.at[pl.ds(place, count)], sems.at[index]
        )
        for index, (source, begin, target, place, count) in enumerate(rows)
    ]
    for copy in copies:
        copy.start()
    for copy in copies:
        copy.wait()


def chunks_of(tokens):
    step = min(ROWS, tokens)
    return [slice(i, i + step) for i in range(0, tokens, step)]


def pack_kernel(gate, up, down, keys, values, queries, upstream, first, second, sems):
    rows = []
    for target, sources in (
        (first, (gate.at[0], up.at[0], down.at[0], keys, values)),
        (second, (queries.at[1], upstream.at[1])),
    ):
        begin = 0
        for source in sources:
            rows.append((source, 0, target, begin, source.shape[0]))
            begin += source.shape[0]
    move(rows, sems)


def place_rows(layout, ring, me, pieces, targets):
    rows = []
    for (outer, flip, slot), piece in zip(layout, pieces):
        owner = owner_of(ring, me, outer, flip)
        begin = 0
        for index, target in enumerate(targets):
            count = target.shape[0] // (2 * ring)
            place = pl.multiple_of(owner * count, 16) if index < 3 else slot * count
            rows.append((piece, begin, target, place, count))
            begin += count
    return rows


def place_kernel(layout, ring, carried, me_ref, *refs):
    sems = refs[-1]
    refs = refs[:-1]
    targets = refs[-6:-1] if carried else refs[-5:]
    rows = place_rows(layout, ring, me_ref[0], refs, targets)
    begin = 0
    for source in refs[len(layout):len(layout) + carried]:
        rows.append((source, 0, refs[-1], begin, source.shape[0]))
        begin += source.shape[0]
    move(rows, sems)


def fast_kernel(layout, ring, me_ref, *refs):
    pieces, refs = refs[:len(layout)], refs[len(layout) + 5:]
    wg, wu, wd, keys, values, by_gate, by_up, by_lower, by_upper = refs[:9]
    totals_g, totals_u, totals_d, pk, rk, hk, d_gate, d_up, hidden, sems = refs[9:]
    move(place_rows(layout, ring, me_ref[0], pieces, (wg, wu, wd, keys, values)), sems)
    for part in chunks_of(keys.shape[0]):
        gk = product(keys[part], wg[...])
        uk = product(keys[part], wu[...])
        back = -against(values[part], wd[...])
        sigma = jax.nn.sigmoid(gk)
        active = gk * sigma
        slope = sigma * (1.0 + gk * (1.0 - sigma))
        curve = sigma * (1.0 - sigma) * (2.0 + gk * (1.0 - 2.0 * sigma))
        along = uk * slope
        hidden[part] = (active * uk).astype(bf16)
        d_gate[part] = (back * along).astype(bf16)
        d_up[part] = (back * active).astype(bf16)
        by_gate[part], by_up[part] = along, active
        by_lower[part], by_upper[part] = back * uk * curve, back * slope
    totals_g[...] = across(keys[...], d_gate[...])
    totals_u[...] = across(keys[...], d_up[...])
    totals_d[...] = -across(hidden[...], values[...])
    own = pk.shape[0]
    pk[...], rk[...], hk[...] = d_gate[:own], d_up[:own], hidden[:own]


def schulz_kernel(count, *refs):
    totals, weights = refs[:count], refs[count:2 * count]
    outs = [refs[i:i + 5] for i in range(2 * count, 7 * count, 5)]
    for total_ref, (xs, _, _, _, root_ref) in zip(totals, outs):
        total = total_ref[...]
        root = jnp.sqrt(jnp.sum(total * total, keepdims=True))
        root_ref[...] = jnp.broadcast_to(root, root_ref.shape)
        xs[0] = (total / (root + fro_eps)).astype(bf16)
    for sweep in range(NS_STEPS):
        for xs, grams, _, _, _ in outs:
            grams[sweep] = against(xs[sweep], xs[sweep]).astype(bf16)
        for _, grams, blends, _, _ in outs:
            gram = grams[sweep]
            blends[sweep] = (
                cube_coef * gram.astype(f32) + fifth_coef * product(gram, gram)
            ).astype(bf16)
        for weight, (xs, _, blends, following_ref, _) in zip(weights, outs):
            current = xs[sweep]
            following = (
                lin_coef * current.astype(f32) + product(blends[sweep], current)
            ).astype(bf16)
            if sweep + 1 < NS_STEPS:
                xs[sweep + 1] = following
            else:
                following_ref[...] = (weight[...].astype(f32) - following.astype(f32)).astype(bf16)


def row_sums(columns, tokens):
    lanes = lax.broadcasted_iota(jnp.int32, (tokens, 128), 1)
    spread = jnp.where(lanes == 0, columns[0], jnp.where(lanes == 1, columns[1], 0.0))
    return spread.T[:8]


def forward_part(
    parts, queries, upstream, gain, wg, wu, wd, by_gate, by_up, hidden_ref, out_ref, stats
):
    for part in parts:
        gq = product(queries[part], wg[...])
        uq = product(queries[part], wu[...])
        sigma = jax.nn.sigmoid(gq)
        active = gq * sigma
        hidden = (active * uq).astype(bf16)
        output = product(hidden, wd[...])
        weighted = gain[...] * upstream[part].astype(f32)
        sums = (
            jnp.sum(output * output, axis=1, keepdims=True),
            jnp.sum(weighted * output, axis=1, keepdims=True),
        )
        stats[:, part] = row_sums(sums, output.shape[0])
        by_gate[part], by_up[part] = uq * sigma * (1.0 + gq * (1.0 - sigma)), active
        hidden_ref[part], out_ref[part] = hidden, output


def backward_part(
    width, queries, upstream, gain, wg, wu, wd, by_gate, by_up, hidden, out_ref, sums,
    grad_ref, d_gate, d_up, d_out, own,
):
    for part in chunks_of(queries.shape[0]):
        total = sum(term[:, part] for term in sums)
        tokens = total.shape[1]
        square = total[0:1] / width
        inverse = lax.rsqrt(square + rms_eps)
        pull = inverse * inverse * inverse * (total[1:2] / width)
        index = lax.broadcasted_iota(jnp.int32, (128, tokens), 0)
        columns = jnp.where(index == 0, inverse, jnp.where(index == 1, pull, 0.0)).T
        inverse, pull = columns[:, 0:1], columns[:, 1:2]
        weighted = gain[...] * upstream[part].astype(f32)
        d_output = (inverse * weighted - out_ref[part] * pull).astype(bf16)
        back = against(d_output, wd[...])
        d_gate[part] = (back * by_gate[part]).astype(bf16)
        d_up[part] = (back * by_up[part]).astype(bf16)
        d_out[part] = d_output
    grad_ref[...] = (
        against(d_gate[:own], wg[...]) + against(d_up[:own], wu[...])
    ).astype(bf16)


def first_forward_kernel(
    queries_ref, upstream_ref, gain, wg, wu, wd, queries, upstream, gq, uq, hidden, out, stats
):
    queries[...], upstream[...] = queries_ref[0], upstream_ref[0]
    parts = chunks_of(queries.shape[0])
    forward_part(parts, queries, upstream, gain, wg, wu, wd, gq, uq, hidden, out, stats)


def first_backward_kernel(
    width, ring, me_ref, queries, upstream, gain, wg, wu, wd, gq, uq, hidden, out, *refs
):
    count = len(refs) - 7
    sums = refs[:count]
    grad, kept, sent, d_gate, d_up, d_out, partial = refs[count:]
    backward_part(
        width, queries, upstream, gain, wg, wu, wd, gq, uq, hidden, out, sums,
        grad, d_gate, d_up, d_out, queries.shape[0],
    )
    inner = me_ref[0] % 2
    rows = kept.shape[2]
    for which, (left, right) in enumerate(((queries, d_gate), (queries, d_up), (hidden, d_out))):
        partial[...] = across(left[...], right[...]).astype(bf16)
        for outer in range(ring):
            mine = pl.multiple_of((outer * 2 + inner) * rows, 16)
            other = pl.multiple_of((outer * 2 + 1 - inner) * rows, 16)
            kept[outer, which] = partial[pl.ds(mine, rows)]
            sent[outer, which] = partial[pl.ds(other, rows)]


def pair_kernel(ring, me_ref, kept, received, own, *others):
    outer = me_ref[0] // 2
    own[...] = kept[outer].astype(f32) + received[outer].astype(f32)
    for step, target in enumerate(others, 1):
        place = (outer + step) % ring
        target[...] = (kept[place].astype(f32) + received[place].astype(f32)).astype(bf16)


def second_forward_kernel(first, count, gain, wg, wu, wd, *refs):
    pieces = refs[:count]
    queries, upstream, gq, uq, hidden, out, stats, sems = refs[-8:]
    tokens = pieces[0].shape[0] // 4
    rows = []
    for slot, piece in enumerate(pieces):
        for half in range(2):
            place = (2 * (first + slot) + half) * tokens
            rows.append((piece, 2 * half * tokens, queries, place, tokens))
            rows.append((piece, (2 * half + 1) * tokens, upstream, place, tokens))
    move(rows, sems)
    parts = [
        slice(part.start + 2 * first * tokens, part.stop + 2 * first * tokens)
        for part in chunks_of(2 * count * tokens)
    ]
    forward_part(parts, queries, upstream, gain, wg, wu, wd, gq, uq, hidden, out, stats)


def second_backward_kernel(
    width, own, grad_first, queries, upstream, gain, wg, wu, wd, gq, uq, hidden, out, *refs
):
    count = len(refs) - 7
    sums = refs[:count]
    grad, rate_g, rate_u, rate_d, d_gate, d_up, d_out = refs[count:]
    grad[0] = grad_first[...]
    backward_part(
        width, queries, upstream, gain, wg, wu, wd, gq, uq, hidden, out, sums,
        grad.at[1], d_gate, d_up, d_out, own,
    )
    rate_g[...] = across(queries[...], d_gate[...])
    rate_u[...] = across(queries[...], d_up[...])
    rate_d[...] = across(hidden[...], d_out[...])


def schulz_back_kernel(*refs):
    rates, totals, xs, grams, blends, roots, cots = (refs[i:i + 3] for i in range(0, 21, 3))
    symmetric, mixed = refs[21:]
    for which in range(3):
        cots[which][...] = (-rates[which][...]).astype(bf16)
    for sweep in reversed(range(NS_STEPS)):
        for which in range(3):
            cross = against(cots[which][...], xs[which][sweep])
            symmetric[which] = (cross + cross.T).astype(bf16)
        for which in range(3):
            bent = product(symmetric[which], grams[which][sweep])
            mixed[which] = (
                cube_coef * symmetric[which].astype(f32) + fifth_coef * (bent + bent.T)
            ).astype(bf16)
        for which in range(3):
            cots[which][...] = (
                lin_coef * cots[which][...].astype(f32)
                + product(blends[which][sweep], cots[which][...])
                + product(mixed[which], xs[which][sweep])
            ).astype(bf16)
    for which in range(3):
        root = roots[which][0:1, 0:1]
        norm = root + fro_eps
        total = totals[which][...]
        bottom = cots[which][...].astype(f32)
        inner = jnp.sum(bottom * total, keepdims=True)
        cots[which][...] = (bottom / norm - total * (inner / (norm * norm * root))).astype(bf16)


def last_kernel(
    own, me_ref, keys, values, wg, wu, wd, by_gate, by_up, by_lower, by_upper, pk, rk, hk,
    cot_g, cot_u, cot_d, rate_g, rate_u, rate_d, *refs,
):
    grad_keys, grad_values, rest_g, rest_u, rest_d, lower, upper, d_back, keys_t, back_t = refs
    for part in chunks_of(keys.shape[0]):
        along, active, bent = by_gate[part], by_up[part], by_upper[part]
        ek = product(keys[part], cot_g[...])
        fk = product(keys[part], cot_u[...])
        hk_part = -against(values[part], cot_d[...])
        d_back_part = (ek * along + fk * active).astype(bf16)
        d_back[part] = d_back_part
        back_t[:, part] = d_back_part.T
        keys_t[:, part] = keys[part].T
        upper[part] = (ek * bent + hk_part * active).astype(bf16)
        lower[part] = (ek * by_lower[part] + fk * bent + hk_part * along).astype(bf16)
    grad_keys[...] = (
        against(pk[...], cot_g[...])
        + against(rk[...], cot_u[...])
        + against(lower[:own], wg[...])
        + against(upper[:own], wu[...])
    ).astype(bf16)
    grad_values[...] = (
        -product(hk[...], cot_d[...]) - product(d_back[:own], wd[...])
    ).astype(bf16)
    rows = rest_g.shape[0]
    start = pl.multiple_of(me_ref[0] * rows, 16)
    for left, right, rate, rest, sign in (
        (keys_t, lower, rate_g, rest_g, 1.0),
        (keys_t, upper, rate_u, rest_u, 1.0),
        (back_t, values, rate_d, rest_d, -1.0),
    ):
        second = product(left[pl.ds(start, rows)], right[...])
        rest[...] = rate[pl.ds(start, rows)] + sign * second


def total_kernel(scale, rest_g, rest_u, rest_d, *refs):
    firsts, grads = refs[:-3], refs[-3:]
    for which, (rest, grad) in enumerate(zip((rest_g, rest_u, rest_d), grads)):
        first = sum(ref[which].astype(f32) for ref in firsts)
        grad[0] = (first + rest[...]) * scale


def vmem():
    return pl.BlockSpec(memory_space=pltpu.VMEM)


def smem():
    return pl.BlockSpec(memory_space=pltpu.SMEM)


def hbm():
    return pl.BlockSpec(memory_space=pltpu.HBM)


def anywhere():
    return pl.BlockSpec(memory_space=pl.ANY)


def light():
    return pl.CostEstimate(flops=1, bytes_accessed=1, transcendentals=0)


def params(mib):
    return pltpu.CompilerParams(vmem_limit_bytes=mib * 2**20)


def gather_tokens(queries, keys, values, upstream, out_gain, gate_weight, up_weight, down_weight):
    shards = lax.axis_size("tok")
    ring = shards // 2
    me = lax.axis_index("tok")
    me_ref = jnp.reshape(me, (1,)).astype(jnp.int32)
    own, depth = keys.shape
    rows = gate_weight.shape[1]
    hidden = gate_weight.shape[2]
    tokens = own * shards
    width = out_gain.shape[0] * lax.axis_size("head")
    scale = 1.0 / math.sqrt(tokens)
    gain = out_gain[None]
    S = jax.ShapeDtypeStruct

    matrix = (depth, hidden)
    wide, narrow = S(matrix, f32), S(matrix, bf16)

    packed, packed_second = pl.pallas_call(
        pack_kernel,
        out_shape=(
            S((2 * rows + down_weight.shape[1] + 2 * own, depth), bf16), S((2 * own, depth), bf16),
        ),
        in_specs=[hbm()] * 7,
        out_specs=[vmem()] * 2,
        scratch_shapes=[pltpu.SemaphoreType.DMA((7,))],
        compiler_params=params(60),
    )(gate_weight, up_weight, down_weight, keys, values, queries, upstream)
    buffers = (narrow, narrow, narrow, S((tokens, depth), bf16), S((tokens, depth), bf16))

    def place(pieces, layout, state=(), carry=(), others=()):
        out_shape = buffers
        if carry:
            out_shape += (S((sum(array.shape[0] for array in carry), depth), bf16),)
        start = 1 + len(pieces) + len(carry) + len(others)
        out = pl.pallas_call(
            functools.partial(place_kernel, layout, ring, len(carry)),
            out_shape=out_shape,
            in_specs=[smem()] + [anywhere()] * (start - 1 + len(state)),
            out_specs=[anywhere()] * len(out_shape),
            scratch_shapes=[pltpu.SemaphoreType.DMA((5 * len(pieces) + len(carry),))],
            input_output_aliases={start + index: index for index in range(len(state))},
            cost_estimate=light(),
            compiler_params=params(4),
        )(me_ref, *pieces, *carry, *others, *state)
        return (out[:5], out[5]) if carry else (out, None)

    crossed = swap(packed, ring)
    crossed_second = swap(packed_second, ring)
    up = shift(packed, ring, 1)
    down = shift(tie(packed, crossed), ring, -1)
    state, _ = place((packed, crossed), ((0, 0, 0), (0, 1, 1)))
    crossed_up = swap(up, ring)
    crossed_down = swap(down, ring)
    state, carried = place((up,), ((-1, 0, 2),), state, (up,), (crossed_second,))
    far = shift(carried, ring, 1)
    crossed_far = swap(far, ring)
    state, pair = place(
        (down, crossed_up), ((1, 0, 3), (-1, 1, 4)), state, (packed_second, crossed_second)
    )
    state, _ = place((far, crossed_down), ((-2, 0, 5), (1, 1, 6)), state)
    layout = ((-2, 1, 7),)
    (wg, wu, wd, all_keys, all_values, *rest) = pl.pallas_call(
        functools.partial(fast_kernel, layout, ring),
        out_shape=(
            narrow, narrow, narrow, S((tokens, depth), bf16), S((tokens, depth), bf16),
            *[S((tokens, hidden), f32)] * 4, wide, wide, wide, *[S((own, hidden), bf16)] * 3,
        ),
        in_specs=[smem(), anywhere()] + [anywhere()] * 5,
        out_specs=[vmem()] * 15,
        scratch_shapes=[pltpu.VMEM((tokens, hidden), bf16)] * 3 + [pltpu.SemaphoreType.DMA((5,))],
        input_output_aliases={2 + index: index for index in range(5)},
        cost_estimate=light(),
        compiler_params=params(24),
    )(me_ref, crossed_far, *state)
    slopes, totals, own_rows = rest[:4], rest[4:7], rest[7:]

    up, down = shift(pair, ring, 1), shift(pair, ring, -1)
    pairs = [pair, up, down, shift(tie(down, totals[0]), ring, -1)]

    queries0, upstream0, gq0, uq0, hidden0, out0, stats0 = pl.pallas_call(
        first_forward_kernel,
        out_shape=(
            S((own, depth), bf16), S((own, depth), bf16),
            S((own, hidden), f32), S((own, hidden), f32), S((own, hidden), bf16),
            S((own, depth), f32), S((8, own), f32),
        ),
        in_specs=[vmem()] * 6,
        out_specs=[vmem()] * 7,
        cost_estimate=light(),
        compiler_params=params(16),
    )(queries, upstream, gain, wg, wu, wd)

    def schulz(begin, *sums):
        count = len(sums)
        out = pl.pallas_call(
            functools.partial(schulz_kernel, count),
            out_shape=(
                S((NS_STEPS, *matrix), bf16), S((NS_STEPS, *matrix), bf16),
                S((NS_STEPS, *matrix), bf16), narrow, S((8, 128), f32),
            ) * count,
            in_specs=[vmem()] * (2 * count),
            out_specs=[vmem()] * (5 * count),
            cost_estimate=light(),
            compiler_params=params(16),
        )(*sums, *(wg, wu, wd)[begin:begin + count])
        return [out[i:i + 5] for i in range(0, 5 * count, 5)]

    terms0 = head_terms(stats0)
    first_weight = schulz(0, totals[0])[0]
    terms0[0] = tie(terms0[0], first_weight[4])
    grad_first, kept, sent = pl.pallas_call(
        functools.partial(first_backward_kernel, width, ring),
        out_shape=(
            S((own, depth), bf16), S((ring, 3, rows, hidden), bf16), S((ring, 3, rows, hidden), bf16),
        ),
        in_specs=[smem()] + [vmem()] * (10 + len(terms0)),
        out_specs=[vmem()] * 3,
        scratch_shapes=[pltpu.VMEM((own, hidden), bf16)] * 2
        + [pltpu.VMEM((own, depth), bf16), pltpu.VMEM(matrix, bf16)],
        cost_estimate=light(),
        compiler_params=params(20),
    )(me_ref, queries0, upstream0, gain, wg, wu, wd, gq0, uq0, hidden0, out0, *terms0)

    forward = [first_weight, *schulz(1, *totals[1:])]

    seconds = [forward[which][3] for which in range(3)]
    def second_forward(first, arrived, state=()):
        start = 4 + len(arrived)
        return pl.pallas_call(
            functools.partial(second_forward_kernel, first, len(arrived)),
            out_shape=(
                S((tokens, depth), bf16), S((tokens, depth), bf16),
                S((tokens, hidden), f32), S((tokens, hidden), f32), S((tokens, hidden), bf16),
                S((tokens, depth), f32), S((8, tokens), f32),
            ),
            in_specs=[vmem()] * 4 + [anywhere()] * (len(arrived) + len(state)),
            out_specs=[vmem()] * 7,
            scratch_shapes=[pltpu.SemaphoreType.DMA((4 * len(arrived),))],
            input_output_aliases={start + index: index for index in range(len(state))},
            cost_estimate=light(),
            compiler_params=params(14),
        )(gain, *seconds, *arrived, *state)

    state = second_forward(0, pairs[:-1])
    all_queries, all_upstream, gq, uq, hidden_q, out, stats = second_forward(
        len(pairs) - 1, pairs[-1:], state
    )
    terms = head_terms(stats)

    block = S((3, rows, hidden), bf16)
    summed = pl.pallas_call(
        functools.partial(pair_kernel, ring),
        out_shape=(S((3, rows, hidden), f32),) + (block,) * (ring - 1),
        in_specs=[smem()] + [vmem()] * 2,
        out_specs=[vmem()] * ring,
        compiler_params=params(12),
    )(me_ref, tie(kept, *terms[1:]), swap(tie(sent, up), ring))
    firsts = [summed[0]] + [shift(summed[step], ring, step) for step in range(1, ring)]

    grad_queries, *rates = pl.pallas_call(
        functools.partial(second_backward_kernel, width, own),
        out_shape=(S((2, own, depth), bf16), wide, wide, wide),
        in_specs=[vmem()] * (11 + len(terms)),
        out_specs=[vmem()] * 4,
        scratch_shapes=[pltpu.VMEM((tokens, hidden), bf16)] * 2
        + [pltpu.VMEM((tokens, depth), bf16)],
        cost_estimate=light(),
        compiler_params=params(20),
    )(grad_first, all_queries, all_upstream, gain, *seconds, gq, uq, hidden_q, out, *terms)

    cots = pl.pallas_call(
        schulz_back_kernel,
        out_shape=(narrow,) * 3,
        in_specs=[vmem()] * 18,
        out_specs=[vmem()] * 3,
        scratch_shapes=[pltpu.VMEM((3, *matrix), bf16)] * 2,
        cost_estimate=light(),
        compiler_params=params(20),
    )(
        *rates, *totals, *(forward[which][part] for part in (0, 1, 2) for which in range(3)),
        *(forward[which][4] for which in range(3)),
    )

    grad_keys, grad_values, *rests = pl.pallas_call(
        functools.partial(last_kernel, own),
        out_shape=(
            S((own, depth), bf16), S((own, depth), bf16),
            *[S((rows, hidden), f32)] * 3,
        ),
        in_specs=[smem()] + [vmem()] * 18,
        out_specs=[vmem()] * 5,
        scratch_shapes=[
            pltpu.VMEM((tokens, hidden), bf16),
            pltpu.VMEM((tokens, hidden), bf16),
            pltpu.VMEM((tokens, hidden), bf16),
            pltpu.VMEM((depth, tokens), bf16),
            pltpu.VMEM((hidden, tokens), bf16),
        ],
        cost_estimate=light(),
        compiler_params=params(24),
    )(
        me_ref, all_keys, all_values, wg, wu, wd, *slopes, *own_rows, *cots, *rates,
    )

    grads = pl.pallas_call(
        functools.partial(total_kernel, scale),
        out_shape=(S((1, rows, hidden), f32),) * 3,
        in_specs=[vmem()] * (3 + len(firsts)),
        out_specs=[vmem()] * 3,
        cost_estimate=light(),
        compiler_params=params(6),
    )(*rests, *firsts)
    return (grad_queries, grad_keys, grad_values, *grads)


def per_device(queries, keys, values, upstream, out_gain, gate_weight, up_weight, down_weight):
    shards = lax.axis_size("tok")
    tokens = keys.shape[0] * shards
    few = 4 * tokens <= 12 * gate_weight.shape[2] and shards == 8
    plan = gather_tokens if few else split_tokens
    return plan(queries, keys, values, upstream, out_gain, gate_weight, up_weight, down_weight)


def solution(mesh):
    in_specs = (
        P(None, "tok", "head"),
        P("tok", "head"),
        P("tok", "head"),
        P(None, "tok", "head"),
        P("head"),
        P("head", "tok", None),
        P("head", "tok", None),
        P("head", "tok", None),
    )
    out_specs = (
        P(None, "tok", "head"),
        P("tok", "head"),
        P("tok", "head"),
        P("head", "tok", None),
        P("head", "tok", None),
        P("head", "tok", None),
    )
    return jax.shard_map(
        per_device, mesh=mesh, in_specs=in_specs, out_specs=out_specs, check_vma=False
    )
```
